512 devices in a mesh: dom: 64 (over z_lo, y, core), member: 4 (over x), dp: 2 (over z_hi).
Axes of the slice: x: 4, y: 4, z: 16 (z_hi: 2, z_lo: 8; z = z_hi * 8 + z_lo), core: 2. Of those that a mesh axis runs over, the one named last changes fastest.
Arguments:
- edges: bfloat16 [8, 16384, 512], P(('member', 'dp'), 'dom'), may hold values from -6 to 6
- cotangent: bfloat16 [8, 16384, 512], P(('member', 'dp'), 'dom'), may hold values from -6 to 6
- fine_latents: bfloat16 [8, 4096, 512], P(('member', 'dp'), 'dom'), may hold values from -6 to 6
- coarse_block: bfloat16 [8, 4096, 512], P(('member', 'dp'), 'dom'), may hold values from -6 to 6
- w_in: bfloat16 [1536, 512], replicated, may hold values from -0.15625 to 0.15625
- w_out: bfloat16 [512, 512], replicated, may hold values from -0.25 to 0.25
- senders: int32 [16384], P('dom'), may hold values from 0 to 159
- receivers: int32 [16384], P('dom'), may hold values from 0 to 63
- edge_count: int32 [64], P('dom'), may hold values from 128 to 256, as said below
- coarse_ids: int32 [64, 64], replicated, may hold values from 0 to 641
Outputs:
- grad_edges: bfloat16 [8, 16384, 512], P(('member', 'dp'), 'dom')
- grad_fine: bfloat16 [8, 4096, 512], P(('member', 'dp'), 'dom')
- grad_coarse: bfloat16 [8, 4096, 512], P(('member', 'dp'), 'dom')
- grad_w_in: float32 [1536, 512], P('dom')
- grad_w_out: float32 [512, 512], P('dom')
The draws below stay inside these ranges and needn't reach their ends.
Inputs may be any that keep to these rules, and one draw needn't show every extreme that they name: `edge_count`: one partition holds exactly 256 live edge slots.
All inputs are finite; a program needn't handle non-finite values.
Results may differ from the reference program's by a relative error of at most 0.015.
Values may be sent and summed in bfloat16 or wider, within the bound.
No kernel may reach another device: no remote copies, remote signals or barrier semaphores. Data moves between devices by JAX's collectives and lax.ppermute only.
A program may use at most 64 MiB of HBM per device.

```python
import math
import jax
import jax.numpy as jnp
from jax import lax

D = 512
NF_DEV = 64
RIM = 16
CB = 64
NC = 642
E_DEV = 256
PARTITIONS = 64
SAMPLES = 8
EDGES = 16384
NODES = 4096
SLOTS = 4096
ALL_EDGES = 131072


def draw_edge_count(key, part):
    key = jax.random.fold_in(key, 11)
    counts = jax.random.randint(key, (PARTITIONS,), E_DEV // 2, E_DEV + 1)
    chosen = jax.random.randint(jax.random.fold_in(key, 5), (), 0, PARTITIONS)
    return jnp.where(jnp.arange(PARTITIONS) == chosen, E_DEV, counts).astype(jnp.int32)


def set_ends(drawn, stream_key, least, high):
    dims = drawn.shape
    place = [jax.random.randint(jax.random.fold_in(stream_key, axis), (), 0, dims[axis]) for axis in range(len(dims))]
    drawn = drawn.at[tuple(place)].set(least)
    longest = dims.index(max(dims))
    place[longest] = (place[longest] + 1) % dims[longest]
    return drawn.at[tuple(place)].set(high)


def levels(stream_key, dims, cuts, smallest, largest):
    factor_of, own = 1.0, jax.random.fold_in(stream_key, 6)
    for axis_at, blocks in cuts:
        heights = jnp.exp(jax.random.uniform(jax.random.fold_in(own, axis_at), (blocks,), jnp.float32, smallest / len(cuts), largest / len(cuts)))
        factor_of = factor_of * jnp.repeat(heights, dims[axis_at] // blocks).reshape([-1 if axis == axis_at else 1 for axis in range(len(dims))])
    return factor_of


def normal_values(own_key, extent, spread, bound, cuts=(), kind=jnp.bfloat16):
    entries = jax.random.normal(own_key, extent, jnp.float32) * spread
    if len(cuts) > 0:
        entries = levels(own_key, extent, cuts, -0.22, 0.18) * entries
    return jnp.clip(entries, min=-bound, max=bound).astype(kind)


def setup_inputs(seed: int = 0) -> dict:
    key_of = jax.random.split(jax.random.key(seed), 11)
    return {
        "edges": normal_values(key_of[0], (SAMPLES, EDGES, D), 1.0, 6.0, ((0, 8), (1, 64))),
        "cotangent": normal_values(key_of[1], (SAMPLES, EDGES, D), 1.0, 6.0, ((0, 8), (1, 64))),
        "fine_latents": normal_values(key_of[2], (SAMPLES, NODES, D), 1.0, 6.0, ((0, 8), (1, 64))),
        "coarse_block": normal_values(key_of[3], (SAMPLES, SLOTS, D), 1.0, 6.0, ((0, 8), (1, 64))),
        "w_in": normal_values(key_of[4], (3 * D, D), (3 * D) ** -0.5, 0.15625),
        "w_out": normal_values(key_of[5], (D, D), D ** -0.5, 0.25),
        "senders": set_ends(jax.random.randint(key_of[6], (EDGES,), 0, NF_DEV + 2 * RIM + CB), jax.random.fold_in(key_of[6], 1), 0, (NF_DEV + 2 * RIM + CB) - 1).astype(jnp.int32),
        "receivers": set_ends(jax.random.randint(key_of[7], (EDGES,), 0, NF_DEV), jax.random.fold_in(key_of[7], 1), 0, NF_DEV - 1).astype(jnp.int32),
        "edge_count": draw_edge_count(jax.random.fold_in(key_of[10], 71), 0),
        "coarse_ids": set_ends(jax.random.randint(key_of[9], (PARTITIONS, CB), 0, NC), jax.random.fold_in(key_of[9], 1), 0, NC - 1).astype(jnp.int32),
    }


def edge_backward(edge_rows, cot_rows, table, senders_p, receivers_p, count, w_in, w_out):
    width = edge_rows.shape[1]
    slots = jnp.arange(edge_rows.shape[0], dtype=jnp.int32)
    valid = (slots < count).astype(jnp.float32)
    onehot_send = (senders_p[:, None] == jnp.arange(table.shape[0], dtype=jnp.int32)[None, :]).astype(jnp.bfloat16)
    onehot_recv = (receivers_p[:, None] == jnp.arange(NF_DEV, dtype=jnp.int32)[None, :]).astype(jnp.bfloat16)
    h_send = jnp.dot(onehot_send, table, preferred_element_type=jnp.float32).astype(jnp.bfloat16)
    h_recv = jnp.dot(onehot_recv, table[RIM:RIM + NF_DEV], preferred_element_type=jnp.float32).astype(jnp.bfloat16)
    inputs = jnp.concatenate([edge_rows, h_send, h_recv], axis=1)
    pre = jnp.dot(inputs, w_in, preferred_element_type=jnp.float32)
    sig = jax.nn.sigmoid(pre)
    act = (pre * sig).astype(jnp.bfloat16)
    hidden = jnp.dot(act, w_out, preferred_element_type=jnp.float32)
    centred = hidden - lax.optimization_barrier(jnp.mean(hidden, axis=-1, keepdims=True))
    rstd = lax.rsqrt(lax.optimization_barrier(jnp.mean(centred * centred, axis=-1, keepdims=True)) + 1e-05)
    normed = centred * rstd
    dnorm = cot_rows.astype(jnp.float32) * valid[:, None]
    dhidden = rstd * (dnorm - lax.optimization_barrier(jnp.mean(dnorm, axis=-1, keepdims=True)) - normed * lax.optimization_barrier(jnp.mean(dnorm * normed, axis=-1, keepdims=True)))
    dhidden_b = dhidden.astype(jnp.bfloat16)
    dw_out = jnp.dot(act.T, dhidden_b, preferred_element_type=jnp.float32)
    dact = jnp.dot(dhidden_b, w_out.T, preferred_element_type=jnp.float32)
    dpre = dact * sig * (1.0 + pre * (1.0 - sig))
    dpre_b = dpre.astype(jnp.bfloat16)
    dw_in = jnp.dot(inputs.T, dpre_b, preferred_element_type=jnp.float32)
    dinputs = jnp.dot(dpre_b, w_in.T, preferred_element_type=jnp.float32)
    grad_rows = (dnorm + dinputs[:, :width]).astype(jnp.bfloat16)
    d_send = dinputs[:, width:2 * width].astype(jnp.bfloat16)
    d_recv = dinputs[:, 2 * width:].astype(jnp.bfloat16)
    d_table = jnp.dot(onehot_send.T, d_send, preferred_element_type=jnp.float32)
    d_own = jnp.dot(onehot_recv.T, d_recv, preferred_element_type=jnp.float32)
    return (grad_rows, d_table, d_own, dw_in, dw_out)

def reference(edges, cotangent, fine_latents, coarse_block, w_in, w_out, senders, receivers, edge_count, coarse_ids):
    flat_ids = coarse_ids.reshape(-1).astype(jnp.int32)
    grad_in = jnp.zeros((3 * D, D), jnp.float32)
    grad_out = jnp.zeros((D, D), jnp.float32)
    edge_list, fine_list, coarse_list = ([], [], [])
    send_all = senders.reshape(PARTITIONS, E_DEV).astype(jnp.int32)
    recv_all = receivers.reshape(PARTITIONS, E_DEV).astype(jnp.int32)
    for sample in range(SAMPLES):
        fine = fine_latents[sample].reshape(PARTITIONS, NF_DEV, D)
        lower = jnp.roll(fine[:, NF_DEV - RIM:], 1, axis=0)
        upper = jnp.roll(fine[:, :RIM], -1, axis=0)
        tables = jnp.concatenate([lower, fine, upper, coarse_block[sample].reshape(PARTITIONS, CB, D)], axis=1)

        def step(carry, pieces):
            e_rows, c_rows, table, snd, rcv, count = pieces
            grad_rows, d_table, d_own, dw_in, dw_out = edge_backward(e_rows, c_rows, table, snd, rcv, count, w_in, w_out)
            return ((carry[0] + dw_in, carry[1] + dw_out), (grad_rows, d_table, d_own))
        (grad_in, grad_out), (grad_rows, d_table, d_own) = lax.scan(step, (grad_in, grad_out), (edges[sample].reshape(PARTITIONS, E_DEV, D), cotangent[sample].reshape(PARTITIONS, E_DEV, D), tables, send_all, recv_all, edge_count))
        fine_total = d_table[:, RIM:RIM + NF_DEV] + d_own
        from_upper = jnp.roll(d_table[:, :RIM], -1, axis=0)
        from_lower = jnp.roll(d_table[:, RIM + NF_DEV:2 * RIM + NF_DEV], 1, axis=0)
        fine_total = fine_total.at[:, :RIM].add(from_lower)
        fine_total = fine_total.at[:, NF_DEV - RIM:].add(from_upper)
        partial_value = d_table[:, 2 * RIM + NF_DEV:].reshape(SLOTS, D)
        total = jax.ops.segment_sum(partial_value, flat_ids, num_segments=NC)
        edge_list.append(grad_rows.reshape(EDGES, D))
        fine_list.append(fine_total.reshape(NODES, D).astype(jnp.bfloat16))
        coarse_list.append(jnp.take(total, flat_ids, axis=0).astype(jnp.bfloat16))
    scale = 1.0 / math.sqrt(ALL_EDGES)
    return (jnp.stack(edge_list), jnp.stack(fine_list), jnp.stack(coarse_list), grad_in * scale, grad_out * scale)
```

```python
import functools
import math

import jax
import jax.numpy as jnp
from jax import lax
from jax.experimental import pallas as pl
from jax.experimental.pallas import tpu as pltpu
from jax.sharding import Mesh
from jax.sharding import PartitionSpec as P

RIM = 16
NC = 642
YS = 4
CORES = 2
LANES = 128
TILE = 16

F32 = jnp.float32
BF16 = jnp.bfloat16


def dot(left, right, dims):
    return lax.dot_general(left, right, (dims, ((), ())), preferred_element_type=F32)


def edge_kernel(
    zs,
    count_ref,
    place_ref,
    edges_ref,
    cot_ref,
    before_ref,
    fine_ref,
    after_ref,
    coarse_ref,
    w_in_ref,
    w_out_ref,
    senders_ref,
    receivers_ref,
    ids_ref,
    grad_edges_ref,
    own_ref,
    down_ref,
    up_ref,
    keep_ref,
    send_ref,
    dw_in_ref,
    dw_out_ref,
    dense_ref,
):
    rows, width = edges_ref.shape
    nodes = fine_ref.shape[0]
    slots = coarse_ref.shape[0]
    depth = 2 * RIM + nodes + slots
    dom = place_ref[0]
    core = lax.rem(dom, CORES)

    senders = senders_ref[...]
    pick_send_t = jnp.where(
        lax.broadcasted_iota(jnp.int32, (depth, rows), 0) == senders, 1.0, 0.0
    ).astype(BF16)
    pick_recv_t = jnp.where(
        lax.broadcasted_iota(jnp.int32, (nodes, rows), 0) == receivers_ref[...], 1.0, 0.0
    ).astype(BF16)

    table = jnp.concatenate(
        [before_ref[...], fine_ref[...], after_ref[...], coarse_ref[...]], axis=0
    )
    h_send = dot(pick_send_t, table, ((0,), (0,))).astype(BF16)
    h_recv = dot(pick_recv_t, fine_ref[...], ((0,), (0,))).astype(BF16)
    inputs = jnp.concatenate([edges_ref[...], h_send, h_recv], axis=1)

    pre = dot(inputs, w_in_ref[...], ((1,), (0,)))
    sig = jax.nn.sigmoid(pre)
    act = (pre * sig).astype(BF16)
    hidden = dot(act, w_out_ref[...], ((1,), (0,)))
    centred = hidden - jnp.mean(hidden, axis=-1, keepdims=True)
    rstd = lax.rsqrt(jnp.mean(centred * centred, axis=-1, keepdims=True) + 1e-05)
    normed = centred * rstd
    live = lax.broadcasted_iota(jnp.int32, (rows, width), 0) < count_ref[0]
    dnorm = jnp.where(live, cot_ref[...].astype(F32), 0.0)
    dhidden = rstd * (
        dnorm
        - jnp.mean(dnorm, axis=-1, keepdims=True)
        - normed * jnp.mean(dnorm * normed, axis=-1, keepdims=True)
    )
    dhidden_b = dhidden.astype(BF16)
    dw_out_ref[...] = dot(act, dhidden_b, ((0,), (0,)))
    dact = dot(dhidden_b, w_out_ref[...], ((1,), (1,)))
    dpre_b = (dact * sig * (1.0 + pre * (1.0 - sig))).astype(BF16)
    dw_in_ref[...] = dot(inputs, dpre_b, ((0,), (0,)))
    dinputs = dot(dpre_b, w_in_ref[...], ((1,), (1,)))
    grad_edges_ref[...] = (dnorm + dinputs[:, :width]).astype(BF16)
    d_send = dinputs[:, width : 2 * width].astype(BF16)
    d_recv = dinputs[:, 2 * width :].astype(BF16)

    border = dot(pick_send_t[: 2 * RIM + nodes], d_send, ((1,), (0,)))
    down_ref[...] = border[:RIM].astype(BF16)
    up_ref[...] = border[RIM + nodes :].astype(BF16)
    own_ref[...] = border[RIM : RIM + nodes] + dot(pick_recv_t, d_recv, ((1,), (0,)))

    padded = dense_ref.shape[0]
    ids = ids_ref[pl.ds(dom, 1), :]
    name_t = jnp.where(
        lax.broadcasted_iota(jnp.int32, (padded, slots), 0) == ids, 1.0, 0.0
    ).astype(BF16)
    route = dot(name_t, pick_send_t[2 * RIM + nodes :], ((1,), (0,))).astype(BF16)
    dense_ref[...] = dot(route, d_send, ((1,), (0,)))

    r_in = dw_in_ref.shape[0] // (zs * YS * CORES)
    r_out = dw_out_ref.shape[0] // (zs * YS * CORES)
    r_coarse = padded // (zs * CORES)
    row_tiles = (r_in + r_out) // TILE
    col_tiles = width // LANES
    mine_first = core == 0

    def put(y, z, tile, first, second):
        keep_ref[y, z, tile] = jnp.where(mine_first, first, second).astype(BF16)
        send_ref[y, z, tile] = jnp.where(mine_first, second, first).astype(BF16)

    def per_z(z, carry):
        for y in range(YS):
            weight = []
            for c in range(CORES):
                block = (z * YS + y) * CORES + c
                weight.append(
                    jnp.concatenate(
                        [
                            dw_in_ref[pl.ds(pl.multiple_of(block * r_in, 8), r_in), :],
                            dw_out_ref[pl.ds(pl.multiple_of(block * r_out, 8), r_out), :],
                        ],
                        axis=0,
                    )
                )
            for rt in range(row_tiles):
                for ct in range(col_tiles):
                    at = (slice(rt * TILE, (rt + 1) * TILE), slice(ct * LANES, (ct + 1) * LANES))
                    put(y, z, rt * col_tiles + ct, weight[0][at], weight[1][at])
            for t in range(r_coarse // TILE):
                parts = [
                    dense_ref[
                        pl.ds(pl.multiple_of((c * zs + z) * r_coarse + t * TILE, TILE), TILE),
                        y * LANES : (y + 1) * LANES,
                    ]
                    for c in range(CORES)
                ]
                put(y, z, row_tiles * col_tiles + t, parts[0], parts[1])
        return carry

    lax.fori_loop(0, zs, per_z, 0)


def last_kernel(
    place_ref, ids_ref, mine_ref, other_ref, own_ref, from_up_ref, from_down_ref, coarse_ref, fine_ref
):
    ys, zs, tiles, tile, lanes = mine_ref.shape
    rows = zs * tiles * tile
    slots = ids_ref.shape[1]
    dom = place_ref[0]
    core = lax.rem(dom, CORES)
    ids = ids_ref[pl.ds(dom, 1), :]
    node = lax.broadcasted_iota(jnp.int32, (rows, slots), 0)
    pick_mine = jnp.where(node + core * rows == ids, 1.0, 0.0).astype(BF16)
    pick_other = jnp.where(node + (1 - core) * rows == ids, 1.0, 0.0).astype(BF16)
    for y in range(ys):
        total = dot(pick_mine, mine_ref[y].reshape(rows, lanes), ((0,), (0,))) + dot(
            pick_other, other_ref[y].reshape(rows, lanes), ((0,), (0,))
        )
        coarse_ref[:, y * lanes : (y + 1) * lanes] = total.astype(BF16)
    nodes = own_ref.shape[0]
    fine_ref[:RIM] = (own_ref[:RIM] + from_down_ref[...].astype(F32)).astype(BF16)
    fine_ref[RIM : nodes - RIM] = own_ref[RIM : nodes - RIM].astype(BF16)
    fine_ref[nodes - RIM :] = (own_ref[nodes - RIM :] + from_up_ref[...].astype(F32)).astype(BF16)


SMEM = pl.BlockSpec(memory_space=pltpu.SMEM)
VMEM = pl.BlockSpec(memory_space=pltpu.VMEM)


def added(parts):
    return jnp.sum(parts.astype(F32), axis=0).astype(BF16)


def shards(
    zs,
    xs,
    edges,
    cotangent,
    fine_latents,
    coarse_block,
    w_in,
    w_out,
    senders,
    receivers,
    edge_count,
    coarse_ids,
):
    rows, width = edges.shape[1:]
    nodes = fine_latents.shape[1]
    slots = coarse_block.shape[1]
    dom_axes = ("z", "y", "core")
    doms = zs * YS * CORES
    up = [(i, (i + 1) % doms) for i in range(doms)]
    down = [(j, i) for i, j in up]
    place = lax.axis_index(dom_axes).astype(jnp.int32).reshape(1)

    fine = fine_latents[0]
    before = lax.ppermute(fine[nodes - RIM :], dom_axes, up)
    after = lax.ppermute(fine[:RIM], dom_axes, down)

    r_weight = (w_in.shape[0] + w_out.shape[0]) // doms
    w_tiles = r_weight // TILE * (width // LANES)
    c_tiles = -(-NC // (zs * CORES * TILE))
    tiles = w_tiles + c_tiles
    padded = c_tiles * TILE * zs * CORES

    grad_edges, own, to_down, to_up, keep, send = pl.pallas_call(
        functools.partial(edge_kernel, zs),
        out_shape=(
            jax.ShapeDtypeStruct((rows, width), BF16),
            jax.ShapeDtypeStruct((nodes, width), F32),
            jax.ShapeDtypeStruct((RIM, width), BF16),
            jax.ShapeDtypeStruct((RIM, width), BF16),
            jax.ShapeDtypeStruct((YS, zs, tiles, TILE, LANES), BF16),
            jax.ShapeDtypeStruct((YS, zs, tiles, TILE, LANES), BF16),
        ),
        in_specs=[SMEM, SMEM] + [VMEM] * 11,
        out_specs=(VMEM,) * 6,
        scratch_shapes=[
            pltpu.VMEM(w_in.shape, F32),
            pltpu.VMEM(w_out.shape, F32),
            pltpu.VMEM((padded, width), F32),
        ],
        compiler_params=pltpu.CompilerParams(vmem_limit_bytes=44 * 2**20),
        cost_estimate=pl.CostEstimate(
            flops=2_200_000_000, bytes_accessed=6_000_000, transcendentals=rows * width
        ),
        name="edge_backward",
    )(
        edge_count,
        place,
        edges[0],
        cotangent[0],
        before,
        fine,
        after,
        coarse_block[0],
        w_in,
        w_out,
        senders.reshape(1, rows),
        receivers.reshape(1, rows),
        coarse_ids,
    )

    swap = [(0, 1), (1, 0)]
    other = lax.ppermute(send, "core", swap)
    from_up = lax.ppermute(to_down, dom_axes, down)
    from_down = lax.ppermute(to_up, dom_axes, up)
    part = (keep.astype(F32) + other.astype(F32)).astype(BF16)
    part = added(lax.all_to_all(part, "y", 0, 0, tiled=True).reshape(YS, zs, tiles, TILE, LANES))
    part = added(lax.all_to_all(part, "z", 0, 0, tiled=True).reshape(zs, tiles, TILE, LANES))
    weight, coarse = part[:w_tiles], part[w_tiles:]

    far = lax.ppermute(weight, "dp", swap)
    coarse = lax.all_to_all(
        jnp.broadcast_to(coarse[None], (zs, c_tiles, TILE, LANES)), "z", 0, 0, tiled=True
    )
    weight = (weight.astype(F32) + far.astype(F32)).astype(BF16)
    rest = [
        lax.ppermute(weight, "member", [(i, (i + k) % xs) for i in range(xs)])
        for k in range(1, xs)
    ]
    coarse = lax.all_to_all(
        jnp.broadcast_to(coarse[None], (YS, zs, c_tiles, TILE, LANES)), "y", 0, 0, tiled=True
    )
    terms = [term.astype(F32) for term in [weight] + rest]
    while len(terms) > 1:
        half = len(terms) // 2
        terms = [terms[i] + terms[i + half] for i in range(half)]
    weight = terms[0]
    samples_edges = rows * doms * xs * lax.axis_size("dp")
    weight = weight * (1.0 / math.sqrt(samples_edges))
    weight = weight.reshape(-1, width // LANES, TILE, LANES).transpose(0, 2, 1, 3)
    weight = weight.reshape(r_weight, width)
    r_in = w_in.shape[0] // doms

    coarse_other = lax.ppermute(coarse, "core", swap)
    grad_coarse, grad_fine = pl.pallas_call(
        last_kernel,
        out_shape=(
            jax.ShapeDtypeStruct((slots, width), BF16),
            jax.ShapeDtypeStruct((nodes, width), BF16),
        ),
        in_specs=[SMEM] + [VMEM] * 6,
        out_specs=(VMEM,) * 2,
        compiler_params=pltpu.CompilerParams(vmem_limit_bytes=16 * 2**20),
        name="coarse_rows",
    )(place, coarse_ids, coarse, coarse_other, own, from_up, from_down)
    return (
        grad_edges[None],
        grad_fine[None],
        grad_coarse[None],
        weight[:r_in],
        weight[r_in:],
    )


def solution(mesh):
    doms, xs, dps = (mesh.shape[name] for name in ("dom", "member", "dp"))
    zs = doms // (YS * CORES)
    split = Mesh(
        mesh.devices.reshape(zs, YS, CORES, xs, dps), ("z", "y", "core", "member", "dp")
    )
    dom = ("z", "y", "core")
    sample = ("member", "dp")
    latent = P(sample, dom, None)
    return jax.shard_map(
        functools.partial(shards, zs, xs),
        mesh=split,
        in_specs=(latent,) * 4 + (P(), P(), P(dom), P(dom), P(dom), P()),
        out_specs=(latent,) * 3 + (P(dom, None), P(dom, None)),
        check_vma=False,
    )
```

```python
import functools
import math

import jax
import jax.numpy as jnp
from jax import lax
from jax.experimental import pallas as pl
from jax.experimental.pallas import tpu as pltpu
from jax.sharding import Mesh
from jax.sharding import PartitionSpec as P

RIM = 16
NC = 642
YS = 4
CORES = 2
LANES = 128
TILE = 16

F32 = jnp.float32
BF16 = jnp.bfloat16

Y_ORDERS = ((0, 3, 1, 2), (0, 1, 3, 2))
Y_STEPS = ((1, 3), (3, 1))


def dot(left, right, dims):
    return lax.dot_general(left, right, (dims, ((), ())), preferred_element_type=F32)


def position(dom):
    core = lax.rem(dom, CORES)
    y = lax.rem(dom // CORES, YS)
    z = dom // (CORES * YS)
    return z, y, core


def bits(count):
    return count.bit_length() - 1


def picks(names, count):
    rows = lax.broadcasted_iota(jnp.int32, (count, names.shape[1]), 0)
    return jnp.where(rows == names, 1.0, 0.0).astype(BF16)


def load_kernel(
    count_ref,
    place_ref,
    edges_hbm,
    cot_hbm,
    fine_hbm,
    coarse_hbm,
    w_in_hbm,
    w_out_hbm,
    senders_hbm,
    receivers_hbm,
    ids_hbm,
    inputs_ref,
    cot_ref,
    pre_ref,
    w_in_ref,
    w_out_ref,
    pick_send_ref,
    pick_recv_ref,
    route_ref,
    fine_ref,
    coarse_ref,
    senders_ref,
    receivers_ref,
    ids_ref,
    edges_ref,
    sems,
):
    copies = [
        pltpu.make_async_copy(source, target, sems.at[i])
        for i, (source, target) in enumerate(
            [
                (senders_hbm, senders_ref),
                (receivers_hbm, receivers_ref),
                (fine_hbm, fine_ref),
                (coarse_hbm, coarse_ref),
                (ids_hbm, ids_ref),
                (edges_hbm, edges_ref),
                (w_in_hbm, w_in_ref),
                (cot_hbm, cot_ref),
                (w_out_hbm, w_out_ref),
            ]
        )
    ]
    for copy in copies:
        copy.start()
    rows, width = edges_ref.shape
    nodes = fine_ref.shape[0]
    slots = coarse_ref.shape[0]
    depth = 2 * RIM + nodes + slots
    dom = place_ref[0]

    for copy in copies[:5]:
        copy.wait()
    pick_send = picks(senders_ref[...], depth)
    pick_recv = picks(receivers_ref[...], nodes)
    pick_send_ref[...] = pick_send
    pick_recv_ref[...] = pick_recv
    name = picks(ids_ref[pl.ds(dom, 1), :], route_ref.shape[0])
    route_ref[...] = dot(name, pick_send[2 * RIM + nodes :], ((1,), (0,))).astype(BF16)
    h_send = dot(pick_send[RIM : RIM + nodes], fine_ref[...], ((0,), (0,))) + dot(
        pick_send[2 * RIM + nodes :], coarse_ref[...], ((0,), (0,))
    )
    h_recv = dot(pick_recv, fine_ref[...], ((0,), (0,)))
    copies[5].wait()
    inputs_ref[:, :width] = edges_ref[...]
    inputs_ref[:, width : 2 * width] = h_send.astype(BF16)
    inputs_ref[:, 2 * width :] = h_recv.astype(BF16)
    copies[6].wait()
    pre_ref[...] = dot(inputs_ref[...], w_in_ref[...], ((1,), (0,)))
    copies[7].wait()
    live = lax.broadcasted_iota(jnp.int32, (rows, width), 0) < count_ref[0]
    cot_ref[...] = jnp.where(live, cot_ref[...].astype(F32), 0.0).astype(BF16)
    copies[8].wait()


def edge_kernel(
    zs,
    place_ref,
    inputs_ref,
    cot_ref,
    pre_ref,
    w_in_ref,
    w_out_ref,
    pick_send_ref,
    pick_recv_ref,
    route_ref,
    before_ref,
    after_ref,
    grad_edges_ref,
    own_ref,
    down_ref,
    up_ref,
    keep_a_ref,
    send_a_ref,
    keep_b_ref,
    send_b_ref,
    dw_in_ref,
    dw_out_ref,
    dense_ref,
):
    rows, width = cot_ref.shape
    nodes = pick_recv_ref.shape[0]
    z_me, y_me, core_me = position(place_ref[0])

    pick_send = pick_send_ref[...]
    pick_recv = pick_recv_ref[...]
    h_halo = (
        dot(pick_send[:RIM], before_ref[...], ((0,), (0,)))
        + dot(pick_send[RIM + nodes : 2 * RIM + nodes], after_ref[...], ((0,), (0,)))
    ).astype(BF16)
    h_send = (inputs_ref[:, width : 2 * width] + h_halo).astype(BF16)
    inputs = jnp.concatenate(
        [inputs_ref[:, :width], h_send, inputs_ref[:, 2 * width :]], axis=1
    )
    pre = pre_ref[...] + dot(h_halo, w_in_ref[width : 2 * width, :], ((1,), (0,)))
    sig = jax.nn.sigmoid(pre)
    act = (pre * sig).astype(BF16)
    hidden = dot(act, w_out_ref[...], ((1,), (0,)))
    centred = hidden - jnp.mean(hidden, axis=-1, keepdims=True)
    rstd = lax.rsqrt(jnp.mean(centred * centred, axis=-1, keepdims=True) + 1e-05)
    normed = centred * rstd
    dnorm = cot_ref[...].astype(F32)
    dhidden = rstd * (
        dnorm
        - jnp.mean(dnorm, axis=-1, keepdims=True)
        - normed * jnp.mean(dnorm * normed, axis=-1, keepdims=True)
    )
    dhidden_b = dhidden.astype(BF16)
    dw_out_ref[...] = dot(act, dhidden_b, ((0,), (0,)))
    dact = dot(dhidden_b, w_out_ref[...], ((1,), (1,)))
    dpre_b = (dact * sig * (1.0 + pre * (1.0 - sig))).astype(BF16)
    dw_in_ref[...] = dot(inputs, dpre_b, ((0,), (0,)))
    dinputs = dot(dpre_b, w_in_ref[...], ((1,), (1,)))
    grad_edges_ref[...] = (dnorm + dinputs[:, :width]).astype(BF16)
    d_send = dinputs[:, width : 2 * width].astype(BF16)
    d_recv = dinputs[:, 2 * width :].astype(BF16)

    border = dot(pick_send[: 2 * RIM + nodes], d_send, ((1,), (0,)))
    down_ref[...] = border[:RIM].astype(BF16)
    up_ref[...] = border[RIM + nodes :].astype(BF16)
    own_ref[...] = border[RIM : RIM + nodes] + dot(pick_recv, d_recv, ((1,), (0,)))
    dense = dot(route_ref[...], d_send, ((1,), (0,)))
    for y in range(YS):
        dense_ref[y] = dense[:, y * LANES : (y + 1) * LANES]

    doms = zs * YS * CORES
    r_in = dw_in_ref.shape[0] // doms
    r_out = dw_out_ref.shape[0] // doms
    r_coarse = dense_ref.shape[1] // (zs * CORES)
    row_tiles = (r_in + r_out) // TILE
    col_tiles = width // LANES
    half = zs // 2

    def lay(base, y_order, refs, i, carry):
        index = base + i
        reverse = 0
        for b in range(bits(zs)):
            reverse = reverse | (((index >> b) & 1) << (bits(zs) - 1 - b))
        z = z_me ^ reverse
        for iy, ry in enumerate(y_order):
            y = y_me ^ ry
            for rc, ref in enumerate(refs):
                core = core_me ^ rc
                block = (z * YS + y) * CORES + core
                weight = jnp.concatenate(
                    [
                        dw_in_ref[pl.ds(pl.multiple_of(block * r_in, 8), r_in), :],
                        dw_out_ref[pl.ds(pl.multiple_of(block * r_out, 8), r_out), :],
                    ],
                    axis=0,
                ).astype(BF16)
                for rt in range(row_tiles):
                    for ct in range(col_tiles):
                        ref[iy, i, rt * col_tiles + ct] = weight[
                            rt * TILE : (rt + 1) * TILE, ct * LANES : (ct + 1) * LANES
                        ]
                first = pl.multiple_of((core * zs + z) * r_coarse, TILE)
                coarse = dense_ref[y, pl.ds(first, r_coarse), :].astype(BF16)
                for t in range(r_coarse // TILE):
                    ref[iy, i, row_tiles * col_tiles + t] = coarse[t * TILE : (t + 1) * TILE]
        return carry

    halves = ((keep_a_ref, send_a_ref), (keep_b_ref, send_b_ref))
    for h in range(2):
        lax.fori_loop(0, half, functools.partial(lay, h * half, Y_ORDERS[h], halves[h]), 0)


def last_kernel(
    z_order,
    scale,
    place_ref,
    ids_ref,
    mine_ref,
    other_ref,
    own_ref,
    from_up_ref,
    from_down_ref,
    weight_ref,
    weight_other_ref,
    coarse_ref,
    fine_ref,
    grad_in_ref,
    grad_out_ref,
):
    ys, zs, tiles, tile, lanes = mine_ref.shape
    per = tiles * tile
    rows = zs * per
    slots = ids_ref.shape[1]
    z_me, y_me, core_me = position(place_ref[0])
    ids = ids_ref[pl.ds(place_ref[0], 1), :]
    row = lax.broadcasted_iota(jnp.int32, (per, slots), 0)

    def pick(core):
        return jnp.concatenate(
            [
                jnp.where(row + (core * zs + (z_me ^ rz)) * per == ids, 1.0, 0.0)
                for rz in z_order
            ],
            axis=0,
        ).astype(BF16)

    pick_mine, pick_other = pick(core_me), pick(1 - core_me)
    for y in range(ys):
        at = y_me ^ y
        total = dot(pick_mine, mine_ref[at].reshape(rows, lanes), ((0,), (0,))) + dot(
            pick_other, other_ref[at].reshape(rows, lanes), ((0,), (0,))
        )
        coarse_ref[:, y * lanes : (y + 1) * lanes] = total.astype(BF16)
    nodes = own_ref.shape[0]
    fine_ref[:RIM] = (own_ref[:RIM] + from_down_ref[...].astype(F32)).astype(BF16)
    fine_ref[RIM : nodes - RIM] = own_ref[RIM : nodes - RIM].astype(BF16)
    fine_ref[nodes - RIM :] = (own_ref[nodes - RIM :] + from_up_ref[...].astype(F32)).astype(BF16)

    r_in = grad_in_ref.shape[0]
    col_tiles = grad_in_ref.shape[1] // lanes
    for t in range(weight_ref.shape[0]):
        value = (weight_ref[t].astype(F32) + weight_other_ref[t].astype(F32)) * scale
        cols = slice(t % col_tiles * lanes, (t % col_tiles + 1) * lanes)
        for part in range(0, tile, 8):
            first = t // col_tiles * tile + part
            if first < r_in:
                grad_in_ref[first : first + 8, cols] = value[part : part + 8]
            else:
                grad_out_ref[first - r_in : first - r_in + 8, cols] = value[part : part + 8]


SMEM = pl.BlockSpec(memory_space=pltpu.SMEM)
VMEM = pl.BlockSpec(memory_space=pltpu.VMEM)
HBM = pl.BlockSpec(memory_space=pltpu.HBM)


def plus(a, b):
    return (a.astype(F32) + b.astype(F32)).astype(BF16)


def swap(value, axis, mask):
    count = lax.axis_size(axis)
    return lax.ppermute(value, axis, [(i, i ^ mask) for i in range(count)])


def shards(
    zs,
    xs,
    edges,
    cotangent,
    fine_latents,
    coarse_block,
    w_in,
    w_out,
    senders,
    receivers,
    edge_count,
    coarse_ids,
):
    rows, width = edges.shape[1:]
    nodes = fine_latents.shape[1]
    slots = coarse_block.shape[1]
    depth = 2 * RIM + nodes + slots
    dom_axes = ("z", "y", "core")
    doms = zs * YS * CORES
    up = [(i, (i + 1) % doms) for i in range(doms)]
    down = [(j, i) for i, j in up]
    place = lax.axis_index(dom_axes).astype(jnp.int32).reshape(1)

    fine = fine_latents[0]
    before = lax.ppermute(fine[nodes - RIM :], dom_axes, up)
    after = lax.ppermute(fine[:RIM], dom_axes, down)

    r_weight = (w_in.shape[0] + w_out.shape[0]) // doms
    w_tiles = r_weight // TILE * (width // LANES)
    c_tiles = -(-NC // (zs * CORES * TILE))
    tiles = w_tiles + c_tiles
    padded = c_tiles * TILE * zs * CORES
    half = zs // 2

    shape = jax.ShapeDtypeStruct
    loaded = pl.pallas_call(
        load_kernel,
        out_shape=(
            shape((rows, 3 * width), BF16),
            shape((rows, width), BF16),
            shape((rows, width), F32),
            shape(w_in.shape, BF16),
            shape(w_out.shape, BF16),
            shape((depth, rows), BF16),
            shape((nodes, rows), BF16),
            shape((padded, rows), BF16),
        ),
        in_specs=[SMEM, SMEM] + [HBM] * 9,
        out_specs=(VMEM,) * 8,
        scratch_shapes=[
            pltpu.VMEM((nodes, width), BF16),
            pltpu.VMEM((slots, width), BF16),
            pltpu.VMEM((1, rows), jnp.int32),
            pltpu.VMEM((1, rows), jnp.int32),
            pltpu.VMEM(coarse_ids.shape, jnp.int32),
            pltpu.VMEM((rows, width), BF16),
            pltpu.SemaphoreType.DMA((9,)),
        ],
        compiler_params=pltpu.CompilerParams(vmem_limit_bytes=24 * 2**20),
        cost_estimate=pl.CostEstimate(
            flops=600_000_000, bytes_accessed=6_000_000, transcendentals=0
        ),
        name="edge_inputs",
    )(
        edge_count,
        place,
        edges[0],
        cotangent[0],
        fine,
        coarse_block[0],
        w_in,
        w_out,
        senders.reshape(1, rows),
        receivers.reshape(1, rows),
        coarse_ids,
    )

    block = shape((YS, half, tiles, TILE, LANES), BF16)
    grad_edges, own, to_down, to_up, keep_a, send_a, keep_b, send_b = pl.pallas_call(
        functools.partial(edge_kernel, zs),
        out_shape=(
            shape((rows, width), BF16),
            shape((nodes, width), F32),
            shape((RIM, width), BF16),
            shape((RIM, width), BF16),
            block,
            block,
            block,
            block,
        ),
        in_specs=[SMEM] + [VMEM] * 10,
        out_specs=(VMEM,) * 8,
        scratch_shapes=[
            pltpu.VMEM(w_in.shape, F32),
            pltpu.VMEM(w_out.shape, F32),
            pltpu.VMEM((YS, padded, LANES), F32),
        ],
        compiler_params=pltpu.CompilerParams(vmem_limit_bytes=36 * 2**20),
        cost_estimate=pl.CostEstimate(
            flops=1_800_000_000, bytes_accessed=6_000_000, transcendentals=rows * width
        ),
        name="edge_backward",
    )(place, *loaded, before, after)

    other_a = swap(send_a, "core", 1)
    other_b = swap(send_b, "core", 1)
    two = YS // 2

    def split_plus(a, b, at):
        return plus(a[:at], b[:at]), plus(a[at:], b[at:])

    keep_a, send_a = split_plus(keep_a, other_a, two)
    keep_b, send_b = split_plus(keep_b, other_b, two)
    send_a, to_down, to_up = lax.optimization_barrier((send_a, to_down, to_up))
    other_a = swap(send_a, "y", Y_STEPS[0][0])
    other_b = swap(send_b, "y", Y_STEPS[1][0])
    from_up = lax.ppermute(to_down, dom_axes, down)
    from_down = lax.ppermute(to_up, dom_axes, up)
    other_a, other_b, from_up, from_down = lax.optimization_barrier(
        (other_a, other_b, from_up, from_down)
    )
    keep_a, send_a = split_plus(keep_a, other_a, 1)
    keep_b, send_b = split_plus(keep_b, other_b, 1)
    other_b = swap(send_b, "y", Y_STEPS[1][1])
    other_a = swap(send_a, "y", Y_STEPS[0][1])
    send = plus(keep_b[0], other_b[0])
    keep = plus(keep_a[0], other_a[0])
    masks = [1 << b for b in range(bits(zs))]
    for mask in masks[:-1]:
        other = swap(send, "z", mask)
        keep, send = split_plus(keep, other, keep.shape[0] // 2)
    keep, send = keep[0], send[0]
    other = swap(jnp.concatenate([send, keep[w_tiles:]], axis=0), "z", masks[-1])
    weight = plus(keep[:w_tiles], other[:w_tiles])
    coarse = jnp.stack(
        [
            plus(keep[w_tiles:], other[w_tiles:tiles]),
            plus(send[w_tiles:], other[tiles:]),
        ]
    )

    x_masks = [2 * (1 << b) - 1 for b in range(bits(xs))]
    steps = [("dp", 1)] + [("member", mask) for mask in x_masks[:-1]]
    z_order = [0, masks[-1]]
    for i in range(max(len(steps), len(masks) - 1)):
        weight_other, coarse_other = weight, coarse
        if i < len(steps):
            weight_other = swap(weight, *steps[i])
        if i < len(masks) - 1:
            mask = masks[-2 - i]
            coarse_other = swap(coarse, "z", mask)
        weight_other, coarse_other = lax.optimization_barrier((weight_other, coarse_other))
        if i < len(steps):
            weight = plus(weight, weight_other)
        if i < len(masks) - 1:
            coarse = jnp.concatenate([coarse, coarse_other], axis=0)
            z_order = z_order + [r ^ mask for r in z_order]
    weight_other = swap(weight, "member", x_masks[-1])
    others = [swap(coarse, "y", r) for r in range(1, YS)]
    weight_other, *others = lax.optimization_barrier((weight_other, *others))
    coarse = jnp.stack([coarse] + others)
    coarse_other = swap(coarse, "core", 1)

    all_edges = rows * doms * xs * lax.axis_size("dp")
    grad_coarse, grad_fine, grad_in, grad_out = pl.pallas_call(
        functools.partial(last_kernel, z_order, 1.0 / math.sqrt(all_edges)),
        out_shape=(
            shape((slots, width), BF16),
            shape((nodes, width), BF16),
            shape((w_in.shape[0] // doms, width), F32),
            shape((w_out.shape[0] // doms, width), F32),
        ),
        in_specs=[SMEM] + [VMEM] * 8,
        out_specs=(VMEM,) * 4,
        compiler_params=pltpu.CompilerParams(vmem_limit_bytes=16 * 2**20),
        name="last_sums",
    )(
        place,
        coarse_ids,
        coarse,
        coarse_other,
        own,
        from_up,
        from_down,
        weight,
        weight_other,
    )
    return (grad_edges[None], grad_fine[None], grad_coarse[None], grad_in, grad_out)


def solution(mesh):
    doms, xs, dps = (mesh.shape[name] for name in ("dom", "member", "dp"))
    zs = doms // (YS * CORES)
    split = Mesh(
        mesh.devices.reshape(zs, YS, CORES, xs, dps), ("z", "y", "core", "member", "dp")
    )
    dom = ("z", "y", "core")
    sample = ("member", "dp")
    latent = P(sample, dom, None)
    return jax.shard_map(
        functools.partial(shards, zs, xs),
        mesh=split,
        in_specs=(latent,) * 4 + (P(), P(), P(dom), P(dom), P(dom), P()),
        out_specs=(latent,) * 3 + (P(dom, None), P(dom, None)),
        check_vma=False,
    )
```

```python
import functools
import math

import jax
import jax.numpy as jnp
from jax import lax
from jax.experimental import pallas as pl
from jax.experimental.pallas import tpu as pltpu
from jax.sharding import Mesh
from jax.sharding import PartitionSpec as P

RIM = 16
NC = 642
YS = 4
CORES = 2
LANES = 128
TILE = 16

F32 = jnp.float32
BF16 = jnp.bfloat16

Y_ORDERS = ((0, 3, 1, 2), (0, 1, 3, 2))
Y_STEPS = ((1, 3), (3, 1))


def dot(left, right, dims):
    return lax.dot_general(left, right, (dims, ((), ())), preferred_element_type=F32)


def position(dom):
    core = lax.rem(dom, CORES)
    y = lax.rem(dom // CORES, YS)
    z = dom // (CORES * YS)
    return z, y, core


def bits(count):
    return count.bit_length() - 1


def picks(names, count):
    rows = lax.broadcasted_iota(jnp.int32, (count, names.shape[1]), 0)
    return jnp.where(rows == names, 1.0, 0.0).astype(BF16)


def edge_kernel(
    zs,
    count_ref,
    place_ref,
    edges_hbm,
    cot_hbm,
    fine_hbm,
    coarse_hbm,
    w_in_hbm,
    w_out_hbm,
    senders_hbm,
    receivers_hbm,
    ids_hbm,
    near_ref,
    next_ref,
    grad_edges_hbm,
    own_ref,
    near_out_ref,
    next_out_ref,
    keep_a_hbm,
    send_a_hbm,
    keep_b_hbm,
    send_b_hbm,
    edges_ref,
    cot_ref,
    fine_ref,
    coarse_ref,
    w_in_ref,
    w_out_ref,
    senders_ref,
    receivers_ref,
    ids_ref,
    grad_edges_ref,
    keep_a_ref,
    send_a_ref,
    keep_b_ref,
    send_b_ref,
    dw_in_ref,
    dw_out_ref,
    dense_ref,
    in_sems,
    out_sems,
):
    copies = [
        pltpu.make_async_copy(source, target, in_sems.at[i])
        for i, (source, target) in enumerate(
            [
                (senders_hbm, senders_ref),
                (receivers_hbm, receivers_ref),
                (fine_hbm, fine_ref),
                (coarse_hbm, coarse_ref),
                (edges_hbm, edges_ref),
                (w_in_hbm, w_in_ref),
                (ids_hbm, ids_ref),
                (w_out_hbm, w_out_ref),
                (cot_hbm, cot_ref),
            ]
        )
    ]
    for copy in copies:
        copy.start()
    rows, width = edges_ref.shape
    nodes = fine_ref.shape[0]
    slots = coarse_ref.shape[0]
    depth = 2 * RIM + nodes + slots
    dom = place_ref[0]
    z_me, y_me, core_me = position(dom)

    for copy in copies[:4]:
        copy.wait()
    pick_send = picks(senders_ref[...], depth)
    pick_recv = picks(receivers_ref[...], nodes)
    even = core_me == 0
    before = jnp.where(even, next_ref[...], near_ref[...])
    after = jnp.where(even, near_ref[...], next_ref[...])
    table = jnp.concatenate([before, fine_ref[...], after, coarse_ref[...]], axis=0)
    h_send = dot(pick_send, table, ((0,), (0,))).astype(BF16)
    h_recv = dot(pick_recv, fine_ref[...], ((0,), (0,))).astype(BF16)
    copies[4].wait()
    inputs = jnp.concatenate([edges_ref[...], h_send, h_recv], axis=1)
    copies[5].wait()
    pre = dot(inputs, w_in_ref[...], ((1,), (0,)))
    sig = jax.nn.sigmoid(pre)
    act = (pre * sig).astype(BF16)
    for copy in copies[6:]:
        copy.wait()
    hidden = dot(act, w_out_ref[...], ((1,), (0,)))
    centred = hidden - jnp.mean(hidden, axis=-1, keepdims=True)
    rstd = lax.rsqrt(jnp.mean(centred * centred, axis=-1, keepdims=True) + 1e-05)
    normed = centred * rstd
    live = lax.broadcasted_iota(jnp.int32, (rows, width), 0) < count_ref[0]
    dnorm = jnp.where(live, cot_ref[...].astype(F32), 0.0)
    dhidden = rstd * (
        dnorm
        - jnp.mean(dnorm, axis=-1, keepdims=True)
        - normed * jnp.mean(dnorm * normed, axis=-1, keepdims=True)
    )
    dhidden_b = dhidden.astype(BF16)
    dw_out_ref[...] = dot(act, dhidden_b, ((0,), (0,)))
    dact = dot(dhidden_b, w_out_ref[...], ((1,), (1,)))
    dpre_b = (dact * sig * (1.0 + pre * (1.0 - sig))).astype(BF16)
    dw_in_ref[...] = dot(inputs, dpre_b, ((0,), (0,)))
    dinputs = dot(dpre_b, w_in_ref[...], ((1,), (1,)))
    grad_edges_ref[...] = (dnorm + dinputs[:, :width]).astype(BF16)
    d_send = dinputs[:, width : 2 * width].astype(BF16)
    d_recv = dinputs[:, 2 * width :].astype(BF16)

    border = dot(pick_send[: 2 * RIM + nodes], d_send, ((1,), (0,)))
    down, up = border[:RIM], border[RIM + nodes :]
    near_out_ref[...] = jnp.where(even, up, down).astype(BF16)
    next_out_ref[...] = jnp.where(even, down, up).astype(BF16)
    own_ref[...] = border[RIM : RIM + nodes] + dot(pick_recv, d_recv, ((1,), (0,)))
    name = picks(ids_ref[pl.ds(dom, 1), :], dense_ref.shape[1])
    route = dot(name, pick_send[2 * RIM + nodes :], ((1,), (0,))).astype(BF16)
    dense = dot(route, d_send, ((1,), (0,)))
    for y in range(YS):
        dense_ref[y] = dense[:, y * LANES : (y + 1) * LANES]

    doms = zs * YS * CORES
    r_in = dw_in_ref.shape[0] // doms
    r_out = dw_out_ref.shape[0] // doms
    r_coarse = dense_ref.shape[1] // (zs * CORES)
    row_tiles = (r_in + r_out) // TILE
    col_tiles = width // LANES
    half = zs // 2

    def lay(base, y_order, refs, i, carry):
        index = base + i
        reverse = 0
        for b in range(bits(zs)):
            reverse = reverse | (((index >> b) & 1) << (bits(zs) - 1 - b))
        z = z_me ^ reverse
        for iy, ry in enumerate(y_order):
            y = y_me ^ ry
            for rc, ref in enumerate(refs):
                core = core_me ^ rc
                block = (z * YS + y) * CORES + core
                weight = jnp.concatenate(
                    [
                        dw_in_ref[pl.ds(pl.multiple_of(block * r_in, 8), r_in), :],
                        dw_out_ref[pl.ds(pl.multiple_of(block * r_out, 8), r_out), :],
                    ],
                    axis=0,
                ).astype(BF16)
                for rt in range(row_tiles):
                    for ct in range(col_tiles):
                        ref[iy, i, rt * col_tiles + ct] = weight[
                            rt * TILE : (rt + 1) * TILE, ct * LANES : (ct + 1) * LANES
                        ]
                first = pl.multiple_of((core * zs + z) * r_coarse, TILE)
                coarse = dense_ref[y, pl.ds(first, r_coarse), :].astype(BF16)
                for t in range(r_coarse // TILE):
                    ref[iy, i, row_tiles * col_tiles + t] = coarse[t * TILE : (t + 1) * TILE]
        return carry

    outs = [
        pltpu.make_async_copy(source, target, out_sems.at[i])
        for i, (source, target) in enumerate(
            [
                (grad_edges_ref, grad_edges_hbm),
                (send_a_ref, send_a_hbm),
                (keep_a_ref, keep_a_hbm),
                (send_b_ref, send_b_hbm),
                (keep_b_ref, keep_b_hbm),
            ]
        )
    ]
    outs[0].start()
    halves = ((keep_a_ref, send_a_ref), (keep_b_ref, send_b_ref))
    for h in range(2):
        lax.fori_loop(0, half, functools.partial(lay, h * half, Y_ORDERS[h], halves[h]), 0)
        outs[2 * h + 1].start()
        outs[2 * h + 2].start()
    for out in outs:
        out.wait()


def last_kernel(
    z_order,
    scale,
    place_ref,
    ids_ref,
    mine_ref,
    other_ref,
    own_ref,
    near_ref,
    next_ref,
    weight_ref,
    weight_other_ref,
    coarse_ref,
    fine_ref,
    grad_in_ref,
    grad_out_ref,
):
    ys, zs, tiles, tile, lanes = mine_ref.shape
    per = tiles * tile
    rows = zs * per
    slots = ids_ref.shape[1]
    z_me, y_me, core_me = position(place_ref[0])
    ids = ids_ref[pl.ds(place_ref[0], 1), :]
    row = lax.broadcasted_iota(jnp.int32, (per, slots), 0)

    def pick(core):
        return jnp.concatenate(
            [
                jnp.where(row + (core * zs + (z_me ^ rz)) * per == ids, 1.0, 0.0)
                for rz in z_order
            ],
            axis=0,
        ).astype(BF16)

    pick_mine, pick_other = pick(core_me), pick(1 - core_me)
    for y in range(ys):
        turn = y_me ^ y
        at = turn ^ (turn >> 1)
        total = dot(pick_mine, mine_ref[at].reshape(rows, lanes), ((0,), (0,))) + dot(
            pick_other, other_ref[at].reshape(rows, lanes), ((0,), (0,))
        )
        coarse_ref[:, y * lanes : (y + 1) * lanes] = total.astype(BF16)
    nodes = own_ref.shape[0]
    even = core_me == 0
    near, following = near_ref[...].astype(F32), next_ref[...].astype(F32)
    from_down = jnp.where(even, following, near)
    from_up = jnp.where(even, near, following)
    fine_ref[:RIM] = (own_ref[:RIM] + from_down).astype(BF16)
    fine_ref[RIM : nodes - RIM] = own_ref[RIM : nodes - RIM].astype(BF16)
    fine_ref[nodes - RIM :] = (own_ref[nodes - RIM :] + from_up).astype(BF16)

    r_in = grad_in_ref.shape[0]
    col_tiles = grad_in_ref.shape[1] // lanes
    for t in range(weight_ref.shape[0]):
        value = (weight_ref[t].astype(F32) + weight_other_ref[t].astype(F32)) * scale
        cols = slice(t % col_tiles * lanes, (t % col_tiles + 1) * lanes)
        for part in range(0, tile, 8):
            first = t // col_tiles * tile + part
            if first < r_in:
                grad_in_ref[first : first + 8, cols] = value[part : part + 8]
            else:
                grad_out_ref[first - r_in : first - r_in + 8, cols] = value[part : part + 8]


SMEM = pl.BlockSpec(memory_space=pltpu.SMEM)
VMEM = pl.BlockSpec(memory_space=pltpu.VMEM)
HBM = pl.BlockSpec(memory_space=pltpu.HBM)


def plus(a, b):
    return (a.astype(F32) + b.astype(F32)).astype(BF16)


def swap(value, axis, mask):
    count = lax.axis_size(axis)
    return lax.ppermute(value, axis, [(i, i ^ mask) for i in range(count)])


def shards(
    zs,
    xs,
    edges,
    cotangent,
    fine_latents,
    coarse_block,
    w_in,
    w_out,
    senders,
    receivers,
    edge_count,
    coarse_ids,
):
    rows, width = edges.shape[1:]
    nodes = fine_latents.shape[1]
    slots = coarse_block.shape[1]
    depth = 2 * RIM + nodes + slots
    dom_axes = ("z", "y", "core")
    doms = zs * YS * CORES
    beside = [(i, (i + 1 - 2 * (i % 2)) % doms) for i in range(doms)]
    across = [(i, (i - 1 + 2 * (i % 2)) % doms) for i in range(doms)]
    place = lax.axis_index(dom_axes).astype(jnp.int32).reshape(1)
    even = lax.axis_index("core") == 0

    fine = fine_latents[0]
    first, last = fine[:RIM], fine[nodes - RIM :]
    following = lax.ppermute(jnp.where(even, first, last), dom_axes, across)
    near = lax.ppermute(jnp.where(even, last, first), dom_axes, beside)

    r_weight = (w_in.shape[0] + w_out.shape[0]) // doms
    w_tiles = r_weight // TILE * (width // LANES)
    c_tiles = -(-NC // (zs * CORES * TILE))
    tiles = w_tiles + c_tiles
    padded = c_tiles * TILE * zs * CORES
    half = zs // 2

    shape = jax.ShapeDtypeStruct
    block = (YS, half, tiles, TILE, LANES)
    grad_edges, own, near_out, next_out, keep_a, send_a, keep_b, send_b = pl.pallas_call(
        functools.partial(edge_kernel, zs),
        out_shape=(
            shape((rows, width), BF16),
            shape((nodes, width), F32),
            shape((RIM, width), BF16),
            shape((RIM, width), BF16),
        )
        + (shape(block, BF16),) * 4,
        in_specs=[SMEM, SMEM] + [HBM] * 9 + [VMEM] * 2,
        out_specs=(HBM, VMEM, VMEM, VMEM) + (HBM,) * 4,
        scratch_shapes=[
            pltpu.VMEM((rows, width), BF16),
            pltpu.VMEM((rows, width), BF16),
            pltpu.VMEM((nodes, width), BF16),
            pltpu.VMEM((slots, width), BF16),
            pltpu.VMEM(w_in.shape, BF16),
            pltpu.VMEM(w_out.shape, BF16),
            pltpu.VMEM((1, rows), jnp.int32),
            pltpu.VMEM((1, rows), jnp.int32),
            pltpu.VMEM(coarse_ids.shape, jnp.int32),
            pltpu.VMEM((rows, width), BF16),
        ]
        + [pltpu.VMEM(block, BF16)] * 4
        + [
            pltpu.VMEM(w_in.shape, F32),
            pltpu.VMEM(w_out.shape, F32),
            pltpu.VMEM((YS, padded, LANES), F32),
            pltpu.SemaphoreType.DMA((9,)),
            pltpu.SemaphoreType.DMA((5,)),
        ],
        compiler_params=pltpu.CompilerParams(vmem_limit_bytes=60 * 2**20),
        cost_estimate=pl.CostEstimate(
            flops=2_200_000_000, bytes_accessed=6_000_000, transcendentals=rows * width
        ),
        name="edge_backward",
    )(
        edge_count,
        place,
        edges[0],
        cotangent[0],
        fine,
        coarse_block[0],
        w_in,
        w_out,
        senders.reshape(1, rows),
        receivers.reshape(1, rows),
        coarse_ids,
        near,
        following,
    )

    other_a = swap(send_a, "core", 1)
    other_b = swap(send_b, "core", 1)
    two = YS // 2

    def split_plus(a, b, at):
        return plus(a[:at], b[:at]), plus(a[at:], b[at:])

    keep_a, send_a = split_plus(keep_a, other_a, two)
    keep_b, send_b = split_plus(keep_b, other_b, two)
    send_a, near_out, next_out = lax.optimization_barrier((send_a, near_out, next_out))
    other_a = swap(send_a, "y", Y_STEPS[0][0])
    other_b = swap(send_b, "y", Y_STEPS[1][0])
    following = lax.ppermute(next_out, dom_axes, across)
    near = lax.ppermute(near_out, dom_axes, beside)
    keep_a, send_a = split_plus(keep_a, other_a, 1)
    keep_b, send_b = split_plus(keep_b, other_b, 1)
    other_b = swap(send_b, "y", Y_STEPS[1][1])
    other_a = swap(send_a, "y", Y_STEPS[0][1])
    send = plus(keep_b[0], other_b[0])
    keep = plus(keep_a[0], other_a[0])
    masks = [1 << b for b in range(bits(zs))]
    for mask in masks[:-1]:
        other = swap(send, "z", mask)
        if mask == 1:
            other, near, following = lax.optimization_barrier((other, near, following))
        keep, send = split_plus(keep, other, keep.shape[0] // 2)
    keep, send = keep[0], send[0]
    other = swap(jnp.concatenate([send, keep[w_tiles:]], axis=0), "z", masks[-1])
    weight = plus(keep[:w_tiles], other[:w_tiles])
    coarse = jnp.stack(
        [
            plus(keep[w_tiles:], other[w_tiles:tiles]),
            plus(send[w_tiles:], other[tiles:]),
        ]
    )

    x_masks = [2 * (1 << b) - 1 for b in range(bits(xs))]
    weight_steps = [("dp", 1)] + [("member", mask) for mask in x_masks]
    coarse_steps = [("z", mask) for mask in reversed(masks[:-1])] + [("y", 1), ("y", 3)]
    z_order = [0, masks[-1]]
    for mask in reversed(masks[:-1]):
        z_order = z_order + [r ^ mask for r in z_order]
    for i, (axis, mask) in enumerate(coarse_steps):
        coarse_other = swap(coarse, axis, mask)
        if i < len(weight_steps):
            weight_other = swap(weight, *weight_steps[i])
            weight_other, coarse_other = lax.optimization_barrier((weight_other, coarse_other))
            if i < len(weight_steps) - 1:
                weight = plus(weight, weight_other)
        coarse = jnp.concatenate([coarse, coarse_other], axis=0)
    coarse = coarse.reshape(YS, zs, c_tiles, TILE, LANES)
    coarse_other = swap(coarse, "core", 1)

    all_edges = rows * doms * xs * lax.axis_size("dp")
    grad_coarse, grad_fine, grad_in, grad_out = pl.pallas_call(
        functools.partial(last_kernel, z_order, 1.0 / math.sqrt(all_edges)),
        out_shape=(
            shape((slots, width), BF16),
            shape((nodes, width), BF16),
            shape((w_in.shape[0] // doms, width), F32),
            shape((w_out.shape[0] // doms, width), F32),
        ),
        in_specs=[SMEM] + [VMEM] * 8,
        out_specs=(VMEM,) * 4,
        compiler_params=pltpu.CompilerParams(vmem_limit_bytes=16 * 2**20),
        name="last_sums",
    )(
        place,
        coarse_ids,
        coarse,
        coarse_other,
        own,
        near,
        following,
        weight,
        weight_other,
    )
    return (grad_edges[None], grad_fine[None], grad_coarse[None], grad_in, grad_out)


def solution(mesh):
    doms, xs, dps = (mesh.shape[name] for name in ("dom", "member", "dp"))
    zs = doms // (YS * CORES)
    split = Mesh(
        mesh.devices.reshape(zs, YS, CORES, xs, dps), ("z", "y", "core", "member", "dp")
    )
    dom = ("z", "y", "core")
    sample = ("member", "dp")
    latent = P(sample, dom, None)
    return jax.shard_map(
        functools.partial(shards, zs, xs),
        mesh=split,
        in_specs=(latent,) * 4 + (P(), P(), P(dom), P(dom), P(dom), P()),
        out_specs=(latent,) * 3 + (P(dom, None), P(dom, None)),
        check_vma=False,
    )
```

```python
import functools
import math

import jax
import jax.numpy as jnp
from jax import lax
from jax.experimental import pallas as pl
from jax.experimental.pallas import tpu as pltpu
from jax.sharding import Mesh
from jax.sharding import PartitionSpec as P

RIM = 16
NC = 642
YS = 4
CORES = 2
LANES = 128
TILE = 16

F32 = jnp.float32
BF16 = jnp.bfloat16

Y_ORDERS = ((0, 3, 1, 2), (0, 1, 3, 2))
Y_STEPS = ((1, 3), (3, 1))


def dot(left, right, dims):
    return lax.dot_general(left, right, (dims, ((), ())), preferred_element_type=F32)


def position(dom):
    core = lax.rem(dom, CORES)
    y = lax.rem(dom // CORES, YS)
    z = dom // (CORES * YS)
    return z, y, core


def bits(count):
    return count.bit_length() - 1


def picks(names, count):
    rows = lax.broadcasted_iota(jnp.int32, (count, names.shape[1]), 0)
    return jnp.where(rows == names, 1.0, 0.0).astype(BF16)


def edge_kernel(
    zs,
    count_ref,
    place_ref,
    edges_hbm,
    cot_hbm,
    fine_hbm,
    coarse_hbm,
    w_in_hbm,
    w_out_hbm,
    senders_hbm,
    receivers_hbm,
    ids_hbm,
    near_ref,
    next_ref,
    grad_edges_hbm,
    own_ref,
    near_out_ref,
    next_out_ref,
    keep_a_hbm,
    send_a_hbm,
    keep_b_hbm,
    send_b_hbm,
    edges_ref,
    cot_ref,
    fine_ref,
    coarse_ref,
    w_in_ref,
    w_out_ref,
    senders_ref,
    receivers_ref,
    ids_ref,
    grad_edges_ref,
    keep_a_ref,
    send_a_ref,
    keep_b_ref,
    send_b_ref,
    dw_in_ref,
    dw_out_ref,
    dense_ref,
    in_sems,
    out_sems,
):
    copies = [
        pltpu.make_async_copy(source, target, in_sems.at[i])
        for i, (source, target) in enumerate(
            [
                (senders_hbm, senders_ref),
                (receivers_hbm, receivers_ref),
                (fine_hbm, fine_ref),
                (coarse_hbm, coarse_ref),
                (edges_hbm, edges_ref),
                (w_in_hbm, w_in_ref),
                (ids_hbm, ids_ref),
                (w_out_hbm, w_out_ref),
                (cot_hbm, cot_ref),
            ]
        )
    ]
    for copy in copies:
        copy.start()
    rows, width = edges_ref.shape
    nodes = fine_ref.shape[0]
    slots = coarse_ref.shape[0]
    depth = 2 * RIM + nodes + slots
    dom = place_ref[0]
    z_me, y_me, core_me = position(dom)

    for copy in copies[:4]:
        copy.wait()
    pick_send = picks(senders_ref[...], depth)
    pick_recv = picks(receivers_ref[...], nodes)
    even = core_me == 0
    before = jnp.where(even, next_ref[...], near_ref[...])
    after = jnp.where(even, near_ref[...], next_ref[...])
    table = jnp.concatenate([before, fine_ref[...], after, coarse_ref[...]], axis=0)
    h_send = dot(pick_send, table, ((0,), (0,))).astype(BF16)
    h_recv = dot(pick_recv, fine_ref[...], ((0,), (0,))).astype(BF16)
    copies[4].wait()
    inputs = jnp.concatenate([edges_ref[...], h_send, h_recv], axis=1)
    copies[5].wait()
    pre = dot(inputs, w_in_ref[...], ((1,), (0,)))
    sig = jax.nn.sigmoid(pre)
    act = (pre * sig).astype(BF16)
    for copy in copies[6:]:
        copy.wait()
    hidden = dot(act, w_out_ref[...], ((1,), (0,)))
    centred = hidden - jnp.mean(hidden, axis=-1, keepdims=True)
    rstd = lax.rsqrt(jnp.mean(centred * centred, axis=-1, keepdims=True) + 1e-05)
    normed = centred * rstd
    live = lax.broadcasted_iota(jnp.int32, (rows, width), 0) < count_ref[0]
    dnorm = jnp.where(live, cot_ref[...].astype(F32), 0.0)
    dhidden = rstd * (
        dnorm
        - jnp.mean(dnorm, axis=-1, keepdims=True)
        - normed * jnp.mean(dnorm * normed, axis=-1, keepdims=True)
    )
    dhidden_b = dhidden.astype(BF16)
    dw_out_ref[...] = dot(act, dhidden_b, ((0,), (0,)))
    dact = dot(dhidden_b, w_out_ref[...], ((1,), (1,)))
    dpre_b = (dact * sig * (1.0 + pre * (1.0 - sig))).astype(BF16)
    dw_in_ref[...] = dot(inputs, dpre_b, ((0,), (0,)))
    dinputs = dot(dpre_b, w_in_ref[...], ((1,), (1,)))
    grad_edges_ref[...] = (dnorm + dinputs[:, :width]).astype(BF16)
    d_send = dinputs[:, width : 2 * width].astype(BF16)
    d_recv = dinputs[:, 2 * width :].astype(BF16)

    border = dot(pick_send[: 2 * RIM + nodes], d_send, ((1,), (0,)))
    down, up = border[:RIM], border[RIM + nodes :]
    near_out_ref[...] = jnp.where(even, up, down).astype(BF16)
    next_out_ref[...] = jnp.where(even, down, up).astype(BF16)
    own_ref[...] = border[RIM : RIM + nodes] + dot(pick_recv, d_recv, ((1,), (0,)))
    name = picks(ids_ref[pl.ds(dom, 1), :], dense_ref.shape[1])
    route = dot(name, pick_send[2 * RIM + nodes :], ((1,), (0,)))
    extent = (dense_ref.shape[1], 2 * RIM + nodes)
    lane = lax.broadcasted_iota(jnp.int32, extent, 1)
    down_row = jnp.where((lane < RIM) & (dom == 0), NC + lane, -1)
    end_row = jnp.where(
        (lane >= RIM + nodes) & (dom == zs * YS * CORES - 1), NC + lane - nodes, down_row
    )
    ends = jnp.where(lax.broadcasted_iota(jnp.int32, extent, 0) == end_row, 1.0, 0.0)
    route = route + dot(ends.astype(BF16), pick_send[: 2 * RIM + nodes], ((1,), (0,)))
    route = route.astype(BF16)
    dense = dot(route, d_send, ((1,), (0,)))
    for y in range(YS):
        dense_ref[y] = dense[:, y * LANES : (y + 1) * LANES]

    doms = zs * YS * CORES
    r_in = dw_in_ref.shape[0] // doms
    r_out = dw_out_ref.shape[0] // doms
    r_coarse = dense_ref.shape[1] // (zs * CORES)
    row_tiles = (r_in + r_out) // TILE
    col_tiles = width // LANES
    half = zs // 2

    def lay(base, y_order, refs, i, carry):
        index = base + i
        reverse = 0
        for b in range(bits(zs)):
            reverse = reverse | (((index >> b) & 1) << (bits(zs) - 1 - b))
        z = z_me ^ reverse
        for iy, ry in enumerate(y_order):
            y = y_me ^ ry
            for rc, ref in enumerate(refs):
                core = core_me ^ rc
                block = (z * YS + y) * CORES + core
                weight = jnp.concatenate(
                    [
                        dw_in_ref[pl.ds(pl.multiple_of(block * r_in, 8), r_in), :],
                        dw_out_ref[pl.ds(pl.multiple_of(block * r_out, 8), r_out), :],
                    ],
                    axis=0,
                ).astype(BF16)
                for rt in range(row_tiles):
                    for ct in range(col_tiles):
                        ref[iy, i, rt * col_tiles + ct] = weight[
                            rt * TILE : (rt + 1) * TILE, ct * LANES : (ct + 1) * LANES
                        ]
                first = pl.multiple_of((core * zs + z) * r_coarse, TILE)
                coarse = dense_ref[y, pl.ds(first, r_coarse), :].astype(BF16)
                for t in range(r_coarse // TILE):
                    ref[iy, i, row_tiles * col_tiles + t] = coarse[t * TILE : (t + 1) * TILE]
        return carry

    outs = [
        pltpu.make_async_copy(source, target, out_sems.at[i])
        for i, (source, target) in enumerate(
            [
                (grad_edges_ref, grad_edges_hbm),
                (send_a_ref, send_a_hbm),
                (keep_a_ref, keep_a_hbm),
                (send_b_ref, send_b_hbm),
                (keep_b_ref, keep_b_hbm),
            ]
        )
    ]
    outs[0].start()
    halves = ((keep_a_ref, send_a_ref), (keep_b_ref, send_b_ref))
    for h in range(2):
        lax.fori_loop(0, half, functools.partial(lay, h * half, Y_ORDERS[h], halves[h]), 0)
        outs[2 * h + 1].start()
        outs[2 * h + 2].start()
    for out in outs:
        out.wait()


def last_kernel(
    z_order,
    scale,
    place_ref,
    ids_ref,
    mine_ref,
    other_ref,
    own_ref,
    near_ref,
    next_ref,
    weight_ref,
    weight_other_ref,
    coarse_ref,
    fine_ref,
    grad_in_ref,
    grad_out_ref,
):
    ys, zs, tiles, tile, lanes = mine_ref.shape
    per = tiles * tile
    rows = zs * per
    slots = ids_ref.shape[1]
    z_me, y_me, core_me = position(place_ref[0])
    ids = ids_ref[pl.ds(place_ref[0], 1), :]
    row = lax.broadcasted_iota(jnp.int32, (per, slots), 0)

    last = zs * ys * CORES - 1
    base = jnp.where(place_ref[0] == 0, NC + RIM, jnp.where(place_ref[0] == last, NC, -NC))
    end_ids = base + lax.broadcasted_iota(jnp.int32, (1, RIM), 1)
    end_row = lax.broadcasted_iota(jnp.int32, (per, RIM), 0)

    def pick(core, row, ids):
        return jnp.concatenate(
            [
                jnp.where(row + (core * zs + (z_me ^ rz)) * per == ids, 1.0, 0.0)
                for rz in z_order
            ],
            axis=0,
        ).astype(BF16)

    pick_mine, pick_other = pick(core_me, row, ids), pick(1 - core_me, row, ids)
    end_mine, end_other = pick(core_me, end_row, end_ids), pick(1 - core_me, end_row, end_ids)
    ends = []
    for y in range(ys):
        turn = y_me ^ y
        at = turn ^ (turn >> 1)
        mine = mine_ref[at].reshape(rows, lanes)
        other = other_ref[at].reshape(rows, lanes)
        total = dot(pick_mine, mine, ((0,), (0,))) + dot(pick_other, other, ((0,), (0,)))
        ends.append(dot(end_mine, mine, ((0,), (0,))) + dot(end_other, other, ((0,), (0,))))
        coarse_ref[:, y * lanes : (y + 1) * lanes] = total.astype(BF16)
    nodes = own_ref.shape[0]
    even = core_me == 0
    near = near_ref[...].astype(F32)
    following = jnp.where(base > 0, jnp.concatenate(ends, axis=1), next_ref[...].astype(F32))
    from_down = jnp.where(even, following, near)
    from_up = jnp.where(even, near, following)
    fine_ref[:RIM] = (own_ref[:RIM] + from_down).astype(BF16)
    fine_ref[RIM : nodes - RIM] = own_ref[RIM : nodes - RIM].astype(BF16)
    fine_ref[nodes - RIM :] = (own_ref[nodes - RIM :] + from_up).astype(BF16)

    r_in = grad_in_ref.shape[0]
    col_tiles = grad_in_ref.shape[1] // lanes
    for t in range(weight_ref.shape[0]):
        value = (weight_ref[t].astype(F32) + weight_other_ref[t].astype(F32)) * scale
        cols = slice(t % col_tiles * lanes, (t % col_tiles + 1) * lanes)
        for part in range(0, tile, 8):
            first = t // col_tiles * tile + part
            if first < r_in:
                grad_in_ref[first : first + 8, cols] = value[part : part + 8]
            else:
                grad_out_ref[first - r_in : first - r_in + 8, cols] = value[part : part + 8]


SMEM = pl.BlockSpec(memory_space=pltpu.SMEM)
VMEM = pl.BlockSpec(memory_space=pltpu.VMEM)
HBM = pl.BlockSpec(memory_space=pltpu.HBM)


def plus(a, b):
    return (a.astype(F32) + b.astype(F32)).astype(BF16)


def swap(value, axis, mask):
    count = lax.axis_size(axis)
    return lax.ppermute(value, axis, [(i, i ^ mask) for i in range(count)])


def shards(
    zs,
    xs,
    edges,
    cotangent,
    fine_latents,
    coarse_block,
    w_in,
    w_out,
    senders,
    receivers,
    edge_count,
    coarse_ids,
):
    rows, width = edges.shape[1:]
    nodes = fine_latents.shape[1]
    slots = coarse_block.shape[1]
    depth = 2 * RIM + nodes + slots
    dom_axes = ("z", "y", "core")
    doms = zs * YS * CORES
    beside = [(i, (i + 1 - 2 * (i % 2)) % doms) for i in range(doms)]
    across = [(i, (i - 1 + 2 * (i % 2)) % doms) for i in range(doms)]
    place = lax.axis_index(dom_axes).astype(jnp.int32).reshape(1)
    even = lax.axis_index("core") == 0

    fine = fine_latents[0]
    first, last = fine[:RIM], fine[nodes - RIM :]
    following = lax.ppermute(jnp.where(even, first, last), dom_axes, across)
    near = lax.ppermute(jnp.where(even, last, first), dom_axes, beside)

    r_weight = (w_in.shape[0] + w_out.shape[0]) // doms
    w_tiles = r_weight // TILE * (width // LANES)
    c_tiles = -(-(NC + 2 * RIM) // (zs * CORES * TILE))
    tiles = w_tiles + c_tiles
    padded = c_tiles * TILE * zs * CORES
    half = zs // 2

    shape = jax.ShapeDtypeStruct
    block = (YS, half, tiles, TILE, LANES)
    grad_edges, own, near_out, next_out, keep_a, send_a, keep_b, send_b = pl.pallas_call(
        functools.partial(edge_kernel, zs),
        out_shape=(
            shape((rows, width), BF16),
            shape((nodes, width), F32),
            shape((RIM, width), BF16),
            shape((RIM, width), BF16),
        )
        + (shape(block, BF16),) * 4,
        in_specs=[SMEM, SMEM] + [HBM] * 9 + [VMEM] * 2,
        out_specs=(HBM, VMEM, VMEM, VMEM) + (HBM,) * 4,
        scratch_shapes=[
            pltpu.VMEM((rows, width), BF16),
            pltpu.VMEM((rows, width), BF16),
            pltpu.VMEM((nodes, width), BF16),
            pltpu.VMEM((slots, width), BF16),
            pltpu.VMEM(w_in.shape, BF16),
            pltpu.VMEM(w_out.shape, BF16),
            pltpu.VMEM((1, rows), jnp.int32),
            pltpu.VMEM((1, rows), jnp.int32),
            pltpu.VMEM(coarse_ids.shape, jnp.int32),
            pltpu.VMEM((rows, width), BF16),
        ]
        + [pltpu.VMEM(block, BF16)] * 4
        + [
            pltpu.VMEM(w_in.shape, F32),
            pltpu.VMEM(w_out.shape, F32),
            pltpu.VMEM((YS, padded, LANES), F32),
            pltpu.SemaphoreType.DMA((9,)),
            pltpu.SemaphoreType.DMA((5,)),
        ],
        compiler_params=pltpu.CompilerParams(vmem_limit_bytes=60 * 2**20),
        cost_estimate=pl.CostEstimate(
            flops=2_200_000_000, bytes_accessed=6_000_000, transcendentals=rows * width
        ),
        name="edge_backward",
    )(
        edge_count,
        place,
        edges[0],
        cotangent[0],
        fine,
        coarse_block[0],
        w_in,
        w_out,
        senders.reshape(1, rows),
        receivers.reshape(1, rows),
        coarse_ids,
        near,
        following,
    )

    other_a = swap(send_a, "core", 1)
    other_b = swap(send_b, "core", 1)
    two = YS // 2

    def split_plus(a, b, at):
        return plus(a[:at], b[:at]), plus(a[at:], b[at:])

    keep_a, send_a = split_plus(keep_a, other_a, two)
    keep_b, send_b = split_plus(keep_b, other_b, two)
    send_a, near_out, next_out = lax.optimization_barrier((send_a, near_out, next_out))
    other_a = swap(send_a, "y", Y_STEPS[0][0])
    other_b = swap(send_b, "y", Y_STEPS[1][0])
    inner = [(i, j) for i, j in across if abs(i - j) == 1]
    following = lax.ppermute(next_out, dom_axes, inner)
    near = lax.ppermute(near_out, dom_axes, beside)
    keep_a, send_a = split_plus(keep_a, other_a, 1)
    keep_b, send_b = split_plus(keep_b, other_b, 1)
    other_b = swap(send_b, "y", Y_STEPS[1][1])
    other_a = swap(send_a, "y", Y_STEPS[0][1])
    send = plus(keep_b[0], other_b[0])
    keep = plus(keep_a[0], other_a[0])
    masks = [1 << b for b in range(bits(zs))]
    other, near, following = lax.optimization_barrier((swap(send, "z", 1), near, following))
    keep = plus(keep, other)
    weight, coarse = keep[:, :w_tiles], keep[:, w_tiles:]
    z_order = [
        2 * sum(((i >> b) & 1) << (bits(half) - 1 - b) for b in range(bits(half)))
        for i in range(half)
    ]
    for mask in masks[1:]:
        rest = weight.shape[0] // 2
        turned = jnp.stack([coarse[z_order.index(r ^ mask)] for r in z_order])
        payload = jnp.concatenate(
            [weight[rest:].reshape(-1, TILE, LANES), turned.reshape(-1, TILE, LANES)], axis=0
        )
        other = swap(payload, "z", mask)
        weight = plus(weight[:rest], other[: rest * w_tiles].reshape(-1, w_tiles, TILE, LANES))
        coarse = plus(coarse, other[rest * w_tiles :].reshape(coarse.shape))
    weight = weight[0]

    z_order = z_order + [r ^ 1 for r in z_order]
    x_masks = [2 * (1 << b) - 1 for b in range(bits(xs))]
    coarse_other = swap(coarse, "z", 1)
    for mask in x_masks[:-1]:
        weight_other = swap(weight, "member", mask)
        weight_other, coarse_other = lax.optimization_barrier((weight_other, coarse_other))
        weight = plus(weight, weight_other)
    coarse = jnp.concatenate([coarse, coarse_other], axis=0)
    weight_other = swap(weight, "dp", 1)
    coarse = jnp.concatenate([coarse, swap(coarse, "y", 1)], axis=0)
    coarse_other = swap(coarse, "y", 3)
    weight_other, coarse_other = lax.optimization_barrier((weight_other, coarse_other))
    weight = plus(weight, weight_other)
    weight_other = swap(weight, "member", x_masks[-1])
    coarse = jnp.concatenate([coarse, coarse_other], axis=0)
    coarse = coarse.reshape(YS, zs, c_tiles, TILE, LANES)
    coarse_other = swap(coarse, "core", 1)

    all_edges = rows * doms * xs * lax.axis_size("dp")
    grad_coarse, grad_fine, grad_in, grad_out = pl.pallas_call(
        functools.partial(last_kernel, z_order, 1.0 / math.sqrt(all_edges)),
        out_shape=(
            shape((slots, width), BF16),
            shape((nodes, width), BF16),
            shape((w_in.shape[0] // doms, width), F32),
            shape((w_out.shape[0] // doms, width), F32),
        ),
        in_specs=[SMEM] + [VMEM] * 8,
        out_specs=(VMEM,) * 4,
        compiler_params=pltpu.CompilerParams(vmem_limit_bytes=16 * 2**20),
        name="last_sums",
    )(
        place,
        coarse_ids,
        coarse,
        coarse_other,
        own,
        near,
        following,
        weight,
        weight_other,
    )
    return (grad_edges[None], grad_fine[None], grad_coarse[None], grad_in, grad_out)


def solution(mesh):
    doms, xs, dps = (mesh.shape[name] for name in ("dom", "member", "dp"))
    zs = doms // (YS * CORES)
    split = Mesh(
        mesh.devices.reshape(zs, YS, CORES, xs, dps), ("z", "y", "core", "member", "dp")
    )
    dom = ("z", "y", "core")
    sample = ("member", "dp")
    latent = P(sample, dom, None)
    return jax.shard_map(
        functools.partial(shards, zs, xs),
        mesh=split,
        in_specs=(latent,) * 4 + (P(), P(), P(dom), P(dom), P(dom), P()),
        out_specs=(latent,) * 3 + (P(dom, None), P(dom, None)),
        check_vma=False,
    )
```

```python
import functools
import math

import jax
import jax.numpy as jnp
from jax import lax
from jax.experimental import pallas as pl
from jax.experimental.pallas import tpu as pltpu
from jax.sharding import Mesh
from jax.sharding import PartitionSpec as P

RIM = 16
NC = 642
YS = 4
CORES = 2
LANES = 128
TILE = 16

F32 = jnp.float32
BF16 = jnp.bfloat16

Y_ORDERS = ((0, 3, 1, 2), (0, 1, 3, 2))
Y_STEPS = ((1, 3), (3, 1))


def dot(left, right, dims):
    return lax.dot_general(left, right, (dims, ((), ())), preferred_element_type=F32)


def position(dom):
    core = lax.rem(dom, CORES)
    y = lax.rem(dom // CORES, YS)
    z = dom // (CORES * YS)
    return z, y, core


def bits(count):
    return count.bit_length() - 1


def picks(names, count):
    rows = lax.broadcasted_iota(jnp.int32, (count, names.shape[1]), 0)
    return jnp.where(rows == names, 1.0, 0.0).astype(BF16)


def edge_kernel(
    zs,
    count_ref,
    place_ref,
    edges_hbm,
    cot_hbm,
    fine_hbm,
    coarse_hbm,
    w_in_hbm,
    w_out_hbm,
    senders_hbm,
    receivers_hbm,
    ids_hbm,
    near_hbm,
    next_hbm,
    grad_edges_hbm,
    own_ref,
    near_out_ref,
    next_out_ref,
    keep_a_hbm,
    send_a_hbm,
    keep_b_hbm,
    send_b_hbm,
    edges_ref,
    cot_ref,
    fine_ref,
    coarse_ref,
    w_in_ref,
    w_out_ref,
    senders_ref,
    receivers_ref,
    ids_ref,
    near_ref,
    next_ref,
    grad_edges_ref,
    keep_a_ref,
    send_a_ref,
    keep_b_ref,
    send_b_ref,
    dw_in_ref,
    dw_out_ref,
    dense_ref,
    in_sems,
    out_sems,
):
    copies = [
        pltpu.make_async_copy(source, target, in_sems.at[i])
        for i, (source, target) in enumerate(
            [
                (senders_hbm, senders_ref),
                (receivers_hbm, receivers_ref),
                (near_hbm, near_ref),
                (next_hbm, next_ref),
                (fine_hbm, fine_ref),
                (coarse_hbm, coarse_ref),
                (edges_hbm, edges_ref),
                (w_in_hbm, w_in_ref),
                (ids_hbm, ids_ref),
                (w_out_hbm, w_out_ref),
                (cot_hbm, cot_ref),
            ]
        )
    ]
    for copy in copies:
        copy.start()
    rows, width = edges_ref.shape
    nodes = fine_ref.shape[0]
    slots = coarse_ref.shape[0]
    depth = 2 * RIM + nodes + slots
    dom = place_ref[0]
    z_me, y_me, core_me = position(dom)

    for copy in copies[:6]:
        copy.wait()
    pick_send = picks(senders_ref[...], depth)
    pick_recv = picks(receivers_ref[...], nodes)
    even = core_me == 0
    before = jnp.where(even, next_ref[...], near_ref[...])
    after = jnp.where(even, near_ref[...], next_ref[...])
    table = jnp.concatenate([before, fine_ref[...], after, coarse_ref[...]], axis=0)
    h_send = dot(pick_send, table, ((0,), (0,))).astype(BF16)
    h_recv = dot(pick_recv, fine_ref[...], ((0,), (0,))).astype(BF16)
    copies[6].wait()
    inputs = jnp.concatenate([edges_ref[...], h_send, h_recv], axis=1)
    copies[7].wait()
    pre = dot(inputs, w_in_ref[...], ((1,), (0,)))
    sig = jax.nn.sigmoid(pre)
    act = (pre * sig).astype(BF16)
    for copy in copies[8:]:
        copy.wait()
    hidden = dot(act, w_out_ref[...], ((1,), (0,)))
    centred = hidden - jnp.mean(hidden, axis=-1, keepdims=True)
    rstd = lax.rsqrt(jnp.mean(centred * centred, axis=-1, keepdims=True) + 1e-05)
    normed = centred * rstd
    live = lax.broadcasted_iota(jnp.int32, (rows, width), 0) < count_ref[0]
    dnorm = jnp.where(live, cot_ref[...].astype(F32), 0.0)
    dhidden = rstd * (
        dnorm
        - jnp.mean(dnorm, axis=-1, keepdims=True)
        - normed * jnp.mean(dnorm * normed, axis=-1, keepdims=True)
    )
    dhidden_b = dhidden.astype(BF16)
    dw_out_ref[...] = dot(act, dhidden_b, ((0,), (0,)))
    dact = dot(dhidden_b, w_out_ref[...], ((1,), (1,)))
    dpre_b = (dact * sig * (1.0 + pre * (1.0 - sig))).astype(BF16)
    dw_in_ref[...] = dot(inputs, dpre_b, ((0,), (0,)))
    dinputs = dot(dpre_b, w_in_ref[...], ((1,), (1,)))
    grad_edges_ref[...] = (dnorm + dinputs[:, :width]).astype(BF16)
    d_send = dinputs[:, width : 2 * width].astype(BF16)
    d_recv = dinputs[:, 2 * width :].astype(BF16)

    border = dot(pick_send[: 2 * RIM + nodes], d_send, ((1,), (0,)))
    down, up = border[:RIM], border[RIM + nodes :]
    near_out_ref[...] = jnp.where(even, up, down).astype(BF16)
    next_out_ref[...] = jnp.where(even, down, up).astype(BF16)
    own_ref[...] = border[RIM : RIM + nodes] + dot(pick_recv, d_recv, ((1,), (0,)))
    name = picks(ids_ref[pl.ds(dom, 1), :], dense_ref.shape[1])
    route = dot(name, pick_send[2 * RIM + nodes :], ((1,), (0,)))
    extent = (dense_ref.shape[1], 2 * RIM + nodes)
    lane = lax.broadcasted_iota(jnp.int32, extent, 1)
    down_row = jnp.where((lane < RIM) & (dom == 0), NC + lane, -1)
    end_row = jnp.where(
        (lane >= RIM + nodes) & (dom == zs * YS * CORES - 1), NC + lane - nodes, down_row
    )
    ends = jnp.where(lax.broadcasted_iota(jnp.int32, extent, 0) == end_row, 1.0, 0.0)
    route = route + dot(ends.astype(BF16), pick_send[: 2 * RIM + nodes], ((1,), (0,)))
    route = route.astype(BF16)
    dense = dot(route, d_send, ((1,), (0,)))
    for y in range(YS):
        dense_ref[y] = dense[:, y * LANES : (y + 1) * LANES]

    doms = zs * YS * CORES
    r_in = dw_in_ref.shape[0] // doms
    r_out = dw_out_ref.shape[0] // doms
    r_coarse = dense_ref.shape[1] // (zs * CORES)
    row_tiles = (r_in + r_out) // TILE
    col_tiles = width // LANES
    half = zs // 2

    def lay(base, y_order, refs, i, carry):
        index = base + i
        reverse = 0
        for b in range(bits(zs)):
            reverse = reverse | (((index >> b) & 1) << (bits(zs) - 1 - b))
        z = z_me ^ reverse
        for iy, ry in enumerate(y_order):
            y = y_me ^ ry
            for rc, ref in enumerate(refs):
                core = core_me ^ rc
                block = (z * YS + y) * CORES + core
                weight = jnp.concatenate(
                    [
                        dw_in_ref[pl.ds(pl.multiple_of(block * r_in, 8), r_in), :],
                        dw_out_ref[pl.ds(pl.multiple_of(block * r_out, 8), r_out), :],
                    ],
                    axis=0,
                ).astype(BF16)
                for rt in range(row_tiles):
                    for ct in range(col_tiles):
                        ref[iy, i, rt * col_tiles + ct] = weight[
                            rt * TILE : (rt + 1) * TILE, ct * LANES : (ct + 1) * LANES
                        ]
                first = pl.multiple_of((core * zs + z) * r_coarse, TILE)
                coarse = dense_ref[y, pl.ds(first, r_coarse), :].astype(BF16)
                for t in range(r_coarse // TILE):
                    ref[iy, i, row_tiles * col_tiles + t] = coarse[t * TILE : (t + 1) * TILE]
        return carry

    outs = [
        pltpu.make_async_copy(source, target, out_sems.at[i])
        for i, (source, target) in enumerate(
            [
                (grad_edges_ref, grad_edges_hbm),
                (send_a_ref, send_a_hbm),
                (keep_a_ref, keep_a_hbm),
                (send_b_ref, send_b_hbm),
                (keep_b_ref, keep_b_hbm),
            ]
        )
    ]
    outs[0].start()
    halves = ((keep_a_ref, send_a_ref), (keep_b_ref, send_b_ref))
    for h in range(2):
        lax.fori_loop(0, half, functools.partial(lay, h * half, Y_ORDERS[h], halves[h]), 0)
        outs[2 * h + 1].start()
        outs[2 * h + 2].start()
    for out in outs:
        out.wait()


def last_kernel(
    z_order,
    scale,
    place_ref,
    ids_ref,
    mine_ref,
    other_ref,
    own_ref,
    near_ref,
    next_ref,
    weight_ref,
    weight_other_ref,
    coarse_ref,
    fine_ref,
    grad_in_ref,
    grad_out_ref,
):
    ys, zs, tiles, tile, lanes = mine_ref.shape
    per = tiles * tile
    rows = zs * per
    slots = ids_ref.shape[1]
    z_me, y_me, core_me = position(place_ref[0])
    ids = ids_ref[pl.ds(place_ref[0], 1), :]
    row = lax.broadcasted_iota(jnp.int32, (per, slots), 0)

    last = zs * ys * CORES - 1
    base = jnp.where(place_ref[0] == 0, NC + RIM, jnp.where(place_ref[0] == last, NC, -NC))
    end_ids = base + lax.broadcasted_iota(jnp.int32, (1, RIM), 1)
    end_row = lax.broadcasted_iota(jnp.int32, (per, RIM), 0)

    def pick(core, row, ids):
        return jnp.concatenate(
            [
                jnp.where(row + (core * zs + (z_me ^ rz)) * per == ids, 1.0, 0.0)
                for rz in z_order
            ],
            axis=0,
        ).astype(BF16)

    pick_mine, pick_other = pick(core_me, row, ids), pick(1 - core_me, row, ids)
    end_mine, end_other = pick(core_me, end_row, end_ids), pick(1 - core_me, end_row, end_ids)
    ends = []
    for y in range(ys):
        turn = y_me ^ y
        at = turn ^ (turn >> 1)
        mine = mine_ref[at].reshape(rows, lanes)
        other = other_ref[at].reshape(rows, lanes)
        total = dot(pick_mine, mine, ((0,), (0,))) + dot(pick_other, other, ((0,), (0,)))
        ends.append(dot(end_mine, mine, ((0,), (0,))) + dot(end_other, other, ((0,), (0,))))
        coarse_ref[:, y * lanes : (y + 1) * lanes] = total.astype(BF16)
    nodes = own_ref.shape[0]
    even = core_me == 0
    near = near_ref[...].astype(F32)
    following = jnp.where(base > 0, jnp.concatenate(ends, axis=1), next_ref[...].astype(F32))
    from_down = jnp.where(even, following, near)
    from_up = jnp.where(even, near, following)
    fine_ref[:RIM] = (own_ref[:RIM] + from_down).astype(BF16)
    fine_ref[RIM : nodes - RIM] = own_ref[RIM : nodes - RIM].astype(BF16)
    fine_ref[nodes - RIM :] = (own_ref[nodes - RIM :] + from_up).astype(BF16)

    r_in = grad_in_ref.shape[0]
    col_tiles = grad_in_ref.shape[1] // lanes
    for t in range(weight_ref.shape[0]):
        value = (weight_ref[t].astype(F32) + weight_other_ref[t].astype(F32)) * scale
        cols = slice(t % col_tiles * lanes, (t % col_tiles + 1) * lanes)
        for part in range(0, tile, 8):
            first = t // col_tiles * tile + part
            if first < r_in:
                grad_in_ref[first : first + 8, cols] = value[part : part + 8]
            else:
                grad_out_ref[first - r_in : first - r_in + 8, cols] = value[part : part + 8]


SMEM = pl.BlockSpec(memory_space=pltpu.SMEM)
VMEM = pl.BlockSpec(memory_space=pltpu.VMEM)
HBM = pl.BlockSpec(memory_space=pltpu.HBM)


def plus(a, b):
    return (a.astype(F32) + b.astype(F32)).astype(BF16)


def swap(value, axis, mask):
    count = lax.axis_size(axis)
    return lax.ppermute(value, axis, [(i, i ^ mask) for i in range(count)])


def shards(
    zs,
    xs,
    edges,
    cotangent,
    fine_latents,
    coarse_block,
    w_in,
    w_out,
    senders,
    receivers,
    edge_count,
    coarse_ids,
):
    rows, width = edges.shape[1:]
    nodes = fine_latents.shape[1]
    slots = coarse_block.shape[1]
    depth = 2 * RIM + nodes + slots
    dom_axes = ("z", "y", "core")
    doms = zs * YS * CORES
    beside = [(i, (i + 1 - 2 * (i % 2)) % doms) for i in range(doms)]
    across = [(i, (i - 1 + 2 * (i % 2)) % doms) for i in range(doms)]
    place = lax.axis_index(dom_axes).astype(jnp.int32).reshape(1)
    even = lax.axis_index("core") == 0

    fine = fine_latents[0]
    first, last = fine[:RIM], fine[nodes - RIM :]
    following = lax.ppermute(jnp.where(even, first, last), dom_axes, across)
    near = lax.ppermute(jnp.where(even, last, first), dom_axes, beside)

    r_weight = (w_in.shape[0] + w_out.shape[0]) // doms
    w_tiles = r_weight // TILE * (width // LANES)
    c_tiles = -(-(NC + 2 * RIM) // (zs * CORES * TILE))
    tiles = w_tiles + c_tiles
    padded = c_tiles * TILE * zs * CORES
    half = zs // 2

    shape = jax.ShapeDtypeStruct
    block = (YS, half, tiles, TILE, LANES)
    grad_edges, own, near_out, next_out, keep_a, send_a, keep_b, send_b = pl.pallas_call(
        functools.partial(edge_kernel, zs),
        out_shape=(
            shape((rows, width), BF16),
            shape((nodes, width), F32),
            shape((RIM, width), BF16),
            shape((RIM, width), BF16),
        )
        + (shape(block, BF16),) * 4,
        in_specs=[SMEM, SMEM] + [HBM] * 11,
        out_specs=(HBM, VMEM, VMEM, VMEM) + (HBM,) * 4,
        scratch_shapes=[
            pltpu.VMEM((rows, width), BF16),
            pltpu.VMEM((rows, width), BF16),
            pltpu.VMEM((nodes, width), BF16),
            pltpu.VMEM((slots, width), BF16),
            pltpu.VMEM(w_in.shape, BF16),
            pltpu.VMEM(w_out.shape, BF16),
            pltpu.VMEM((1, rows), jnp.int32),
            pltpu.VMEM((1, rows), jnp.int32),
            pltpu.VMEM(coarse_ids.shape, jnp.int32),
            pltpu.VMEM((RIM, width), BF16),
            pltpu.VMEM((RIM, width), BF16),
            pltpu.VMEM((rows, width), BF16),
        ]
        + [pltpu.VMEM(block, BF16)] * 4
        + [
            pltpu.VMEM(w_in.shape, F32),
            pltpu.VMEM(w_out.shape, F32),
            pltpu.VMEM((YS, padded, LANES), F32),
            pltpu.SemaphoreType.DMA((11,)),
            pltpu.SemaphoreType.DMA((5,)),
        ],
        compiler_params=pltpu.CompilerParams(vmem_limit_bytes=60 * 2**20),
        cost_estimate=pl.CostEstimate(
            flops=2_200_000_000, bytes_accessed=6_000_000, transcendentals=rows * width
        ),
        name="edge_backward",
    )(
        edge_count,
        place,
        edges[0],
        cotangent[0],
        fine,
        coarse_block[0],
        w_in,
        w_out,
        senders.reshape(1, rows),
        receivers.reshape(1, rows),
        coarse_ids,
        near,
        following,
    )

    other_a = swap(send_a, "core", 1)
    other_b = swap(send_b, "core", 1)
    two = YS // 2

    def split_plus(a, b, at):
        return plus(a[:at], b[:at]), plus(a[at:], b[at:])

    keep_a, send_a = split_plus(keep_a, other_a, two)
    keep_b, send_b = split_plus(keep_b, other_b, two)
    send_a, near_out, next_out = lax.optimization_barrier((send_a, near_out, next_out))
    other_a = swap(send_a, "y", Y_STEPS[0][0])
    other_b = swap(send_b, "y", Y_STEPS[1][0])
    inner = [(i, j) for i, j in across if abs(i - j) == 1]
    following = lax.ppermute(next_out, dom_axes, inner)
    near = lax.ppermute(near_out, dom_axes, beside)
    other_a, other_b, near, following = lax.optimization_barrier(
        (other_a, other_b, near, following)
    )
    keep_a, send_a = split_plus(keep_a, other_a, 1)
    keep_b, send_b = split_plus(keep_b, other_b, 1)
    other_b = swap(send_b, "y", Y_STEPS[1][1])
    other_a = swap(send_a, "y", Y_STEPS[0][1])
    send = plus(keep_b[0], other_b[0])
    keep = plus(keep_a[0], other_a[0])
    masks = [1 << b for b in range(bits(zs))]
    keep = plus(keep, swap(send, "z", 1))
    weight, coarse = keep[:, :w_tiles], keep[:, w_tiles:]
    z_order = [
        2 * sum(((i >> b) & 1) << (bits(half) - 1 - b) for b in range(bits(half)))
        for i in range(half)
    ]
    for mask in masks[1:]:
        rest = weight.shape[0] // 2
        turned = jnp.stack([coarse[z_order.index(r ^ mask)] for r in z_order])
        payload = jnp.concatenate(
            [weight[rest:].reshape(-1, TILE, LANES), turned.reshape(-1, TILE, LANES)], axis=0
        )
        other = swap(payload, "z", mask)
        weight = plus(weight[:rest], other[: rest * w_tiles].reshape(-1, w_tiles, TILE, LANES))
        coarse = plus(coarse, other[rest * w_tiles :].reshape(coarse.shape))
    weight = weight[0]

    z_order = z_order + [r ^ 1 for r in z_order]
    x_masks = [2 * (1 << b) - 1 for b in range(bits(xs))]
    weight_steps = [("dp", 1)] + [("member", mask) for mask in x_masks]
    coarse_steps = [("z", 1), ("y", 1), ("y", 3)]
    for i, (axis, mask) in enumerate(coarse_steps):
        coarse_other = swap(coarse, axis, mask)
        if i < len(weight_steps):
            weight_other = swap(weight, *weight_steps[i])
            weight_other, coarse_other = lax.optimization_barrier((weight_other, coarse_other))
            if i < len(weight_steps) - 1:
                weight = plus(weight, weight_other)
        coarse = jnp.concatenate([coarse, coarse_other], axis=0)
    coarse = coarse.reshape(YS, zs, c_tiles, TILE, LANES)
    coarse_other = swap(coarse, "core", 1)

    all_edges = rows * doms * xs * lax.axis_size("dp")
    grad_coarse, grad_fine, grad_in, grad_out = pl.pallas_call(
        functools.partial(last_kernel, z_order, 1.0 / math.sqrt(all_edges)),
        out_shape=(
            shape((slots, width), BF16),
            shape((nodes, width), BF16),
            shape((w_in.shape[0] // doms, width), F32),
            shape((w_out.shape[0] // doms, width), F32),
        ),
        in_specs=[SMEM] + [VMEM] * 8,
        out_specs=(VMEM,) * 4,
        compiler_params=pltpu.CompilerParams(vmem_limit_bytes=16 * 2**20),
        name="last_sums",
    )(
        place,
        coarse_ids,
        coarse,
        coarse_other,
        own,
        near,
        following,
        weight,
        weight_other,
    )
    return (grad_edges[None], grad_fine[None], grad_coarse[None], grad_in, grad_out)


def solution(mesh):
    doms, xs, dps = (mesh.shape[name] for name in ("dom", "member", "dp"))
    zs = doms // (YS * CORES)
    split = Mesh(
        mesh.devices.reshape(zs, YS, CORES, xs, dps), ("z", "y", "core", "member", "dp")
    )
    dom = ("z", "y", "core")
    sample = ("member", "dp")
    latent = P(sample, dom, None)
    return jax.shard_map(
        functools.partial(shards, zs, xs),
        mesh=split,
        in_specs=(latent,) * 4 + (P(), P(), P(dom), P(dom), P(dom), P()),
        out_specs=(latent,) * 3 + (P(dom, None), P(dom, None)),
        check_vma=False,
    )
```

```python
import functools
import math

import jax
import jax.numpy as jnp
from jax import lax
from jax.experimental import pallas as pl
from jax.experimental.pallas import tpu as pltpu
from jax.sharding import Mesh
from jax.sharding import PartitionSpec as P

RIM = 16
NC = 642
YS = 4
CORES = 2
LANES = 128
TILE = 16

F32 = jnp.float32
BF16 = jnp.bfloat16

Y_ORDERS = ((0, 3, 1, 2), (0, 1, 3, 2))
Y_STEPS = ((1, 3), (3, 1))


def dot(left, right, dims):
    return lax.dot_general(left, right, (dims, ((), ())), preferred_element_type=F32)


def position(dom):
    core = lax.rem(dom, CORES)
    y = lax.rem(dom // CORES, YS)
    z = dom // (CORES * YS)
    return z, y, core


def bits(count):
    return count.bit_length() - 1


def picks(names, count):
    rows = lax.broadcasted_iota(jnp.int32, (count, names.shape[1]), 0)
    return jnp.where(rows == names, 1.0, 0.0).astype(BF16)


def load_kernel(
    zs,
    count_ref,
    place_ref,
    edges_ref,
    cot_ref,
    table_ref,
    w_in_ref,
    names_ref,
    inputs_ref,
    live_cot_ref,
    pre_ref,
    pick_send_ref,
    pick_recv_ref,
    route_ref,
):
    rows, width = edges_ref.shape
    nodes = pick_recv_ref.shape[0]
    depth = pick_send_ref.shape[0]
    dom = place_ref[0]

    pick_send = picks(names_ref[:, :rows], depth)
    pick_recv = picks(names_ref[:, rows : 2 * rows], nodes)
    pick_send_ref[...] = pick_send
    pick_recv_ref[...] = pick_recv
    fine, coarse = table_ref[:nodes], table_ref[nodes:]
    h_send = dot(pick_send[RIM : RIM + nodes], fine, ((0,), (0,))) + dot(
        pick_send[2 * RIM + nodes :], coarse, ((0,), (0,))
    )
    h_recv = dot(pick_recv, fine, ((0,), (0,)))
    inputs_ref[:, :width] = edges_ref[...]
    inputs_ref[:, width : 2 * width] = h_send.astype(BF16)
    inputs_ref[:, 2 * width :] = h_recv.astype(BF16)
    pre_ref[...] = dot(inputs_ref[...], w_in_ref[...], ((1,), (0,)))
    live = lax.broadcasted_iota(jnp.int32, (rows, width), 0) < count_ref[0]
    live_cot_ref[...] = jnp.where(live, cot_ref[...].astype(F32), 0.0).astype(BF16)

    padded = route_ref.shape[0]
    ids = names_ref[:, 2 * rows : 2 * rows + depth - 2 * RIM - nodes]
    route = dot(picks(ids, padded), pick_send[2 * RIM + nodes :], ((1,), (0,)))
    extent = (padded, 2 * RIM + nodes)
    lane = lax.broadcasted_iota(jnp.int32, extent, 1)
    down_row = jnp.where((lane < RIM) & (dom == 0), NC + lane, -1)
    end_row = jnp.where(
        (lane >= RIM + nodes) & (dom == zs * YS * CORES - 1), NC + lane - nodes, down_row
    )
    ends = jnp.where(lax.broadcasted_iota(jnp.int32, extent, 0) == end_row, 1.0, 0.0)
    route = route + dot(ends.astype(BF16), pick_send[: 2 * RIM + nodes], ((1,), (0,)))
    route_ref[...] = route.astype(BF16)


def edge_kernel(
    zs,
    place_ref,
    inputs_ref,
    cot_ref,
    pre_ref,
    pick_send_ref,
    pick_recv_ref,
    route_ref,
    w_in_ref,
    w_out_ref,
    near_ref,
    next_ref,
    grad_edges_ref,
    own_ref,
    near_out_ref,
    next_out_ref,
    keep_a_ref,
    send_a_ref,
    keep_b_ref,
    send_b_ref,
    dw_in_ref,
    dw_out_ref,
    dense_ref,
):
    rows, width = cot_ref.shape
    nodes = pick_recv_ref.shape[0]
    z_me, y_me, core_me = position(place_ref[0])
    even = core_me == 0

    pick_send = pick_send_ref[...]
    pick_recv = pick_recv_ref[...]
    before = jnp.where(even, next_ref[...], near_ref[...])
    after = jnp.where(even, near_ref[...], next_ref[...])
    h_halo = (
        dot(pick_send[:RIM], before, ((0,), (0,)))
        + dot(pick_send[RIM + nodes : 2 * RIM + nodes], after, ((0,), (0,)))
    ).astype(BF16)
    h_send = (inputs_ref[:, width : 2 * width] + h_halo).astype(BF16)
    inputs = jnp.concatenate(
        [inputs_ref[:, :width], h_send, inputs_ref[:, 2 * width :]], axis=1
    )
    pre = pre_ref[...] + dot(h_halo, w_in_ref[width : 2 * width, :], ((1,), (0,)))
    sig = jax.nn.sigmoid(pre)
    act = (pre * sig).astype(BF16)
    hidden = dot(act, w_out_ref[...], ((1,), (0,)))
    centred = hidden - jnp.mean(hidden, axis=-1, keepdims=True)
    rstd = lax.rsqrt(jnp.mean(centred * centred, axis=-1, keepdims=True) + 1e-05)
    normed = centred * rstd
    dnorm = cot_ref[...].astype(F32)
    dhidden = rstd * (
        dnorm
        - jnp.mean(dnorm, axis=-1, keepdims=True)
        - normed * jnp.mean(dnorm * normed, axis=-1, keepdims=True)
    )
    dhidden_b = dhidden.astype(BF16)
    dw_out_ref[...] = dot(act, dhidden_b, ((0,), (0,)))
    dact = dot(dhidden_b, w_out_ref[...], ((1,), (1,)))
    dpre_b = (dact * sig * (1.0 + pre * (1.0 - sig))).astype(BF16)
    dw_in_ref[...] = dot(inputs, dpre_b, ((0,), (0,)))
    dinputs = dot(dpre_b, w_in_ref[...], ((1,), (1,)))
    grad_edges_ref[...] = (dnorm + dinputs[:, :width]).astype(BF16)
    d_send = dinputs[:, width : 2 * width].astype(BF16)
    d_recv = dinputs[:, 2 * width :].astype(BF16)

    border = dot(pick_send[: 2 * RIM + nodes], d_send, ((1,), (0,)))
    down, up = border[:RIM], border[RIM + nodes :]
    near_out_ref[...] = jnp.where(even, up, down).astype(BF16)
    next_out_ref[...] = jnp.where(even, down, up).astype(BF16)
    own_ref[...] = border[RIM : RIM + nodes] + dot(pick_recv, d_recv, ((1,), (0,)))
    dense = dot(route_ref[...], d_send, ((1,), (0,)))
    for y in range(YS):
        dense_ref[y] = dense[:, y * LANES : (y + 1) * LANES]

    doms = zs * YS * CORES
    r_in = dw_in_ref.shape[0] // doms
    r_out = dw_out_ref.shape[0] // doms
    r_coarse = dense_ref.shape[1] // (zs * CORES)
    row_tiles = (r_in + r_out) // TILE
    col_tiles = width // LANES
    half = zs // 2

    def lay(base, y_order, refs, i, carry):
        index = base + i
        reverse = 0
        for b in range(bits(zs)):
            reverse = reverse | (((index >> b) & 1) << (bits(zs) - 1 - b))
        z = z_me ^ reverse
        for iy, ry in enumerate(y_order):
            y = y_me ^ ry
            for rc, ref in enumerate(refs):
                core = core_me ^ rc
                block = (z * YS + y) * CORES + core
                weight = jnp.concatenate(
                    [
                        dw_in_ref[pl.ds(pl.multiple_of(block * r_in, 8), r_in), :],
                        dw_out_ref[pl.ds(pl.multiple_of(block * r_out, 8), r_out), :],
                    ],
                    axis=0,
                ).astype(BF16)
                for rt in range(row_tiles):
                    for ct in range(col_tiles):
                        ref[iy, i, rt * col_tiles + ct] = weight[
                            rt * TILE : (rt + 1) * TILE, ct * LANES : (ct + 1) * LANES
                        ]
                first = pl.multiple_of((core * zs + z) * r_coarse, TILE)
                coarse = dense_ref[y, pl.ds(first, r_coarse), :].astype(BF16)
                for t in range(r_coarse // TILE):
                    ref[iy, i, row_tiles * col_tiles + t] = coarse[t * TILE : (t + 1) * TILE]
        return carry

    halves = ((keep_a_ref, send_a_ref), (keep_b_ref, send_b_ref))
    for h in range(2):
        lax.fori_loop(0, half, functools.partial(lay, h * half, Y_ORDERS[h], halves[h]), 0)


def last_kernel(
    z_order,
    scale,
    first_id,
    place_ref,
    side_ref,
    names_ref,
    mine_ref,
    other_ref,
    own_ref,
    near_ref,
    next_ref,
    weight_ref,
    weight_other_ref,
    coarse_ref,
    fine_ref,
    grad_in_ref,
    grad_out_ref,
):
    ys, zs, tiles, tile, lanes = mine_ref.shape
    per = tiles * tile
    rows = zs * per
    slots = coarse_ref.shape[0]
    z_me, y_me, core_me = position(place_ref[0])
    ids = names_ref[:, first_id : first_id + slots]
    row = lax.broadcasted_iota(jnp.int32, (per, slots), 0)

    last = zs * ys * CORES - 1
    base = jnp.where(place_ref[0] == 0, NC + RIM, jnp.where(place_ref[0] == last, NC, -NC))
    end_ids = base + lax.broadcasted_iota(jnp.int32, (1, RIM), 1)
    end_row = lax.broadcasted_iota(jnp.int32, (per, RIM), 0)

    def pick(core, row, ids):
        return jnp.concatenate(
            [
                jnp.where(row + (core * zs + (z_me ^ rz)) * per == ids, 1.0, 0.0)
                for rz in z_order
            ],
            axis=0,
        ).astype(BF16)

    pick_mine, pick_other = pick(core_me, row, ids), pick(1 - core_me, row, ids)
    end_mine, end_other = pick(core_me, end_row, end_ids), pick(1 - core_me, end_row, end_ids)
    ends = []
    for y in range(ys):
        turn = y_me ^ y
        at = turn ^ (turn >> 1)
        mine = mine_ref[at].reshape(rows, lanes)
        other = other_ref[at].reshape(rows, lanes)
        total = dot(pick_mine, mine, ((0,), (0,))) + dot(pick_other, other, ((0,), (0,)))
        ends.append(dot(end_mine, mine, ((0,), (0,))) + dot(end_other, other, ((0,), (0,))))
        coarse_ref[:, y * lanes : (y + 1) * lanes] = total.astype(BF16)
    nodes = own_ref.shape[0]
    even = core_me == 0
    near = near_ref[...].astype(F32)
    following = jnp.where(base > 0, jnp.concatenate(ends, axis=1), next_ref[...].astype(F32))
    from_down = jnp.where(even, following, near)
    from_up = jnp.where(even, near, following)
    fine_ref[:RIM] = (own_ref[:RIM] + from_down).astype(BF16)
    fine_ref[RIM : nodes - RIM] = own_ref[RIM : nodes - RIM].astype(BF16)
    fine_ref[nodes - RIM :] = (own_ref[nodes - RIM :] + from_up).astype(BF16)

    r_in = grad_in_ref.shape[0]
    col_tiles = grad_in_ref.shape[1] // lanes
    half = weight_ref.shape[0]
    low = side_ref[0] == 0
    for t in range(2 * half):
        mine, other = weight_ref[t % half], weight_other_ref[t % half]
        upper = t >= half
        value = jnp.where(low != upper, mine.astype(F32), other.astype(F32)) * scale
        cols = slice(t % col_tiles * lanes, (t % col_tiles + 1) * lanes)
        for part in range(0, tile, 8):
            first = t // col_tiles * tile + part
            if first < r_in:
                grad_in_ref[first : first + 8, cols] = value[part : part + 8]
            else:
                grad_out_ref[first - r_in : first - r_in + 8, cols] = value[part : part + 8]


SMEM = pl.BlockSpec(memory_space=pltpu.SMEM)
VMEM = pl.BlockSpec(memory_space=pltpu.VMEM)


def plus(a, b):
    return (a.astype(F32) + b.astype(F32)).astype(BF16)


def swap(value, axis, mask):
    count = lax.axis_size(axis)
    return lax.ppermute(value, axis, [(i, i ^ mask) for i in range(count)])


def shards(
    zs,
    xs,
    edges,
    cotangent,
    fine_latents,
    coarse_block,
    w_in,
    w_out,
    senders,
    receivers,
    edge_count,
    coarse_ids,
):
    rows, width = edges.shape[1:]
    nodes = fine_latents.shape[1]
    slots = coarse_block.shape[1]
    depth = 2 * RIM + nodes + slots
    dom_axes = ("z", "y", "core")
    doms = zs * YS * CORES
    beside = [(i, (i + 1 - 2 * (i % 2)) % doms) for i in range(doms)]
    across = [(i, (i - 1 + 2 * (i % 2)) % doms) for i in range(doms)]
    place = lax.axis_index(dom_axes).astype(jnp.int32).reshape(1)
    even = lax.axis_index("core") == 0

    fine = fine_latents[0]
    first, last = fine[:RIM], fine[nodes - RIM :]
    following = lax.ppermute(jnp.where(even, first, last), dom_axes, across)
    near = lax.ppermute(jnp.where(even, last, first), dom_axes, beside)

    r_weight = (w_in.shape[0] + w_out.shape[0]) // doms
    w_tiles = r_weight // TILE * (width // LANES)
    c_tiles = -(-(NC + 2 * RIM) // (zs * CORES * TILE))
    tiles = w_tiles + c_tiles
    padded = c_tiles * TILE * zs * CORES
    half = zs // 2

    shape = jax.ShapeDtypeStruct
    own_ids = lax.dynamic_slice_in_dim(coarse_ids, place[0], 1, 0)
    names = jnp.concatenate([senders[None], receivers[None], own_ids], axis=1)
    table = jnp.concatenate([fine, coarse_block[0]], axis=0)
    loaded = pl.pallas_call(
        functools.partial(load_kernel, zs),
        out_shape=(
            shape((rows, 3 * width), BF16),
            shape((rows, width), BF16),
            shape((rows, width), F32),
            shape((2 * RIM + nodes + slots, rows), BF16),
            shape((nodes, rows), BF16),
            shape((padded, rows), BF16),
        ),
        in_specs=[SMEM, SMEM] + [VMEM] * 5,
        out_specs=(VMEM,) * 6,
        compiler_params=pltpu.CompilerParams(vmem_limit_bytes=24 * 2**20),
        cost_estimate=pl.CostEstimate(
            flops=600_000_000, bytes_accessed=6_000_000, transcendentals=0
        ),
        name="edge_inputs",
    )(edge_count, place, edges[0], cotangent[0], table, w_in, names)

    block = shape((YS, half, tiles, TILE, LANES), BF16)
    grad_edges, own, near_out, next_out, keep_a, send_a, keep_b, send_b = pl.pallas_call(
        functools.partial(edge_kernel, zs),
        out_shape=(
            shape((rows, width), BF16),
            shape((nodes, width), F32),
            shape((RIM, width), BF16),
            shape((RIM, width), BF16),
            block,
            block,
            block,
            block,
        ),
        in_specs=[SMEM] + [VMEM] * 10,
        out_specs=(VMEM,) * 8,
        scratch_shapes=[
            pltpu.VMEM(w_in.shape, F32),
            pltpu.VMEM(w_out.shape, F32),
            pltpu.VMEM((YS, padded, LANES), F32),
        ],
        compiler_params=pltpu.CompilerParams(vmem_limit_bytes=36 * 2**20),
        cost_estimate=pl.CostEstimate(
            flops=1_800_000_000, bytes_accessed=6_000_000, transcendentals=rows * width
        ),
        name="edge_backward",
    )(place, *loaded, w_in, w_out, near, following)

    other_a = swap(send_a, "core", 1)
    other_b = swap(send_b, "core", 1)
    two = YS // 2

    def split_plus(a, b, at):
        return plus(a[:at], b[:at]), plus(a[at:], b[at:])

    keep_a, send_a = split_plus(keep_a, other_a, two)
    keep_b, send_b = split_plus(keep_b, other_b, two)
    send_a, near_out, next_out = lax.optimization_barrier((send_a, near_out, next_out))
    other_a = swap(send_a, "y", Y_STEPS[0][0])
    other_b = swap(send_b, "y", Y_STEPS[1][0])
    inner = [(i, j) for i, j in across if abs(i - j) == 1]
    following = lax.ppermute(next_out, dom_axes, inner)
    near = lax.ppermute(near_out, dom_axes, beside)
    other_a, other_b, near, following = lax.optimization_barrier(
        (other_a, other_b, near, following)
    )
    keep_a, send_a = split_plus(keep_a, other_a, 1)
    keep_b, send_b = split_plus(keep_b, other_b, 1)
    other_b = swap(send_b, "y", Y_STEPS[1][1])
    other_a = swap(send_a, "y", Y_STEPS[0][1])
    send = plus(keep_b[0], other_b[0])
    keep = plus(keep_a[0], other_a[0])
    masks = [1 << b for b in range(bits(zs))]
    keep = plus(keep, swap(send, "z", 1))
    weight, coarse = keep[:, :w_tiles], keep[:, w_tiles:]
    z_order = [
        2 * sum(((i >> b) & 1) << (bits(half) - 1 - b) for b in range(bits(half)))
        for i in range(half)
    ]
    for mask in masks[1:]:
        rest = weight.shape[0] // 2
        turned = jnp.stack([coarse[z_order.index(r ^ mask)] for r in z_order])
        payload = jnp.concatenate(
            [weight[rest:].reshape(-1, TILE, LANES), turned.reshape(-1, TILE, LANES)], axis=0
        )
        other = swap(payload, "z", mask)
        weight = plus(weight[:rest], other[: rest * w_tiles].reshape(-1, w_tiles, TILE, LANES))
        coarse = plus(coarse, other[rest * w_tiles :].reshape(coarse.shape))
    weight = weight[0]

    z_order = z_order + [r ^ 1 for r in z_order]
    x = lax.axis_index("member")
    side = ((x ^ (x >> 1)) & 1).astype(jnp.int32).reshape(1)
    low = side[0] == 0
    first, second = weight[: w_tiles // 2], weight[w_tiles // 2 :]
    weight = jnp.where(low, first, second)
    weight_steps = [("dp", 1)] + [("member", 2 * (1 << b) - 1) for b in range(1, bits(xs))]
    coarse_steps = [("z", 1), ("y", 1), ("y", 3)]
    for i, (axis, mask) in enumerate(coarse_steps):
        coarse_other = swap(coarse, axis, mask)
        if i == 0:
            weight_other = swap(jnp.where(low, second, first), "member", 1)
        elif i <= len(weight_steps):
            weight_other = swap(weight, *weight_steps[i - 1])
        if i <= len(weight_steps):
            weight_other, coarse_other = lax.optimization_barrier((weight_other, coarse_other))
            weight = plus(weight, weight_other)
        coarse = jnp.concatenate([coarse, coarse_other], axis=0)
    weight_other = swap(weight, "member", 1)
    coarse = coarse.reshape(YS, zs, c_tiles, TILE, LANES)
    coarse_other = swap(coarse, "core", 1)

    all_edges = rows * doms * xs * lax.axis_size("dp")
    grad_coarse, grad_fine, grad_in, grad_out = pl.pallas_call(
        functools.partial(last_kernel, z_order, 1.0 / math.sqrt(all_edges), 2 * rows),
        out_shape=(
            shape((slots, width), BF16),
            shape((nodes, width), BF16),
            shape((w_in.shape[0] // doms, width), F32),
            shape((w_out.shape[0] // doms, width), F32),
        ),
        in_specs=[SMEM, SMEM] + [VMEM] * 8,
        out_specs=(VMEM,) * 4,
        compiler_params=pltpu.CompilerParams(vmem_limit_bytes=16 * 2**20),
        name="last_sums",
    )(
        place,
        side,
        names,
        coarse,
        coarse_other,
        own,
        near,
        following,
        weight,
        weight_other,
    )
    return (grad_edges[None], grad_fine[None], grad_coarse[None], grad_in, grad_out)


def solution(mesh):
    doms, xs, dps = (mesh.shape[name] for name in ("dom", "member", "dp"))
    zs = doms // (YS * CORES)
    split = Mesh(
        mesh.devices.reshape(zs, YS, CORES, xs, dps), ("z", "y", "core", "member", "dp")
    )
    dom = ("z", "y", "core")
    sample = ("member", "dp")
    latent = P(sample, dom, None)
    return jax.shard_map(
        functools.partial(shards, zs, xs),
        mesh=split,
        in_specs=(latent,) * 4 + (P(), P(), P(dom), P(dom), P(dom), P()),
        out_specs=(latent,) * 3 + (P(dom, None), P(dom, None)),
        check_vma=False,
    )
```

```python
import functools
import math

import jax
import jax.numpy as jnp
from jax import lax
from jax.experimental import pallas as pl
from jax.experimental.pallas import tpu as pltpu
from jax.sharding import Mesh
from jax.sharding import PartitionSpec as P

RIM = 16
NC = 642
YS = 4
CORES = 2
LANES = 128
TILE = 16

F32 = jnp.float32
BF16 = jnp.bfloat16

Y_ORDERS = ((0, 3, 1, 2), (0, 1, 3, 2))
Y_STEPS = ((1, 3), (3, 1))


def dot(left, right, dims):
    return lax.dot_general(left, right, (dims, ((), ())), preferred_element_type=F32)


def position(dom):
    core = lax.rem(dom, CORES)
    y = lax.rem(dom // CORES, YS)
    z = dom // (CORES * YS)
    return z, y, core


def bits(count):
    return count.bit_length() - 1


def picks(names, count):
    rows = lax.broadcasted_iota(jnp.int32, (count, names.shape[1]), 0)
    return jnp.where(rows == names, 1.0, 0.0).astype(BF16)


def load_kernel(
    zs,
    count_ref,
    place_ref,
    edges_ref,
    cot_ref,
    table_ref,
    w_in_ref,
    names_ref,
    inputs_ref,
    live_cot_ref,
    pre_ref,
    pick_send_ref,
    pick_recv_ref,
    route_ref,
):
    rows, width = edges_ref.shape
    nodes = pick_recv_ref.shape[0]
    depth = pick_send_ref.shape[0]
    dom = place_ref[0]

    pick_send = picks(names_ref[:, :rows], depth)
    pick_recv = picks(names_ref[:, rows : 2 * rows], nodes)
    pick_send_ref[...] = pick_send
    pick_recv_ref[...] = pick_recv
    fine, coarse = table_ref[:nodes], table_ref[nodes:]
    h_send = dot(pick_send[RIM : RIM + nodes], fine, ((0,), (0,))) + dot(
        pick_send[2 * RIM + nodes :], coarse, ((0,), (0,))
    )
    h_recv = dot(pick_recv, fine, ((0,), (0,)))
    inputs_ref[:, :width] = edges_ref[...]
    inputs_ref[:, width : 2 * width] = h_send.astype(BF16)
    inputs_ref[:, 2 * width :] = h_recv.astype(BF16)
    pre_ref[...] = dot(inputs_ref[...], w_in_ref[...], ((1,), (0,)))
    live = lax.broadcasted_iota(jnp.int32, (rows, width), 0) < count_ref[0]
    live_cot_ref[...] = jnp.where(live, cot_ref[...].astype(F32), 0.0).astype(BF16)

    padded = route_ref.shape[0]
    ids = names_ref[:, 2 * rows : 2 * rows + depth - 2 * RIM - nodes]
    route = dot(picks(ids, padded), pick_send[2 * RIM + nodes :], ((1,), (0,)))
    extent = (padded, 2 * RIM + nodes)
    lane = lax.broadcasted_iota(jnp.int32, extent, 1)
    down_row = jnp.where((lane < RIM) & (dom == 0), NC + lane, -1)
    end_row = jnp.where(
        (lane >= RIM + nodes) & (dom == zs * YS * CORES - 1), NC + lane - nodes, down_row
    )
    ends = jnp.where(lax.broadcasted_iota(jnp.int32, extent, 0) == end_row, 1.0, 0.0)
    route = route + dot(ends.astype(BF16), pick_send[: 2 * RIM + nodes], ((1,), (0,)))
    route_ref[...] = route.astype(BF16)


def edge_kernel(
    zs,
    place_ref,
    inputs_ref,
    cot_ref,
    pre_ref,
    pick_send_ref,
    pick_recv_ref,
    route_ref,
    w_in_ref,
    w_out_ref,
    near_ref,
    next_ref,
    grad_edges_ref,
    own_ref,
    near_out_ref,
    next_out_ref,
    keep_a_ref,
    send_a_ref,
    keep_b_ref,
    send_b_ref,
    dw_in_ref,
    dw_out_ref,
    dense_ref,
):
    rows, width = cot_ref.shape
    nodes = pick_recv_ref.shape[0]
    z_me, y_me, core_me = position(place_ref[0])
    even = core_me == 0

    pick_send = pick_send_ref[...]
    pick_recv = pick_recv_ref[...]
    before = jnp.where(even, next_ref[...], near_ref[...])
    after = jnp.where(even, near_ref[...], next_ref[...])
    h_halo = (
        dot(pick_send[:RIM], before, ((0,), (0,)))
        + dot(pick_send[RIM + nodes : 2 * RIM + nodes], after, ((0,), (0,)))
    ).astype(BF16)
    h_send = (inputs_ref[:, width : 2 * width] + h_halo).astype(BF16)
    inputs = jnp.concatenate(
        [inputs_ref[:, :width], h_send, inputs_ref[:, 2 * width :]], axis=1
    )
    pre = pre_ref[...] + dot(h_halo, w_in_ref[width : 2 * width, :], ((1,), (0,)))
    sig = jax.nn.sigmoid(pre)
    act = (pre * sig).astype(BF16)
    hidden = dot(act, w_out_ref[...], ((1,), (0,)))
    centred = hidden - jnp.mean(hidden, axis=-1, keepdims=True)
    rstd = lax.rsqrt(jnp.mean(centred * centred, axis=-1, keepdims=True) + 1e-05)
    normed = centred * rstd
    dnorm = cot_ref[...].astype(F32)
    dhidden = rstd * (
        dnorm
        - jnp.mean(dnorm, axis=-1, keepdims=True)
        - normed * jnp.mean(dnorm * normed, axis=-1, keepdims=True)
    )
    dhidden_b = dhidden.astype(BF16)
    dw_out_ref[...] = dot(act, dhidden_b, ((0,), (0,)))
    dact = dot(dhidden_b, w_out_ref[...], ((1,), (1,)))
    dpre_b = (dact * sig * (1.0 + pre * (1.0 - sig))).astype(BF16)
    dw_in_ref[...] = dot(inputs, dpre_b, ((0,), (0,)))
    dinputs = dot(dpre_b, w_in_ref[...], ((1,), (1,)))
    grad_edges_ref[...] = (dnorm + dinputs[:, :width]).astype(BF16)
    d_send = dinputs[:, width : 2 * width].astype(BF16)
    d_recv = dinputs[:, 2 * width :].astype(BF16)

    border = dot(pick_send[: 2 * RIM + nodes], d_send, ((1,), (0,)))
    down, up = border[:RIM], border[RIM + nodes :]
    near_out_ref[...] = jnp.where(even, up, down).astype(BF16)
    next_out_ref[...] = jnp.where(even, down, up).astype(BF16)
    own_ref[...] = border[RIM : RIM + nodes] + dot(pick_recv, d_recv, ((1,), (0,)))
    dense = dot(route_ref[...], d_send, ((1,), (0,)))
    for y in range(YS):
        dense_ref[y] = dense[:, y * LANES : (y + 1) * LANES]

    doms = zs * YS * CORES
    r_in = dw_in_ref.shape[0] // doms
    r_out = dw_out_ref.shape[0] // doms
    r_coarse = dense_ref.shape[1] // (zs * CORES)
    row_tiles = (r_in + r_out) // TILE
    col_tiles = width // LANES
    half = zs // 2

    def lay(base, y_order, refs, i, carry):
        index = base + i
        reverse = 0
        for b in range(bits(zs)):
            reverse = reverse | (((index >> b) & 1) << (bits(zs) - 1 - b))
        z = z_me ^ reverse
        for iy, ry in enumerate(y_order):
            y = y_me ^ ry
            for rc, ref in enumerate(refs):
                core = core_me ^ rc
                block = (z * YS + y) * CORES + core
                weight = jnp.concatenate(
                    [
                        dw_in_ref[pl.ds(pl.multiple_of(block * r_in, 8), r_in), :],
                        dw_out_ref[pl.ds(pl.multiple_of(block * r_out, 8), r_out), :],
                    ],
                    axis=0,
                ).astype(BF16)
                for rt in range(row_tiles):
                    for ct in range(col_tiles):
                        ref[iy, i, rt * col_tiles + ct] = weight[
                            rt * TILE : (rt + 1) * TILE, ct * LANES : (ct + 1) * LANES
                        ]
                first = pl.multiple_of((core * zs + z) * r_coarse, TILE)
                coarse = dense_ref[y, pl.ds(first, r_coarse), :].astype(BF16)
                for t in range(r_coarse // TILE):
                    ref[iy, i, row_tiles * col_tiles + t] = coarse[t * TILE : (t + 1) * TILE]
        return carry

    halves = ((keep_a_ref, send_a_ref), (keep_b_ref, send_b_ref))
    for h in range(2):
        lax.fori_loop(0, half, functools.partial(lay, h * half, Y_ORDERS[h], halves[h]), 0)


def last_kernel(
    z_order,
    scale,
    first_id,
    place_ref,
    names_ref,
    mine_ref,
    other_ref,
    own_ref,
    near_ref,
    next_ref,
    weight_ref,
    weight_other_ref,
    coarse_ref,
    fine_ref,
    grad_in_ref,
    grad_out_ref,
):
    ys, zs, tiles, tile, lanes = mine_ref.shape
    per = tiles * tile
    rows = zs * per
    slots = coarse_ref.shape[0]
    z_me, _, core_me = position(place_ref[0])
    ids = names_ref[:, first_id : first_id + slots]
    row = lax.broadcasted_iota(jnp.int32, (per, slots), 0)

    last = zs * ys * CORES - 1
    base = jnp.where(place_ref[0] == 0, NC + RIM, jnp.where(place_ref[0] == last, NC, -NC))
    end_ids = base + lax.broadcasted_iota(jnp.int32, (1, RIM), 1)
    end_row = lax.broadcasted_iota(jnp.int32, (per, RIM), 0)

    def pick(core, row, ids):
        return jnp.concatenate(
            [
                jnp.where(row + (core * zs + (z_me ^ rz)) * per == ids, 1.0, 0.0)
                for rz in z_order
            ],
            axis=0,
        ).astype(BF16)

    pick_mine, pick_other = pick(core_me, row, ids), pick(1 - core_me, row, ids)
    end_mine, end_other = pick(core_me, end_row, end_ids), pick(1 - core_me, end_row, end_ids)
    ends = []
    for y in range(ys):
        mine = mine_ref[y].reshape(rows, lanes)
        other = other_ref[y].reshape(rows, lanes)
        total = dot(pick_mine, mine, ((0,), (0,))) + dot(pick_other, other, ((0,), (0,)))
        ends.append(dot(end_mine, mine, ((0,), (0,))) + dot(end_other, other, ((0,), (0,))))
        coarse_ref[:, y * lanes : (y + 1) * lanes] = total.astype(BF16)
    nodes = own_ref.shape[0]
    even = core_me == 0
    near = near_ref[...].astype(F32)
    following = jnp.where(base > 0, jnp.concatenate(ends, axis=1), next_ref[...].astype(F32))
    from_down = jnp.where(even, following, near)
    from_up = jnp.where(even, near, following)
    fine_ref[:RIM] = (own_ref[:RIM] + from_down).astype(BF16)
    fine_ref[RIM : nodes - RIM] = own_ref[RIM : nodes - RIM].astype(BF16)
    fine_ref[nodes - RIM :] = (own_ref[nodes - RIM :] + from_up).astype(BF16)

    r_in = grad_in_ref.shape[0]
    col_tiles = grad_in_ref.shape[1] // lanes
    for t in range(weight_ref.shape[0]):
        value = (weight_ref[t].astype(F32) + weight_other_ref[t].astype(F32)) * scale
        cols = slice(t % col_tiles * lanes, (t % col_tiles + 1) * lanes)
        for part in range(0, tile, 8):
            first = t // col_tiles * tile + part
            if first < r_in:
                grad_in_ref[first : first + 8, cols] = value[part : part + 8]
            else:
                grad_out_ref[first - r_in : first - r_in + 8, cols] = value[part : part + 8]


SMEM = pl.BlockSpec(memory_space=pltpu.SMEM)
VMEM = pl.BlockSpec(memory_space=pltpu.VMEM)


def plus(a, b):
    return (a.astype(F32) + b.astype(F32)).astype(BF16)


def swap(value, axis, mask):
    count = lax.axis_size(axis)
    return lax.ppermute(value, axis, [(i, i ^ mask) for i in range(count)])


def shards(
    zs,
    xs,
    edges,
    cotangent,
    fine_latents,
    coarse_block,
    w_in,
    w_out,
    senders,
    receivers,
    edge_count,
    coarse_ids,
):
    rows, width = edges.shape[1:]
    nodes = fine_latents.shape[1]
    slots = coarse_block.shape[1]
    depth = 2 * RIM + nodes + slots
    dom_axes = ("z", "y", "core")
    doms = zs * YS * CORES
    beside = [(i, (i + 1 - 2 * (i % 2)) % doms) for i in range(doms)]
    across = [(i, (i - 1 + 2 * (i % 2)) % doms) for i in range(doms)]
    place = lax.axis_index(dom_axes).astype(jnp.int32).reshape(1)
    even = lax.axis_index("core") == 0

    fine = fine_latents[0]
    first, last = fine[:RIM], fine[nodes - RIM :]
    following = lax.ppermute(jnp.where(even, first, last), dom_axes, across)
    near = lax.ppermute(jnp.where(even, last, first), dom_axes, beside)

    r_weight = (w_in.shape[0] + w_out.shape[0]) // doms
    w_tiles = r_weight // TILE * (width // LANES)
    c_tiles = -(-(NC + 2 * RIM) // (zs * CORES * TILE))
    tiles = w_tiles + c_tiles
    padded = c_tiles * TILE * zs * CORES
    half = zs // 2

    shape = jax.ShapeDtypeStruct
    own_ids = lax.dynamic_slice_in_dim(coarse_ids, place[0], 1, 0)
    names = jnp.concatenate([senders[None], receivers[None], own_ids], axis=1)
    table = jnp.concatenate([fine, coarse_block[0]], axis=0)
    loaded = pl.pallas_call(
        functools.partial(load_kernel, zs),
        out_shape=(
            shape((rows, 3 * width), BF16),
            shape((rows, width), BF16),
            shape((rows, width), F32),
            shape((2 * RIM + nodes + slots, rows), BF16),
            shape((nodes, rows), BF16),
            shape((padded, rows), BF16),
        ),
        in_specs=[SMEM, SMEM] + [VMEM] * 5,
        out_specs=(VMEM,) * 6,
        compiler_params=pltpu.CompilerParams(vmem_limit_bytes=24 * 2**20),
        cost_estimate=pl.CostEstimate(
            flops=600_000_000, bytes_accessed=6_000_000, transcendentals=0
        ),
        name="edge_inputs",
    )(edge_count, place, edges[0], cotangent[0], table, w_in, names)

    block = shape((YS, half, tiles, TILE, LANES), BF16)
    grad_edges, own, near_out, next_out, keep_a, send_a, keep_b, send_b = pl.pallas_call(
        functools.partial(edge_kernel, zs),
        out_shape=(
            shape((rows, width), BF16),
            shape((nodes, width), F32),
            shape((RIM, width), BF16),
            shape((RIM, width), BF16),
            block,
            block,
            block,
            block,
        ),
        in_specs=[SMEM] + [VMEM] * 10,
        out_specs=(VMEM,) * 8,
        scratch_shapes=[
            pltpu.VMEM(w_in.shape, F32),
            pltpu.VMEM(w_out.shape, F32),
            pltpu.VMEM((YS, padded, LANES), F32),
        ],
        compiler_params=pltpu.CompilerParams(vmem_limit_bytes=36 * 2**20),
        cost_estimate=pl.CostEstimate(
            flops=1_800_000_000, bytes_accessed=6_000_000, transcendentals=rows * width
        ),
        name="edge_backward",
    )(place, *loaded, w_in, w_out, near, following)

    other_a = swap(send_a, "core", 1)
    other_b = swap(send_b, "core", 1)
    two = YS // 2

    def split_plus(a, b, at):
        return plus(a[:at], b[:at]), plus(a[at:], b[at:])

    keep_a, send_a = split_plus(keep_a, other_a, two)
    keep_b, send_b = split_plus(keep_b, other_b, two)
    send_a, near_out, next_out = lax.optimization_barrier((send_a, near_out, next_out))
    other_a = swap(send_a, "y", Y_STEPS[0][0])
    other_b = swap(send_b, "y", Y_STEPS[1][0])
    inner = [(i, j) for i, j in across if abs(i - j) == 1]
    following = lax.ppermute(next_out, dom_axes, inner)
    near = lax.ppermute(near_out, dom_axes, beside)
    other_a, other_b, near, following = lax.optimization_barrier(
        (other_a, other_b, near, following)
    )
    keep_a, send_a = split_plus(keep_a, other_a, 1)
    keep_b, send_b = split_plus(keep_b, other_b, 1)
    other_b = swap(send_b, "y", Y_STEPS[1][1])
    other_a = swap(send_a, "y", Y_STEPS[0][1])
    send = plus(keep_b[0], other_b[0])
    keep = plus(keep_a[0], other_a[0])
    masks = [1 << b for b in range(bits(zs))]
    keep = plus(keep, swap(send, "z", 1))
    weight, coarse = keep[:, :w_tiles], keep[:, w_tiles:]
    z_order = [
        2 * sum(((i >> b) & 1) << (bits(half) - 1 - b) for b in range(bits(half)))
        for i in range(half)
    ]
    for mask in masks[1:]:
        rest = weight.shape[0] // 2
        turned = jnp.stack([coarse[z_order.index(r ^ mask)] for r in z_order])
        payload = jnp.concatenate(
            [weight[rest:].reshape(-1, TILE, LANES), turned.reshape(-1, TILE, LANES)], axis=0
        )
        other = swap(payload, "z", mask)
        weight = plus(weight[:rest], other[: rest * w_tiles].reshape(-1, w_tiles, TILE, LANES))
        coarse = plus(coarse, other[rest * w_tiles :].reshape(coarse.shape))
    weight = weight[0]

    z_order = z_order + [r ^ 1 for r in z_order]
    x_masks = [2 * (1 << b) - 1 for b in range(bits(xs))]
    coarse = jnp.concatenate([coarse, swap(coarse, "z", 1)], axis=0)
    weight, coarse = lax.optimization_barrier((weight, coarse))
    coarse = lax.all_to_all(
        jnp.broadcast_to(coarse[None], (YS,) + coarse.shape), "y", 0, 0, tiled=True
    )
    weight = plus(weight, swap(weight, "dp", 1))
    for mask in x_masks[:-1]:
        weight = plus(weight, swap(weight, "member", mask))
    weight_other = swap(weight, "member", x_masks[-1])
    coarse_other = swap(coarse, "core", 1)

    all_edges = rows * doms * xs * lax.axis_size("dp")
    grad_coarse, grad_fine, grad_in, grad_out = pl.pallas_call(
        functools.partial(last_kernel, z_order, 1.0 / math.sqrt(all_edges), 2 * rows),
        out_shape=(
            shape((slots, width), BF16),
            shape((nodes, width), BF16),
            shape((w_in.shape[0] // doms, width), F32),
            shape((w_out.shape[0] // doms, width), F32),
        ),
        in_specs=[SMEM] + [VMEM] * 8,
        out_specs=(VMEM,) * 4,
        compiler_params=pltpu.CompilerParams(vmem_limit_bytes=16 * 2**20),
        name="last_sums",
    )(
        place,
        names,
        coarse,
        coarse_other,
        own,
        near,
        following,
        weight,
        weight_other,
    )
    return (grad_edges[None], grad_fine[None], grad_coarse[None], grad_in, grad_out)


def solution(mesh):
    doms, xs, dps = (mesh.shape[name] for name in ("dom", "member", "dp"))
    zs = doms // (YS * CORES)
    split = Mesh(
        mesh.devices.reshape(zs, YS, CORES, xs, dps), ("z", "y", "core", "member", "dp")
    )
    dom = ("z", "y", "core")
    sample = ("member", "dp")
    latent = P(sample, dom, None)
    return jax.shard_map(
        functools.partial(shards, zs, xs),
        mesh=split,
        in_specs=(latent,) * 4 + (P(), P(), P(dom), P(dom), P(dom), P()),
        out_specs=(latent,) * 3 + (P(dom, None), P(dom, None)),
        check_vma=False,
    )
```

```python
import functools
import math

import jax
import jax.numpy as jnp
from jax import lax
from jax.experimental import pallas as pl
from jax.experimental.pallas import tpu as pltpu
from jax.sharding import Mesh
from jax.sharding import PartitionSpec as P

RIM = 16
NC = 642
YS = 4
CORES = 2
LANES = 128
TILE = 16

F32 = jnp.float32
BF16 = jnp.bfloat16

Y_ORDERS = ((0, 3, 1, 2), (0, 1, 3, 2))
Y_STEPS = ((1, 3), (3, 1))


def dot(left, right, dims):
    return lax.dot_general(left, right, (dims, ((), ())), preferred_element_type=F32)


def position(dom):
    core = lax.rem(dom, CORES)
    y = lax.rem(dom // CORES, YS)
    z = dom // (CORES * YS)
    return z, y, core


def bits(count):
    return count.bit_length() - 1


def picks(names, count):
    rows = lax.broadcasted_iota(jnp.int32, (count, names.shape[1]), 0)
    return jnp.where(rows == names, 1.0, 0.0).astype(BF16)


def load_kernel(
    zs,
    place_ref,
    edges_ref,
    table_ref,
    w_in_ref,
    names_ref,
    inputs_ref,
    pre_ref,
    pick_send_ref,
    pick_recv_ref,
    route_ref,
):
    rows, width = edges_ref.shape
    nodes = pick_recv_ref.shape[0]
    depth = pick_send_ref.shape[0]
    dom = place_ref[0]

    pick_send = picks(names_ref[:, :rows], depth)
    pick_recv = picks(names_ref[:, rows : 2 * rows], nodes)
    pick_send_ref[...] = pick_send
    pick_recv_ref[...] = pick_recv
    fine, coarse = table_ref[:nodes], table_ref[nodes:]
    h_send = dot(pick_send[RIM : RIM + nodes], fine, ((0,), (0,))) + dot(
        pick_send[2 * RIM + nodes :], coarse, ((0,), (0,))
    )
    h_recv = dot(pick_recv, fine, ((0,), (0,)))
    inputs_ref[:, :width] = edges_ref[...]
    inputs_ref[:, width : 2 * width] = h_send.astype(BF16)
    inputs_ref[:, 2 * width :] = h_recv.astype(BF16)
    pre_ref[...] = dot(inputs_ref[...], w_in_ref[...], ((1,), (0,)))

    padded = route_ref.shape[0]
    ids = names_ref[:, 2 * rows : 2 * rows + depth - 2 * RIM - nodes]
    route = dot(picks(ids, padded), pick_send[2 * RIM + nodes :], ((1,), (0,)))
    extent = (padded, 2 * RIM + nodes)
    lane = lax.broadcasted_iota(jnp.int32, extent, 1)
    down_row = jnp.where((lane < RIM) & (dom == 0), NC + lane, -1)
    end_row = jnp.where(
        (lane >= RIM + nodes) & (dom == zs * YS * CORES - 1), NC + lane - nodes, down_row
    )
    ends = jnp.where(lax.broadcasted_iota(jnp.int32, extent, 0) == end_row, 1.0, 0.0)
    route = route + dot(ends.astype(BF16), pick_send[: 2 * RIM + nodes], ((1,), (0,)))
    route_ref[...] = route.astype(BF16)


def edge_kernel(
    zs,
    count_ref,
    place_ref,
    inputs_ref,
    pre_ref,
    pick_send_ref,
    pick_recv_ref,
    route_ref,
    cot_ref,
    w_in_ref,
    w_out_ref,
    near_ref,
    next_ref,
    grad_edges_ref,
    own_ref,
    near_out_ref,
    next_out_ref,
    keep_a_ref,
    send_a_ref,
    keep_b_ref,
    send_b_ref,
    dw_in_ref,
    dw_out_ref,
    dense_ref,
):
    rows, width = cot_ref.shape
    nodes = pick_recv_ref.shape[0]
    z_me, y_me, core_me = position(place_ref[0])
    even = core_me == 0

    pick_send = pick_send_ref[...]
    pick_recv = pick_recv_ref[...]
    before = jnp.where(even, next_ref[...], near_ref[...])
    after = jnp.where(even, near_ref[...], next_ref[...])
    h_halo = (
        dot(pick_send[:RIM], before, ((0,), (0,)))
        + dot(pick_send[RIM + nodes : 2 * RIM + nodes], after, ((0,), (0,)))
    ).astype(BF16)
    h_send = (inputs_ref[:, width : 2 * width] + h_halo).astype(BF16)
    inputs = jnp.concatenate(
        [inputs_ref[:, :width], h_send, inputs_ref[:, 2 * width :]], axis=1
    )
    pre = pre_ref[...] + dot(h_halo, w_in_ref[width : 2 * width, :], ((1,), (0,)))
    sig = jax.nn.sigmoid(pre)
    act = (pre * sig).astype(BF16)
    hidden = dot(act, w_out_ref[...], ((1,), (0,)))
    centred = hidden - jnp.mean(hidden, axis=-1, keepdims=True)
    rstd = lax.rsqrt(jnp.mean(centred * centred, axis=-1, keepdims=True) + 1e-05)
    normed = centred * rstd
    live = lax.broadcasted_iota(jnp.int32, (rows, width), 0) < count_ref[0]
    dnorm = jnp.where(live, cot_ref[...].astype(F32), 0.0)
    dhidden = rstd * (
        dnorm
        - jnp.mean(dnorm, axis=-1, keepdims=True)
        - normed * jnp.mean(dnorm * normed, axis=-1, keepdims=True)
    )
    dhidden_b = dhidden.astype(BF16)
    dw_out_ref[...] = dot(act, dhidden_b, ((0,), (0,)))
    dact = dot(dhidden_b, w_out_ref[...], ((1,), (1,)))
    dpre_b = (dact * sig * (1.0 + pre * (1.0 - sig))).astype(BF16)
    dw_in_ref[...] = dot(inputs, dpre_b, ((0,), (0,)))
    dinputs = dot(dpre_b, w_in_ref[...], ((1,), (1,)))
    grad_edges_ref[...] = (dnorm + dinputs[:, :width]).astype(BF16)
    d_send = dinputs[:, width : 2 * width].astype(BF16)
    d_recv = dinputs[:, 2 * width :].astype(BF16)

    border = dot(pick_send[: 2 * RIM + nodes], d_send, ((1,), (0,)))
    down, up = border[:RIM], border[RIM + nodes :]
    near_out_ref[...] = jnp.where(even, up, down).astype(BF16)
    next_out_ref[...] = jnp.where(even, down, up).astype(BF16)
    own_ref[...] = border[RIM : RIM + nodes] + dot(pick_recv, d_recv, ((1,), (0,)))
    dense = dot(route_ref[...], d_send, ((1,), (0,)))
    for y in range(YS):
        dense_ref[y] = dense[:, y * LANES : (y + 1) * LANES]

    doms = zs * YS * CORES
    r_in = dw_in_ref.shape[0] // doms
    r_out = dw_out_ref.shape[0] // doms
    r_coarse = dense_ref.shape[1] // (zs * CORES)
    row_tiles = (r_in + r_out) // TILE
    col_tiles = width // LANES
    half = zs // 2

    def lay(base, y_order, refs, i, carry):
        index = base + i
        reverse = 0
        for b in range(bits(zs)):
            reverse = reverse | (((index >> b) & 1) << (bits(zs) - 1 - b))
        z = z_me ^ reverse
        for iy, ry in enumerate(y_order):
            y = y_me ^ ry
            for rc, ref in enumerate(refs):
                core = core_me ^ rc
                block = (z * YS + y) * CORES + core
                weight = jnp.concatenate(
                    [
                        dw_in_ref[pl.ds(pl.multiple_of(block * r_in, 8), r_in), :],
                        dw_out_ref[pl.ds(pl.multiple_of(block * r_out, 8), r_out), :],
                    ],
                    axis=0,
                ).astype(BF16)
                for rt in range(row_tiles):
                    for ct in range(col_tiles):
                        ref[iy, i, rt * col_tiles + ct] = weight[
                            rt * TILE : (rt + 1) * TILE, ct * LANES : (ct + 1) * LANES
                        ]
                first = pl.multiple_of((core * zs + z) * r_coarse, TILE)
                coarse = dense_ref[y, pl.ds(first, r_coarse), :].astype(BF16)
                for t in range(r_coarse // TILE):
                    ref[iy, i, row_tiles * col_tiles + t] = coarse[t * TILE : (t + 1) * TILE]
        return carry

    halves = ((keep_a_ref, send_a_ref), (keep_b_ref, send_b_ref))
    for h in range(2):
        lax.fori_loop(0, half, functools.partial(lay, h * half, Y_ORDERS[h], halves[h]), 0)


def last_kernel(
    z_order,
    scale,
    first_id,
    place_ref,
    names_ref,
    mine_ref,
    other_ref,
    own_ref,
    near_ref,
    next_ref,
    weight_ref,
    weight_other_ref,
    coarse_ref,
    fine_ref,
    grad_in_ref,
    grad_out_ref,
):
    ys, zs, tiles, tile, lanes = mine_ref.shape
    per = tiles * tile
    rows = zs * per
    slots = coarse_ref.shape[0]
    z_me, _, core_me = position(place_ref[0])
    ids = names_ref[:, first_id : first_id + slots]
    row = lax.broadcasted_iota(jnp.int32, (per, slots), 0)

    last = zs * ys * CORES - 1
    base = jnp.where(place_ref[0] == 0, NC + RIM, jnp.where(place_ref[0] == last, NC, -NC))
    end_ids = base + lax.broadcasted_iota(jnp.int32, (1, RIM), 1)
    end_row = lax.broadcasted_iota(jnp.int32, (per, RIM), 0)

    def pick(core, row, ids):
        return jnp.concatenate(
            [
                jnp.where(row + (core * zs + (z_me ^ rz)) * per == ids, 1.0, 0.0)
                for rz in z_order
            ],
            axis=0,
        ).astype(BF16)

    pick_mine, pick_other = pick(core_me, row, ids), pick(1 - core_me, row, ids)
    end_mine, end_other = pick(core_me, end_row, end_ids), pick(1 - core_me, end_row, end_ids)
    ends = []
    for y in range(ys):
        mine = mine_ref[y].reshape(rows, lanes)
        other = other_ref[y].reshape(rows, lanes)
        total = dot(pick_mine, mine, ((0,), (0,))) + dot(pick_other, other, ((0,), (0,)))
        ends.append(dot(end_mine, mine, ((0,), (0,))) + dot(end_other, other, ((0,), (0,))))
        coarse_ref[:, y * lanes : (y + 1) * lanes] = total.astype(BF16)
    nodes = own_ref.shape[0]
    even = core_me == 0
    near = near_ref[...].astype(F32)
    following = jnp.where(base > 0, jnp.concatenate(ends, axis=1), next_ref[...].astype(F32))
    from_down = jnp.where(even, following, near)
    from_up = jnp.where(even, near, following)
    fine_ref[:RIM] = (own_ref[:RIM] + from_down).astype(BF16)
    fine_ref[RIM : nodes - RIM] = own_ref[RIM : nodes - RIM].astype(BF16)
    fine_ref[nodes - RIM :] = (own_ref[nodes - RIM :] + from_up).astype(BF16)

    r_in = grad_in_ref.shape[0]
    col_tiles = grad_in_ref.shape[1] // lanes
    for t in range(weight_ref.shape[0]):
        value = (weight_ref[t].astype(F32) + weight_other_ref[t].astype(F32)) * scale
        cols = slice(t % col_tiles * lanes, (t % col_tiles + 1) * lanes)
        for part in range(0, tile, 8):
            first = t // col_tiles * tile + part
            if first < r_in:
                grad_in_ref[first : first + 8, cols] = value[part : part + 8]
            else:
                grad_out_ref[first - r_in : first - r_in + 8, cols] = value[part : part + 8]


SMEM = pl.BlockSpec(memory_space=pltpu.SMEM)
VMEM = pl.BlockSpec(memory_space=pltpu.VMEM)


def plus(a, b):
    return (a.astype(F32) + b.astype(F32)).astype(BF16)


def swap(value, axis, mask):
    count = lax.axis_size(axis)
    return lax.ppermute(value, axis, [(i, i ^ mask) for i in range(count)])


def shards(
    zs,
    xs,
    edges,
    cotangent,
    fine_latents,
    coarse_block,
    w_in,
    w_out,
    senders,
    receivers,
    edge_count,
    coarse_ids,
):
    rows, width = edges.shape[1:]
    nodes = fine_latents.shape[1]
    slots = coarse_block.shape[1]
    depth = 2 * RIM + nodes + slots
    dom_axes = ("z", "y", "core")
    doms = zs * YS * CORES
    beside = [(i, (i + 1 - 2 * (i % 2)) % doms) for i in range(doms)]
    across = [(i, (i - 1 + 2 * (i % 2)) % doms) for i in range(doms)]
    place = lax.axis_index(dom_axes).astype(jnp.int32).reshape(1)
    even = lax.axis_index("core") == 0

    fine = fine_latents[0]
    first, last = fine[:RIM], fine[nodes - RIM :]
    following = lax.ppermute(jnp.where(even, first, last), dom_axes, across)
    near = lax.ppermute(jnp.where(even, last, first), dom_axes, beside)

    r_weight = (w_in.shape[0] + w_out.shape[0]) // doms
    w_tiles = r_weight // TILE * (width // LANES)
    c_tiles = -(-(NC + 2 * RIM) // (zs * CORES * TILE))
    tiles = w_tiles + c_tiles
    padded = c_tiles * TILE * zs * CORES
    half = zs // 2

    shape = jax.ShapeDtypeStruct
    own_ids = lax.dynamic_slice_in_dim(coarse_ids, place[0], 1, 0)
    names = jnp.concatenate([senders[None], receivers[None], own_ids], axis=1)
    table = jnp.concatenate([fine, coarse_block[0]], axis=0)
    loaded = pl.pallas_call(
        functools.partial(load_kernel, zs),
        out_shape=(
            shape((rows, 3 * width), BF16),
            shape((rows, width), F32),
            shape((2 * RIM + nodes + slots, rows), BF16),
            shape((nodes, rows), BF16),
            shape((padded, rows), BF16),
        ),
        in_specs=[SMEM] + [VMEM] * 4,
        out_specs=(VMEM,) * 5,
        compiler_params=pltpu.CompilerParams(vmem_limit_bytes=24 * 2**20),
        cost_estimate=pl.CostEstimate(
            flops=600_000_000, bytes_accessed=6_000_000, transcendentals=0
        ),
        name="edge_inputs",
    )(place, edges[0], table, w_in, names)

    block = shape((YS, half, tiles, TILE, LANES), BF16)
    grad_edges, own, near_out, next_out, keep_a, send_a, keep_b, send_b = pl.pallas_call(
        functools.partial(edge_kernel, zs),
        out_shape=(
            shape((rows, width), BF16),
            shape((nodes, width), F32),
            shape((RIM, width), BF16),
            shape((RIM, width), BF16),
            block,
            block,
            block,
            block,
        ),
        in_specs=[SMEM, SMEM] + [VMEM] * 10,
        out_specs=(VMEM,) * 8,
        scratch_shapes=[
            pltpu.VMEM(w_in.shape, F32),
            pltpu.VMEM(w_out.shape, F32),
            pltpu.VMEM((YS, padded, LANES), F32),
        ],
        compiler_params=pltpu.CompilerParams(vmem_limit_bytes=36 * 2**20),
        cost_estimate=pl.CostEstimate(
            flops=1_800_000_000, bytes_accessed=6_000_000, transcendentals=rows * width
        ),
        name="edge_backward",
    )(edge_count, place, *loaded, cotangent[0], w_in, w_out, near, following)

    other_a = swap(send_a, "core", 1)
    other_b = swap(send_b, "core", 1)
    two = YS // 2

    def split_plus(a, b, at):
        return plus(a[:at], b[:at]), plus(a[at:], b[at:])

    keep_a, send_a = split_plus(keep_a, other_a, two)
    keep_b, send_b = split_plus(keep_b, other_b, two)
    send_a, near_out, next_out = lax.optimization_barrier((send_a, near_out, next_out))
    other_a = swap(send_a, "y", Y_STEPS[0][0])
    other_b = swap(send_b, "y", Y_STEPS[1][0])
    inner = [(i, j) for i, j in across if abs(i - j) == 1]
    following = lax.ppermute(next_out, dom_axes, inner)
    near = lax.ppermute(near_out, dom_axes, beside)
    other_a, other_b, near, following = lax.optimization_barrier(
        (other_a, other_b, near, following)
    )
    keep_a, send_a = split_plus(keep_a, other_a, 1)
    keep_b, send_b = split_plus(keep_b, other_b, 1)
    other_b = swap(send_b, "y", Y_STEPS[1][1])
    other_a = swap(send_a, "y", Y_STEPS[0][1])
    send = plus(keep_b[0], other_b[0])
    keep = plus(keep_a[0], other_a[0])
    masks = [1 << b for b in range(bits(zs))]
    keep = plus(keep, swap(send, "z", 1))
    weight, coarse = keep[:, :w_tiles], keep[:, w_tiles:]
    z_order = [
        2 * sum(((i >> b) & 1) << (bits(half) - 1 - b) for b in range(bits(half)))
        for i in range(half)
    ]
    for mask in masks[1:]:
        rest = weight.shape[0] // 2
        turned = jnp.stack([coarse[z_order.index(r ^ mask)] for r in z_order])
        payload = jnp.concatenate(
            [weight[rest:].reshape(-1, TILE, LANES), turned.reshape(-1, TILE, LANES)], axis=0
        )
        other = swap(payload, "z", mask)
        weight = plus(weight[:rest], other[: rest * w_tiles].reshape(-1, w_tiles, TILE, LANES))
        coarse = plus(coarse, other[rest * w_tiles :].reshape(coarse.shape))
    weight = weight[0]

    z_order = z_order + [r ^ 1 for r in z_order]
    x_masks = [2 * (1 << b) - 1 for b in range(bits(xs))]
    coarse_other = swap(coarse, "z", 1)
    for i, mask in enumerate(x_masks):
        weight_other = swap(weight, "member", mask)
        if i == 0:
            weight_other, coarse_other = lax.optimization_barrier((weight_other, coarse_other))
            coarse = jnp.concatenate([coarse, coarse_other], axis=0)
            coarse = lax.all_to_all(
                jnp.broadcast_to(coarse[None], (YS,) + coarse.shape), "y", 0, 0, tiled=True
            )
        elif i == len(x_masks) - 1:
            weight_other, coarse = lax.optimization_barrier((weight_other, coarse))
        weight = plus(weight, weight_other)
    weight_other = swap(weight, "dp", 1)
    coarse_other = swap(coarse, "core", 1)

    all_edges = rows * doms * xs * lax.axis_size("dp")
    grad_coarse, grad_fine, grad_in, grad_out = pl.pallas_call(
        functools.partial(last_kernel, z_order, 1.0 / math.sqrt(all_edges), 2 * rows),
        out_shape=(
            shape((slots, width), BF16),
            shape((nodes, width), BF16),
            shape((w_in.shape[0] // doms, width), F32),
            shape((w_out.shape[0] // doms, width), F32),
        ),
        in_specs=[SMEM] + [VMEM] * 8,
        out_specs=(VMEM,) * 4,
        compiler_params=pltpu.CompilerParams(vmem_limit_bytes=16 * 2**20),
        name="last_sums",
    )(
        place,
        names,
        coarse,
        coarse_other,
        own,
        near,
        following,
        weight,
        weight_other,
    )
    return (grad_edges[None], grad_fine[None], grad_coarse[None], grad_in, grad_out)


def solution(mesh):
    doms, xs, dps = (mesh.shape[name] for name in ("dom", "member", "dp"))
    zs = doms // (YS * CORES)
    split = Mesh(
        mesh.devices.reshape(zs, YS, CORES, xs, dps), ("z", "y", "core", "member", "dp")
    )
    dom = ("z", "y", "core")
    sample = ("member", "dp")
    latent = P(sample, dom, None)
    return jax.shard_map(
        functools.partial(shards, zs, xs),
        mesh=split,
        in_specs=(latent,) * 4 + (P(), P(), P(dom), P(dom), P(dom), P()),
        out_specs=(latent,) * 3 + (P(dom, None), P(dom, None)),
        check_vma=False,
    )
```

```python
import functools
import math

import jax
import jax.numpy as jnp
from jax import lax
from jax.experimental import pallas as pl
from jax.experimental.pallas import tpu as pltpu
from jax.sharding import Mesh
from jax.sharding import PartitionSpec as P

RIM = 16
NC = 642
YS = 4
CORES = 2
LANES = 128
TILE = 16

F32 = jnp.float32
BF16 = jnp.bfloat16

Y_ORDERS = ((0, 3, 1, 2), (0, 1, 3, 2))
Y_STEPS = ((1, 3), (3, 1))


def dot(left, right, dims):
    return lax.dot_general(left, right, (dims, ((), ())), preferred_element_type=F32)


def position(dom):
    core = lax.rem(dom, CORES)
    y = lax.rem(dom // CORES, YS)
    z = dom // (CORES * YS)
    return z, y, core


def bits(count):
    return count.bit_length() - 1


def picks(names, count):
    rows = lax.broadcasted_iota(jnp.int32, (count, names.shape[1]), 0)
    return jnp.where(rows == names, 1.0, 0.0).astype(BF16)


def load_kernel(
    zs,
    place_ref,
    edges_ref,
    table_ref,
    w_in_ref,
    names_ref,
    inputs_ref,
    pre_ref,
    pick_send_ref,
    pick_recv_ref,
    route_ref,
):
    rows, width = edges_ref.shape
    nodes = pick_recv_ref.shape[0]
    depth = pick_send_ref.shape[0]
    dom = place_ref[0]

    pick_send = picks(names_ref[:, :rows], depth)
    pick_recv = picks(names_ref[:, rows : 2 * rows], nodes)
    pick_send_ref[...] = pick_send
    pick_recv_ref[...] = pick_recv
    fine, coarse = table_ref[:nodes], table_ref[nodes:]
    h_send = dot(pick_send[RIM : RIM + nodes], fine, ((0,), (0,))) + dot(
        pick_send[2 * RIM + nodes :], coarse, ((0,), (0,))
    )
    h_recv = dot(pick_recv, fine, ((0,), (0,)))
    inputs_ref[:, :width] = edges_ref[...]
    inputs_ref[:, width : 2 * width] = h_send.astype(BF16)
    inputs_ref[:, 2 * width :] = h_recv.astype(BF16)
    pre_ref[...] = dot(inputs_ref[...], w_in_ref[...], ((1,), (0,)))

    padded = route_ref.shape[0]
    ids = names_ref[:, 2 * rows : 2 * rows + depth - 2 * RIM - nodes]
    route = dot(picks(ids, padded), pick_send[2 * RIM + nodes :], ((1,), (0,)))
    extent = (padded, 2 * RIM + nodes)
    lane = lax.broadcasted_iota(jnp.int32, extent, 1)
    down_row = jnp.where((lane < RIM) & (dom == 0), NC + lane, -1)
    end_row = jnp.where(
        (lane >= RIM + nodes) & (dom == zs * YS * CORES - 1), NC + lane - nodes, down_row
    )
    ends = jnp.where(lax.broadcasted_iota(jnp.int32, extent, 0) == end_row, 1.0, 0.0)
    route = route + dot(ends.astype(BF16), pick_send[: 2 * RIM + nodes], ((1,), (0,)))
    route_ref[...] = route.astype(BF16)


def edge_kernel(
    zs,
    count_ref,
    place_ref,
    inputs_ref,
    pre_ref,
    pick_send_ref,
    pick_recv_ref,
    route_ref,
    cot_ref,
    w_in_ref,
    w_out_ref,
    near_ref,
    next_ref,
    grad_edges_ref,
    own_ref,
    near_out_ref,
    next_out_ref,
    keep_a_ref,
    send_a_ref,
    keep_b_ref,
    send_b_ref,
    dw_in_ref,
    dw_out_ref,
    dense_ref,
):
    rows, width = cot_ref.shape
    nodes = pick_recv_ref.shape[0]
    z_me, y_me, core_me = position(place_ref[0])
    even = core_me == 0

    pick_send = pick_send_ref[...]
    pick_recv = pick_recv_ref[...]
    before = jnp.where(even, next_ref[...], near_ref[...])
    after = jnp.where(even, near_ref[...], next_ref[...])
    h_halo = (
        dot(pick_send[:RIM], before, ((0,), (0,)))
        + dot(pick_send[RIM + nodes : 2 * RIM + nodes], after, ((0,), (0,)))
    ).astype(BF16)
    h_send = (inputs_ref[:, width : 2 * width] + h_halo).astype(BF16)
    inputs = jnp.concatenate(
        [inputs_ref[:, :width], h_send, inputs_ref[:, 2 * width :]], axis=1
    )
    pre = pre_ref[...] + dot(h_halo, w_in_ref[width : 2 * width, :], ((1,), (0,)))
    sig = jax.nn.sigmoid(pre)
    act = (pre * sig).astype(BF16)
    hidden = dot(act, w_out_ref[...], ((1,), (0,)))
    centred = hidden - jnp.mean(hidden, axis=-1, keepdims=True)
    rstd = lax.rsqrt(jnp.mean(centred * centred, axis=-1, keepdims=True) + 1e-05)
    normed = centred * rstd
    live = lax.broadcasted_iota(jnp.int32, (rows, width), 0) < count_ref[0]
    dnorm = jnp.where(live, cot_ref[...].astype(F32), 0.0)
    dhidden = rstd * (
        dnorm
        - jnp.mean(dnorm, axis=-1, keepdims=True)
        - normed * jnp.mean(dnorm * normed, axis=-1, keepdims=True)
    )
    dhidden_b = dhidden.astype(BF16)
    dw_out_ref[...] = dot(act, dhidden_b, ((0,), (0,)))
    dact = dot(dhidden_b, w_out_ref[...], ((1,), (1,)))
    dpre_b = (dact * sig * (1.0 + pre * (1.0 - sig))).astype(BF16)
    dw_in_ref[...] = dot(inputs, dpre_b, ((0,), (0,)))
    dinputs = dot(dpre_b, w_in_ref[...], ((1,), (1,)))
    grad_edges_ref[...] = (dnorm + dinputs[:, :width]).astype(BF16)
    d_send = dinputs[:, width : 2 * width].astype(BF16)
    d_recv = dinputs[:, 2 * width :].astype(BF16)

    border = dot(pick_send[: 2 * RIM + nodes], d_send, ((1,), (0,)))
    down, up = border[:RIM], border[RIM + nodes :]
    near_out_ref[...] = jnp.where(even, up, down).astype(BF16)
    next_out_ref[...] = jnp.where(even, down, up).astype(BF16)
    own_ref[...] = border[RIM : RIM + nodes] + dot(pick_recv, d_recv, ((1,), (0,)))
    dense = dot(route_ref[...], d_send, ((1,), (0,)))
    for y in range(YS):
        dense_ref[y] = dense[:, y * LANES : (y + 1) * LANES]

    doms = zs * YS * CORES
    r_in = dw_in_ref.shape[0] // doms
    r_out = dw_out_ref.shape[0] // doms
    r_coarse = dense_ref.shape[1] // (zs * CORES)
    row_tiles = (r_in + r_out) // TILE
    col_tiles = width // LANES
    half = zs // 2

    def lay(base, y_order, refs, i, carry):
        index = base + i
        reverse = 0
        for b in range(bits(zs)):
            reverse = reverse | (((index >> b) & 1) << (bits(zs) - 1 - b))
        z = z_me ^ reverse
        for iy, ry in enumerate(y_order):
            y = y_me ^ ry
            for rc, ref in enumerate(refs):
                core = core_me ^ rc
                block = (z * YS + y) * CORES + core
                weight = jnp.concatenate(
                    [
                        dw_in_ref[pl.ds(pl.multiple_of(block * r_in, 8), r_in), :],
                        dw_out_ref[pl.ds(pl.multiple_of(block * r_out, 8), r_out), :],
                    ],
                    axis=0,
                ).astype(BF16)
                for rt in range(row_tiles):
                    for ct in range(col_tiles):
                        ref[iy, i, rt * col_tiles + ct] = weight[
                            rt * TILE : (rt + 1) * TILE, ct * LANES : (ct + 1) * LANES
                        ]
                first = pl.multiple_of((core * zs + z) * r_coarse, TILE)
                coarse = dense_ref[y, pl.ds(first, r_coarse), :].astype(BF16)
                for t in range(r_coarse // TILE):
                    ref[iy, i, row_tiles * col_tiles + t] = coarse[t * TILE : (t + 1) * TILE]
        return carry

    halves = ((keep_a_ref, send_a_ref), (keep_b_ref, send_b_ref))
    for h in range(2):
        lax.fori_loop(0, half, functools.partial(lay, h * half, Y_ORDERS[h], halves[h]), 0)


def last_kernel(
    z_order,
    scale,
    first_id,
    place_ref,
    names_ref,
    mine_ref,
    other_ref,
    own_ref,
    near_ref,
    next_ref,
    weight_ref,
    weight_other_ref,
    coarse_ref,
    fine_ref,
    grad_in_ref,
    grad_out_ref,
):
    ys, zs, tiles, tile, lanes = mine_ref.shape
    per = tiles * tile
    rows = zs * per
    slots = coarse_ref.shape[0]
    z_me, _, core_me = position(place_ref[0])
    ids = names_ref[:, first_id : first_id + slots]
    row = lax.broadcasted_iota(jnp.int32, (per, slots), 0)

    last = zs * ys * CORES - 1
    base = jnp.where(place_ref[0] == 0, NC + RIM, jnp.where(place_ref[0] == last, NC, -NC))
    end_ids = base + lax.broadcasted_iota(jnp.int32, (1, RIM), 1)
    end_row = lax.broadcasted_iota(jnp.int32, (per, RIM), 0)

    def pick(core, row, ids):
        return jnp.concatenate(
            [
                jnp.where(row + (core * zs + (z_me ^ rz)) * per == ids, 1.0, 0.0)
                for rz in z_order
            ],
            axis=0,
        ).astype(BF16)

    pick_mine, pick_other = pick(core_me, row, ids), pick(1 - core_me, row, ids)
    end_mine, end_other = pick(core_me, end_row, end_ids), pick(1 - core_me, end_row, end_ids)
    ends = []
    for y in range(ys):
        mine = mine_ref[y].reshape(rows, lanes)
        other = other_ref[y].reshape(rows, lanes)
        total = dot(pick_mine, mine, ((0,), (0,))) + dot(pick_other, other, ((0,), (0,)))
        ends.append(dot(end_mine, mine, ((0,), (0,))) + dot(end_other, other, ((0,), (0,))))
        coarse_ref[:, y * lanes : (y + 1) * lanes] = total.astype(BF16)
    nodes = own_ref.shape[0]
    even = core_me == 0
    near = near_ref[...].astype(F32)
    following = jnp.where(base > 0, jnp.concatenate(ends, axis=1), next_ref[...].astype(F32))
    from_down = jnp.where(even, following, near)
    from_up = jnp.where(even, near, following)
    fine_ref[:RIM] = (own_ref[:RIM] + from_down).astype(BF16)
    fine_ref[RIM : nodes - RIM] = own_ref[RIM : nodes - RIM].astype(BF16)
    fine_ref[nodes - RIM :] = (own_ref[nodes - RIM :] + from_up).astype(BF16)

    r_in = grad_in_ref.shape[0]
    col_tiles = grad_in_ref.shape[1] // lanes
    for t in range(weight_ref.shape[0]):
        value = (weight_ref[t].astype(F32) + weight_other_ref[t].astype(F32)) * scale
        cols = slice(t % col_tiles * lanes, (t % col_tiles + 1) * lanes)
        for part in range(0, tile, 8):
            first = t // col_tiles * tile + part
            if first < r_in:
                grad_in_ref[first : first + 8, cols] = value[part : part + 8]
            else:
                grad_out_ref[first - r_in : first - r_in + 8, cols] = value[part : part + 8]


SMEM = pl.BlockSpec(memory_space=pltpu.SMEM)
VMEM = pl.BlockSpec(memory_space=pltpu.VMEM)


def plus(a, b):
    return (a.astype(F32) + b.astype(F32)).astype(BF16)


def swap(value, axis, mask):
    count = lax.axis_size(axis)
    return lax.ppermute(value, axis, [(i, i ^ mask) for i in range(count)])


def shards(
    zs,
    xs,
    edges,
    cotangent,
    fine_latents,
    coarse_block,
    w_in,
    w_out,
    senders,
    receivers,
    edge_count,
    coarse_ids,
):
    rows, width = edges.shape[1:]
    nodes = fine_latents.shape[1]
    slots = coarse_block.shape[1]
    depth = 2 * RIM + nodes + slots
    dom_axes = ("z", "y", "core")
    doms = zs * YS * CORES
    beside = [(i, (i + 1 - 2 * (i % 2)) % doms) for i in range(doms)]
    across = [(i, (i - 1 + 2 * (i % 2)) % doms) for i in range(doms)]
    place = lax.axis_index(dom_axes).astype(jnp.int32).reshape(1)
    even = lax.axis_index("core") == 0

    fine = fine_latents[0]
    first, last = fine[:RIM], fine[nodes - RIM :]
    following = lax.ppermute(jnp.where(even, first, last), dom_axes, across)
    near = lax.ppermute(jnp.where(even, last, first), dom_axes, beside)

    r_weight = (w_in.shape[0] + w_out.shape[0]) // doms
    w_tiles = r_weight // TILE * (width // LANES)
    c_tiles = -(-(NC + 2 * RIM) // (zs * CORES * TILE))
    tiles = w_tiles + c_tiles
    padded = c_tiles * TILE * zs * CORES
    half = zs // 2

    shape = jax.ShapeDtypeStruct
    own_ids = lax.dynamic_slice_in_dim(coarse_ids, place[0], 1, 0)
    names = jnp.concatenate([senders[None], receivers[None], own_ids], axis=1)
    table = jnp.concatenate([fine, coarse_block[0]], axis=0)
    loaded = pl.pallas_call(
        functools.partial(load_kernel, zs),
        out_shape=(
            shape((rows, 3 * width), BF16),
            shape((rows, width), F32),
            shape((2 * RIM + nodes + slots, rows), BF16),
            shape((nodes, rows), BF16),
            shape((padded, rows), BF16),
        ),
        in_specs=[SMEM] + [VMEM] * 4,
        out_specs=(VMEM,) * 5,
        compiler_params=pltpu.CompilerParams(vmem_limit_bytes=24 * 2**20),
        cost_estimate=pl.CostEstimate(
            flops=600_000_000, bytes_accessed=6_000_000, transcendentals=0
        ),
        name="edge_inputs",
    )(place, edges[0], table, w_in, names)

    block = shape((YS, half, tiles, TILE, LANES), BF16)
    grad_edges, own, near_out, next_out, keep_a, send_a, keep_b, send_b = pl.pallas_call(
        functools.partial(edge_kernel, zs),
        out_shape=(
            shape((rows, width), BF16),
            shape((nodes, width), F32),
            shape((RIM, width), BF16),
            shape((RIM, width), BF16),
            block,
            block,
            block,
            block,
        ),
        in_specs=[SMEM, SMEM] + [VMEM] * 10,
        out_specs=(VMEM,) * 8,
        scratch_shapes=[
            pltpu.VMEM(w_in.shape, F32),
            pltpu.VMEM(w_out.shape, F32),
            pltpu.VMEM((YS, padded, LANES), F32),
        ],
        compiler_params=pltpu.CompilerParams(vmem_limit_bytes=36 * 2**20),
        cost_estimate=pl.CostEstimate(
            flops=1_800_000_000, bytes_accessed=6_000_000, transcendentals=rows * width
        ),
        name="edge_backward",
    )(edge_count, place, *loaded, cotangent[0], w_in, w_out, near, following)

    other_a = swap(send_a, "core", 1)
    other_b = swap(send_b, "core", 1)
    two = YS // 2

    def split_plus(a, b, at):
        return plus(a[:at], b[:at]), plus(a[at:], b[at:])

    keep_a, send_a = split_plus(keep_a, other_a, two)
    keep_b, send_b = split_plus(keep_b, other_b, two)
    send_a, near_out, next_out = lax.optimization_barrier((send_a, near_out, next_out))
    other_a = swap(send_a, "y", Y_STEPS[0][0])
    other_b = swap(send_b, "y", Y_STEPS[1][0])
    inner = [(i, j) for i, j in across if abs(i - j) == 1]
    following = lax.ppermute(next_out, dom_axes, inner)
    near = lax.ppermute(near_out, dom_axes, beside)
    other_a, other_b, near, following = lax.optimization_barrier(
        (other_a, other_b, near, following)
    )
    keep_a, send_a = split_plus(keep_a, other_a, 1)
    keep_b, send_b = split_plus(keep_b, other_b, 1)
    other_b = swap(send_b, "y", Y_STEPS[1][1])
    other_a = swap(send_a, "y", Y_STEPS[0][1])
    send = plus(keep_b[0], other_b[0])
    keep = plus(keep_a[0], other_a[0])
    masks = [1 << b for b in range(bits(zs))]
    keep = plus(keep, swap(send, "z", 1))
    weight, coarse = keep[:, :w_tiles], keep[:, w_tiles:]
    z_order = [
        2 * sum(((i >> b) & 1) << (bits(half) - 1 - b) for b in range(bits(half)))
        for i in range(half)
    ]
    for mask in masks[1:]:
        rest = weight.shape[0] // 2
        turned = jnp.stack([coarse[z_order.index(r ^ mask)] for r in z_order])
        payload = jnp.concatenate(
            [weight[rest:].reshape(-1, TILE, LANES), turned.reshape(-1, TILE, LANES)], axis=0
        )
        other = swap(payload, "z", mask)
        weight = plus(weight[:rest], other[: rest * w_tiles].reshape(-1, w_tiles, TILE, LANES))
        coarse = plus(coarse, other[rest * w_tiles :].reshape(coarse.shape))
    weight = weight[0]

    z_order = z_order + [r ^ 1 for r in z_order]
    x_masks = [2 * (1 << b) - 1 for b in range(bits(xs))]
    coarse_other = swap(coarse, "z", 1)
    weight_steps = [("member", mask) for mask in x_masks]
    weight_steps.insert(1, ("dp", 1))
    weight_other = swap(weight, *weight_steps[0])
    weight_other, coarse_other = lax.optimization_barrier((weight_other, coarse_other))
    coarse = jnp.concatenate([coarse, coarse_other], axis=0)
    weight = plus(weight, weight_other)
    weight, coarse = lax.optimization_barrier((weight, coarse))
    weight_other = swap(weight, *weight_steps[1])
    coarse = lax.all_to_all(
        jnp.broadcast_to(coarse[None], (YS,) + coarse.shape), "y", 0, 0, tiled=True
    )
    weight_other, coarse = lax.optimization_barrier((weight_other, coarse))
    for step in weight_steps[2:]:
        weight = plus(weight, weight_other)
        weight_other = swap(weight, *step)
    coarse_other = swap(coarse, "core", 1)

    all_edges = rows * doms * xs * lax.axis_size("dp")
    grad_coarse, grad_fine, grad_in, grad_out = pl.pallas_call(
        functools.partial(last_kernel, z_order, 1.0 / math.sqrt(all_edges), 2 * rows),
        out_shape=(
            shape((slots, width), BF16),
            shape((nodes, width), BF16),
            shape((w_in.shape[0] // doms, width), F32),
            shape((w_out.shape[0] // doms, width), F32),
        ),
        in_specs=[SMEM] + [VMEM] * 8,
        out_specs=(VMEM,) * 4,
        compiler_params=pltpu.CompilerParams(vmem_limit_bytes=16 * 2**20),
        name="last_sums",
    )(
        place,
        names,
        coarse,
        coarse_other,
        own,
        near,
        following,
        weight,
        weight_other,
    )
    return (grad_edges[None], grad_fine[None], grad_coarse[None], grad_in, grad_out)


def solution(mesh):
    doms, xs, dps = (mesh.shape[name] for name in ("dom", "member", "dp"))
    zs = doms // (YS * CORES)
    split = Mesh(
        mesh.devices.reshape(zs, YS, CORES, xs, dps), ("z", "y", "core", "member", "dp")
    )
    dom = ("z", "y", "core")
    sample = ("member", "dp")
    latent = P(sample, dom, None)
    return jax.shard_map(
        functools.partial(shards, zs, xs),
        mesh=split,
        in_specs=(latent,) * 4 + (P(), P(), P(dom), P(dom), P(dom), P()),
        out_specs=(latent,) * 3 + (P(dom, None), P(dom, None)),
        check_vma=False,
    )
```

```python
import functools
import math

import jax
import jax.numpy as jnp
from jax import lax
from jax.experimental import pallas as pl
from jax.experimental.pallas import tpu as pltpu
from jax.sharding import Mesh
from jax.sharding import PartitionSpec as P

RIM = 16
NC = 642
YS = 4
CORES = 2
LANES = 128
TILE = 16

F32 = jnp.float32
BF16 = jnp.bfloat16

Y_ORDERS = ((0, 3, 1, 2), (0, 1, 3, 2))
Y_STEPS = ((1, 3), (3, 1))


def dot(left, right, dims):
    return lax.dot_general(left, right, (dims, ((), ())), preferred_element_type=F32)


def position(dom):
    core = lax.rem(dom, CORES)
    y = lax.rem(dom // CORES, YS)
    z = dom // (CORES * YS)
    return z, y, core


def bits(count):
    return count.bit_length() - 1


def picks(names, count):
    rows = lax.broadcasted_iota(jnp.int32, (count, names.shape[1]), 0)
    return jnp.where(rows == names, 1.0, 0.0).astype(BF16)


def load_kernel(
    zs,
    place_ref,
    table_ref,
    names_ref,
    picked_ref,
    pick_send_ref,
    pick_recv_ref,
    route_ref,
):
    rows, width = picked_ref.shape[0], table_ref.shape[1]
    nodes = pick_recv_ref.shape[0]
    depth = pick_send_ref.shape[0]
    dom = place_ref[0]

    pick_send = picks(names_ref[:, :rows], depth)
    pick_recv = picks(names_ref[:, rows : 2 * rows], nodes)
    pick_send_ref[...] = pick_send
    pick_recv_ref[...] = pick_recv
    fine, coarse = table_ref[:nodes], table_ref[nodes:]
    h_send = dot(pick_send[RIM : RIM + nodes], fine, ((0,), (0,))) + dot(
        pick_send[2 * RIM + nodes :], coarse, ((0,), (0,))
    )
    h_recv = dot(pick_recv, fine, ((0,), (0,)))
    picked_ref[:, :width] = h_send.astype(BF16)
    picked_ref[:, width:] = h_recv.astype(BF16)

    padded = route_ref.shape[0]
    ids = names_ref[:, 2 * rows : 2 * rows + depth - 2 * RIM - nodes]
    route = dot(picks(ids, padded), pick_send[2 * RIM + nodes :], ((1,), (0,)))
    extent = (padded, 2 * RIM + nodes)
    lane = lax.broadcasted_iota(jnp.int32, extent, 1)
    down_row = jnp.where((lane < RIM) & (dom == 0), NC + lane, -1)
    end_row = jnp.where(
        (lane >= RIM + nodes) & (dom == zs * YS * CORES - 1), NC + lane - nodes, down_row
    )
    ends = jnp.where(lax.broadcasted_iota(jnp.int32, extent, 0) == end_row, 1.0, 0.0)
    route = route + dot(ends.astype(BF16), pick_send[: 2 * RIM + nodes], ((1,), (0,)))
    route_ref[...] = route.astype(BF16)


def edge_kernel(
    zs,
    count_ref,
    place_ref,
    picked_ref,
    pick_send_ref,
    pick_recv_ref,
    route_ref,
    edges_ref,
    cot_ref,
    w_in_ref,
    w_out_ref,
    near_ref,
    next_ref,
    grad_edges_ref,
    own_ref,
    near_out_ref,
    next_out_ref,
    keep_a_ref,
    send_a_ref,
    keep_b_ref,
    send_b_ref,
    dw_in_ref,
    dw_out_ref,
    dense_ref,
):
    rows, width = cot_ref.shape
    nodes = pick_recv_ref.shape[0]
    z_me, y_me, core_me = position(place_ref[0])
    even = core_me == 0

    pick_send = pick_send_ref[...]
    pick_recv = pick_recv_ref[...]
    before = jnp.where(even, next_ref[...], near_ref[...])
    after = jnp.where(even, near_ref[...], next_ref[...])
    h_halo = (
        dot(pick_send[:RIM], before, ((0,), (0,)))
        + dot(pick_send[RIM + nodes : 2 * RIM + nodes], after, ((0,), (0,)))
    ).astype(BF16)
    h_send = (picked_ref[:, :width] + h_halo).astype(BF16)
    inputs = jnp.concatenate([edges_ref[...], h_send, picked_ref[:, width:]], axis=1)
    pre = dot(inputs, w_in_ref[...], ((1,), (0,)))
    sig = jax.nn.sigmoid(pre)
    act = (pre * sig).astype(BF16)
    hidden = dot(act, w_out_ref[...], ((1,), (0,)))
    centred = hidden - jnp.mean(hidden, axis=-1, keepdims=True)
    rstd = lax.rsqrt(jnp.mean(centred * centred, axis=-1, keepdims=True) + 1e-05)
    normed = centred * rstd
    live = lax.broadcasted_iota(jnp.int32, (rows, width), 0) < count_ref[0]
    dnorm = jnp.where(live, cot_ref[...].astype(F32), 0.0)
    dhidden = rstd * (
        dnorm
        - jnp.mean(dnorm, axis=-1, keepdims=True)
        - normed * jnp.mean(dnorm * normed, axis=-1, keepdims=True)
    )
    dhidden_b = dhidden.astype(BF16)
    dw_out_ref[...] = dot(act, dhidden_b, ((0,), (0,)))
    dact = dot(dhidden_b, w_out_ref[...], ((1,), (1,)))
    dpre_b = (dact * sig * (1.0 + pre * (1.0 - sig))).astype(BF16)
    dw_in_ref[...] = dot(inputs, dpre_b, ((0,), (0,)))
    dinputs = dot(dpre_b, w_in_ref[...], ((1,), (1,)))
    grad_edges_ref[...] = (dnorm + dinputs[:, :width]).astype(BF16)
    d_send = dinputs[:, width : 2 * width].astype(BF16)
    d_recv = dinputs[:, 2 * width :].astype(BF16)

    border = dot(pick_send[: 2 * RIM + nodes], d_send, ((1,), (0,)))
    down, up = border[:RIM], border[RIM + nodes :]
    near_out_ref[...] = jnp.where(even, up, down).astype(BF16)
    next_out_ref[...] = jnp.where(even, down, up).astype(BF16)
    own_ref[...] = border[RIM : RIM + nodes] + dot(pick_recv, d_recv, ((1,), (0,)))
    dense = dot(route_ref[...], d_send, ((1,), (0,)))
    for y in range(YS):
        dense_ref[y] = dense[:, y * LANES : (y + 1) * LANES]

    doms = zs * YS * CORES
    r_in = dw_in_ref.shape[0] // doms
    r_out = dw_out_ref.shape[0] // doms
    r_coarse = dense_ref.shape[1] // (zs * CORES)
    row_tiles = (r_in + r_out) // TILE
    col_tiles = width // LANES
    half = zs // 2

    def lay(base, y_order, refs, i, carry):
        index = base + i
        reverse = 0
        for b in range(bits(zs)):
            reverse = reverse | (((index >> b) & 1) << (bits(zs) - 1 - b))
        z = z_me ^ reverse
        for iy, ry in enumerate(y_order):
            y = y_me ^ ry
            for rc, ref in enumerate(refs):
                core = core_me ^ rc
                block = (z * YS + y) * CORES + core
                weight = jnp.concatenate(
                    [
                        dw_in_ref[pl.ds(pl.multiple_of(block * r_in, 8), r_in), :],
                        dw_out_ref[pl.ds(pl.multiple_of(block * r_out, 8), r_out), :],
                    ],
                    axis=0,
                ).astype(BF16)
                for rt in range(row_tiles):
                    for ct in range(col_tiles):
                        ref[iy, i, rt * col_tiles + ct] = weight[
                            rt * TILE : (rt + 1) * TILE, ct * LANES : (ct + 1) * LANES
                        ]
                first = pl.multiple_of((core * zs + z) * r_coarse, TILE)
                coarse = dense_ref[y, pl.ds(first, r_coarse), :].astype(BF16)
                for t in range(r_coarse // TILE):
                    ref[iy, i, row_tiles * col_tiles + t] = coarse[t * TILE : (t + 1) * TILE]
        return carry

    halves = ((keep_a_ref, send_a_ref), (keep_b_ref, send_b_ref))
    for h in range(2):
        lax.fori_loop(0, half, functools.partial(lay, h * half, Y_ORDERS[h], halves[h]), 0)


def last_kernel(
    z_order,
    scale,
    first_id,
    place_ref,
    names_ref,
    mine_ref,
    other_ref,
    own_ref,
    near_ref,
    next_ref,
    weight_ref,
    weight_other_ref,
    coarse_ref,
    fine_ref,
    grad_in_ref,
    grad_out_ref,
):
    ys, zs, tiles, tile, lanes = mine_ref.shape
    per = tiles * tile
    rows = zs * per
    slots = coarse_ref.shape[0]
    z_me, _, core_me = position(place_ref[0])
    ids = names_ref[:, first_id : first_id + slots]
    row = lax.broadcasted_iota(jnp.int32, (per, slots), 0)

    last = zs * ys * CORES - 1
    base = jnp.where(place_ref[0] == 0, NC + RIM, jnp.where(place_ref[0] == last, NC, -NC))
    end_ids = base + lax.broadcasted_iota(jnp.int32, (1, RIM), 1)
    end_row = lax.broadcasted_iota(jnp.int32, (per, RIM), 0)

    def pick(core, row, ids):
        return jnp.concatenate(
            [
                jnp.where(row + (core * zs + (z_me ^ rz)) * per == ids, 1.0, 0.0)
                for rz in z_order
            ],
            axis=0,
        ).astype(BF16)

    pick_mine, pick_other = pick(core_me, row, ids), pick(1 - core_me, row, ids)
    end_mine, end_other = pick(core_me, end_row, end_ids), pick(1 - core_me, end_row, end_ids)
    ends = []
    for y in range(ys):
        mine = mine_ref[y].reshape(rows, lanes)
        other = other_ref[y].reshape(rows, lanes)
        total = dot(pick_mine, mine, ((0,), (0,))) + dot(pick_other, other, ((0,), (0,)))
        ends.append(dot(end_mine, mine, ((0,), (0,))) + dot(end_other, other, ((0,), (0,))))
        coarse_ref[:, y * lanes : (y + 1) * lanes] = total.astype(BF16)
    nodes = own_ref.shape[0]
    even = core_me == 0
    near = near_ref[...].astype(F32)
    following = jnp.where(base > 0, jnp.concatenate(ends, axis=1), next_ref[...].astype(F32))
    from_down = jnp.where(even, following, near)
    from_up = jnp.where(even, near, following)
    fine_ref[:RIM] = (own_ref[:RIM] + from_down).astype(BF16)
    fine_ref[RIM : nodes - RIM] = own_ref[RIM : nodes - RIM].astype(BF16)
    fine_ref[nodes - RIM :] = (own_ref[nodes - RIM :] + from_up).astype(BF16)

    r_in = grad_in_ref.shape[0]
    col_tiles = grad_in_ref.shape[1] // lanes
    for t in range(weight_ref.shape[0]):
        value = (weight_ref[t].astype(F32) + weight_other_ref[t].astype(F32)) * scale
        cols = slice(t % col_tiles * lanes, (t % col_tiles + 1) * lanes)
        for part in range(0, tile, 8):
            first = t // col_tiles * tile + part
            if first < r_in:
                grad_in_ref[first : first + 8, cols] = value[part : part + 8]
            else:
                grad_out_ref[first - r_in : first - r_in + 8, cols] = value[part : part + 8]


SMEM = pl.BlockSpec(memory_space=pltpu.SMEM)
VMEM = pl.BlockSpec(memory_space=pltpu.VMEM)


def plus(a, b):
    return (a.astype(F32) + b.astype(F32)).astype(BF16)


def swap(value, axis, mask):
    count = lax.axis_size(axis)
    return lax.ppermute(value, axis, [(i, i ^ mask) for i in range(count)])


def shards(
    zs,
    xs,
    edges,
    cotangent,
    fine_latents,
    coarse_block,
    w_in,
    w_out,
    senders,
    receivers,
    edge_count,
    coarse_ids,
):
    rows, width = edges.shape[1:]
    nodes = fine_latents.shape[1]
    slots = coarse_block.shape[1]
    depth = 2 * RIM + nodes + slots
    dom_axes = ("z", "y", "core")
    doms = zs * YS * CORES
    beside = [(i, (i + 1 - 2 * (i % 2)) % doms) for i in range(doms)]
    across = [(i, (i - 1 + 2 * (i % 2)) % doms) for i in range(doms)]
    place = lax.axis_index(dom_axes).astype(jnp.int32).reshape(1)
    even = lax.axis_index("core") == 0

    fine = fine_latents[0]
    first, last = fine[:RIM], fine[nodes - RIM :]
    following = lax.ppermute(jnp.where(even, first, last), dom_axes, across)
    near = lax.ppermute(jnp.where(even, last, first), dom_axes, beside)

    r_weight = (w_in.shape[0] + w_out.shape[0]) // doms
    w_tiles = r_weight // TILE * (width // LANES)
    c_tiles = -(-(NC + 2 * RIM) // (zs * CORES * TILE))
    tiles = w_tiles + c_tiles
    padded = c_tiles * TILE * zs * CORES
    half = zs // 2

    shape = jax.ShapeDtypeStruct
    own_ids = lax.dynamic_slice_in_dim(coarse_ids, place[0], 1, 0)
    names = jnp.concatenate([senders[None], receivers[None], own_ids], axis=1)
    table = jnp.concatenate([fine, coarse_block[0]], axis=0)
    loaded = pl.pallas_call(
        functools.partial(load_kernel, zs),
        out_shape=(
            shape((rows, 2 * width), BF16),
            shape((2 * RIM + nodes + slots, rows), BF16),
            shape((nodes, rows), BF16),
            shape((padded, rows), BF16),
        ),
        in_specs=[SMEM] + [VMEM] * 2,
        out_specs=(VMEM,) * 4,
        compiler_params=pltpu.CompilerParams(vmem_limit_bytes=24 * 2**20),
        cost_estimate=pl.CostEstimate(
            flops=2_000_000_000, bytes_accessed=8_000_000, transcendentals=0
        ),
        name="edge_inputs",
    )(place, table, names)

    block = shape((YS, half, tiles, TILE, LANES), BF16)
    grad_edges, own, near_out, next_out, keep_a, send_a, keep_b, send_b = pl.pallas_call(
        functools.partial(edge_kernel, zs),
        out_shape=(
            shape((rows, width), BF16),
            shape((nodes, width), F32),
            shape((RIM, width), BF16),
            shape((RIM, width), BF16),
            block,
            block,
            block,
            block,
        ),
        in_specs=[SMEM, SMEM] + [VMEM] * 10,
        out_specs=(VMEM,) * 8,
        scratch_shapes=[
            pltpu.VMEM(w_in.shape, F32),
            pltpu.VMEM(w_out.shape, F32),
            pltpu.VMEM((YS, padded, LANES), F32),
        ],
        compiler_params=pltpu.CompilerParams(vmem_limit_bytes=36 * 2**20),
        cost_estimate=pl.CostEstimate(
            flops=1_800_000_000, bytes_accessed=6_000_000, transcendentals=rows * width
        ),
        name="edge_backward",
    )(edge_count, place, *loaded, edges[0], cotangent[0], w_in, w_out, near, following)

    other_a = swap(send_a, "core", 1)
    other_b = swap(send_b, "core", 1)
    two = YS // 2

    def split_plus(a, b, at):
        return plus(a[:at], b[:at]), plus(a[at:], b[at:])

    keep_a, send_a = split_plus(keep_a, other_a, two)
    keep_b, send_b = split_plus(keep_b, other_b, two)
    send_a, near_out, next_out = lax.optimization_barrier((send_a, near_out, next_out))
    other_a = swap(send_a, "y", Y_STEPS[0][0])
    other_b = swap(send_b, "y", Y_STEPS[1][0])
    inner = [(i, j) for i, j in across if abs(i - j) == 1]
    following = lax.ppermute(next_out, dom_axes, inner)
    near = lax.ppermute(near_out, dom_axes, beside)
    other_a, other_b, near, following = lax.optimization_barrier(
        (other_a, other_b, near, following)
    )
    keep_a, send_a = split_plus(keep_a, other_a, 1)
    keep_b, send_b = split_plus(keep_b, other_b, 1)
    other_b = swap(send_b, "y", Y_STEPS[1][1])
    other_a = swap(send_a, "y", Y_STEPS[0][1])
    send = plus(keep_b[0], other_b[0])
    keep = plus(keep_a[0], other_a[0])
    masks = [1 << b for b in range(bits(zs))]
    keep = plus(keep, swap(send, "z", 1))
    weight, coarse = keep[:, :w_tiles], keep[:, w_tiles:]
    z_order = [
        2 * sum(((i >> b) & 1) << (bits(half) - 1 - b) for b in range(bits(half)))
        for i in range(half)
    ]
    for mask in masks[1:]:
        rest = weight.shape[0] // 2
        turned = jnp.stack([coarse[z_order.index(r ^ mask)] for r in z_order])
        payload = jnp.concatenate(
            [weight[rest:].reshape(-1, TILE, LANES), turned.reshape(-1, TILE, LANES)], axis=0
        )
        other = swap(payload, "z", mask)
        weight = plus(weight[:rest], other[: rest * w_tiles].reshape(-1, w_tiles, TILE, LANES))
        coarse = plus(coarse, other[rest * w_tiles :].reshape(coarse.shape))
    weight = weight[0]

    z_order = z_order + [r ^ 1 for r in z_order]
    x_masks = [2 * (1 << b) - 1 for b in range(bits(xs))]
    coarse_other = swap(coarse, "z", 1)
    weight_steps = [("member", mask) for mask in x_masks]
    weight_steps.insert(1, ("dp", 1))
    weight_other = swap(weight, *weight_steps[0])
    weight_other, coarse_other = lax.optimization_barrier((weight_other, coarse_other))
    coarse = jnp.concatenate([coarse, coarse_other], axis=0)
    weight = plus(weight, weight_other)
    weight, coarse = lax.optimization_barrier((weight, coarse))
    weight_other = swap(weight, *weight_steps[1])
    coarse = lax.all_to_all(
        jnp.broadcast_to(coarse[None], (YS,) + coarse.shape), "y", 0, 0, tiled=True
    )
    weight_other, coarse = lax.optimization_barrier((weight_other, coarse))
    for step in weight_steps[2:]:
        weight = plus(weight, weight_other)
        weight_other = swap(weight, *step)
    coarse_other = swap(coarse, "core", 1)

    all_edges = rows * doms * xs * lax.axis_size("dp")
    grad_coarse, grad_fine, grad_in, grad_out = pl.pallas_call(
        functools.partial(last_kernel, z_order, 1.0 / math.sqrt(all_edges), 2 * rows),
        out_shape=(
            shape((slots, width), BF16),
            shape((nodes, width), BF16),
            shape((w_in.shape[0] // doms, width), F32),
            shape((w_out.shape[0] // doms, width), F32),
        ),
        in_specs=[SMEM] + [VMEM] * 8,
        out_specs=(VMEM,) * 4,
        compiler_params=pltpu.CompilerParams(vmem_limit_bytes=16 * 2**20),
        name="last_sums",
    )(
        place,
        names,
        coarse,
        coarse_other,
        own,
        near,
        following,
        weight,
        weight_other,
    )
    return (grad_edges[None], grad_fine[None], grad_coarse[None], grad_in, grad_out)


def solution(mesh):
    doms, xs, dps = (mesh.shape[name] for name in ("dom", "member", "dp"))
    zs = doms // (YS * CORES)
    split = Mesh(
        mesh.devices.reshape(zs, YS, CORES, xs, dps), ("z", "y", "core", "member", "dp")
    )
    dom = ("z", "y", "core")
    sample = ("member", "dp")
    latent = P(sample, dom, None)
    return jax.shard_map(
        functools.partial(shards, zs, xs),
        mesh=split,
        in_specs=(latent,) * 4 + (P(), P(), P(dom), P(dom), P(dom), P()),
        out_specs=(latent,) * 3 + (P(dom, None), P(dom, None)),
        check_vma=False,
    )
```

```python
import functools
import math

import jax
import jax.numpy as jnp
from jax import lax
from jax.experimental import pallas as pl
from jax.experimental.pallas import tpu as pltpu
from jax.sharding import Mesh
from jax.sharding import PartitionSpec as P

RIM = 16
NC = 642
YS = 4
CORES = 2
LANES = 128
TILE = 16

F32 = jnp.float32
BF16 = jnp.bfloat16

Y_ORDERS = ((0, 3, 1, 2), (0, 1, 3, 2))
Y_STEPS = ((1, 3), (3, 1))


def dot(left, right, dims):
    return lax.dot_general(left, right, (dims, ((), ())), preferred_element_type=F32)


def position(dom):
    core = lax.rem(dom, CORES)
    y = lax.rem(dom // CORES, YS)
    z = dom // (CORES * YS)
    return z, y, core


def bits(count):
    return count.bit_length() - 1


def picks(names, count):
    rows = lax.broadcasted_iota(jnp.int32, (count, names.shape[1]), 0)
    return jnp.where(rows == names, 1.0, 0.0).astype(BF16)


def load_kernel(
    zs,
    place_ref,
    table_ref,
    names_ref,
    picked_ref,
    pick_send_ref,
    pick_recv_ref,
    route_ref,
):
    rows, width = picked_ref.shape[0], table_ref.shape[1]
    nodes = pick_recv_ref.shape[0]
    depth = pick_send_ref.shape[0]
    dom = place_ref[0]

    pick_send = picks(names_ref[:, :rows], depth)
    pick_recv = picks(names_ref[:, rows : 2 * rows], nodes)
    pick_send_ref[...] = pick_send
    pick_recv_ref[...] = pick_recv
    fine, coarse = table_ref[:nodes], table_ref[nodes:]
    h_send = dot(pick_send[RIM : RIM + nodes], fine, ((0,), (0,))) + dot(
        pick_send[2 * RIM + nodes :], coarse, ((0,), (0,))
    )
    h_recv = dot(pick_recv, fine, ((0,), (0,)))
    picked_ref[:, :width] = h_send.astype(BF16)
    picked_ref[:, width:] = h_recv.astype(BF16)

    padded = route_ref.shape[0]
    ids = names_ref[:, 2 * rows : 2 * rows + depth - 2 * RIM - nodes]
    route = dot(picks(ids, padded), pick_send[2 * RIM + nodes :], ((1,), (0,)))
    extent = (padded, 2 * RIM + nodes)
    lane = lax.broadcasted_iota(jnp.int32, extent, 1)
    down_row = jnp.where((lane < RIM) & (dom == 0), NC + lane, -1)
    end_row = jnp.where(
        (lane >= RIM + nodes) & (dom == zs * YS * CORES - 1), NC + lane - nodes, down_row
    )
    ends = jnp.where(lax.broadcasted_iota(jnp.int32, extent, 0) == end_row, 1.0, 0.0)
    route = route + dot(ends.astype(BF16), pick_send[: 2 * RIM + nodes], ((1,), (0,)))
    route_ref[...] = route.astype(BF16)


def edge_kernel(
    zs,
    count_ref,
    place_ref,
    picked_ref,
    pick_send_ref,
    pick_recv_ref,
    route_ref,
    edges_ref,
    cot_ref,
    w_in_ref,
    w_out_ref,
    near_ref,
    next_ref,
    grad_edges_ref,
    own_ref,
    near_out_ref,
    next_out_ref,
    keep_a_ref,
    send_a_ref,
    keep_b_ref,
    send_b_ref,
    dw_in_ref,
    dw_out_ref,
    dense_ref,
):
    rows, width = cot_ref.shape
    nodes = pick_recv_ref.shape[0]
    z_me, y_me, core_me = position(place_ref[0])
    even = core_me == 0

    pick_send = pick_send_ref[...]
    pick_recv = pick_recv_ref[...]
    before = jnp.where(even, next_ref[...], near_ref[...])
    after = jnp.where(even, near_ref[...], next_ref[...])
    h_halo = (
        dot(pick_send[:RIM], before, ((0,), (0,)))
        + dot(pick_send[RIM + nodes : 2 * RIM + nodes], after, ((0,), (0,)))
    ).astype(BF16)
    h_send = (picked_ref[:, :width] + h_halo).astype(BF16)
    inputs = jnp.concatenate([edges_ref[...], h_send, picked_ref[:, width:]], axis=1)
    pre = dot(inputs, w_in_ref[...], ((1,), (0,)))
    sig = jax.nn.sigmoid(pre)
    act = (pre * sig).astype(BF16)
    hidden = dot(act, w_out_ref[...], ((1,), (0,)))
    centred = hidden - jnp.mean(hidden, axis=-1, keepdims=True)
    rstd = lax.rsqrt(jnp.mean(centred * centred, axis=-1, keepdims=True) + 1e-05)
    normed = centred * rstd
    live = lax.broadcasted_iota(jnp.int32, (rows, width), 0) < count_ref[0]
    dnorm = jnp.where(live, cot_ref[...].astype(F32), 0.0)
    dhidden = rstd * (
        dnorm
        - jnp.mean(dnorm, axis=-1, keepdims=True)
        - normed * jnp.mean(dnorm * normed, axis=-1, keepdims=True)
    )
    dhidden_b = dhidden.astype(BF16)
    dw_out_ref[...] = dot(act, dhidden_b, ((0,), (0,)))
    dact = dot(dhidden_b, w_out_ref[...], ((1,), (1,)))
    dpre_b = (dact * sig * (1.0 + pre * (1.0 - sig))).astype(BF16)
    dw_in_ref[...] = dot(inputs, dpre_b, ((0,), (0,)))
    dinputs = dot(dpre_b, w_in_ref[...], ((1,), (1,)))
    grad_edges_ref[...] = (dnorm + dinputs[:, :width]).astype(BF16)
    d_send = dinputs[:, width : 2 * width].astype(BF16)
    d_recv = dinputs[:, 2 * width :].astype(BF16)

    border = dot(pick_send[: 2 * RIM + nodes], d_send, ((1,), (0,)))
    down, up = border[:RIM], border[RIM + nodes :]
    near_out_ref[...] = jnp.where(even, up, down).astype(BF16)
    next_out_ref[...] = jnp.where(even, down, up).astype(BF16)
    own_ref[...] = border[RIM : RIM + nodes] + dot(pick_recv, d_recv, ((1,), (0,)))
    dense = dot(route_ref[...], d_send, ((1,), (0,)))
    for y in range(YS):
        dense_ref[y] = dense[:, y * LANES : (y + 1) * LANES]

    doms = zs * YS * CORES
    r_in = dw_in_ref.shape[0] // doms
    r_out = dw_out_ref.shape[0] // doms
    r_coarse = dense_ref.shape[1] // (zs * CORES)
    row_tiles = (r_in + r_out) // TILE
    col_tiles = width // LANES
    half = zs // 2

    def lay(base, y_order, refs, i, carry):
        index = base + i
        reverse = 0
        for b in range(bits(zs)):
            reverse = reverse | (((index >> b) & 1) << (bits(zs) - 1 - b))
        z = z_me ^ reverse
        for iy, ry in enumerate(y_order):
            y = y_me ^ ry
            for rc, ref in enumerate(refs):
                core = core_me ^ rc
                block = (z * YS + y) * CORES + core
                weight = jnp.concatenate(
                    [
                        dw_in_ref[pl.ds(pl.multiple_of(block * r_in, 8), r_in), :],
                        dw_out_ref[pl.ds(pl.multiple_of(block * r_out, 8), r_out), :],
                    ],
                    axis=0,
                ).astype(BF16)
                for rt in range(row_tiles):
                    for ct in range(col_tiles):
                        ref[iy, i, rt * col_tiles + ct] = weight[
                            rt * TILE : (rt + 1) * TILE, ct * LANES : (ct + 1) * LANES
                        ]
                first = pl.multiple_of((core * zs + z) * r_coarse, TILE)
                coarse = dense_ref[y, pl.ds(first, r_coarse), :].astype(BF16)
                for t in range(r_coarse // TILE):
                    ref[iy, i, row_tiles * col_tiles + t] = coarse[t * TILE : (t + 1) * TILE]
        return carry

    halves = ((keep_a_ref, send_a_ref), (keep_b_ref, send_b_ref))
    for h in range(2):
        lax.fori_loop(0, half, functools.partial(lay, h * half, Y_ORDERS[h], halves[h]), 0)


def last_kernel(
    z_order,
    scale,
    first_id,
    place_ref,
    names_ref,
    mine_ref,
    other_ref,
    own_ref,
    near_ref,
    next_ref,
    weight_ref,
    weight_other_ref,
    coarse_ref,
    fine_ref,
    grad_in_ref,
    grad_out_ref,
):
    sides, ys, half, tiles, tile, lanes = mine_ref.shape
    zs = sides * half
    per = tiles * tile
    rows = zs * per
    slots = coarse_ref.shape[0]
    z_me, _, core_me = position(place_ref[0])
    ids = names_ref[:, first_id : first_id + slots]
    row = lax.broadcasted_iota(jnp.int32, (per, slots), 0)

    last = zs * ys * CORES - 1
    z_pair = z_me - lax.rem(z_me, sides)
    base = jnp.where(place_ref[0] == 0, NC + RIM, jnp.where(place_ref[0] == last, NC, -NC))
    end_ids = base + lax.broadcasted_iota(jnp.int32, (1, RIM), 1)
    end_row = lax.broadcasted_iota(jnp.int32, (per, RIM), 0)

    def pick(core, row, ids):
        return jnp.concatenate(
            [
                jnp.where(row + (core * zs + ((z_pair + side) ^ rz)) * per == ids, 1.0, 0.0)
                for side in range(sides)
                for rz in z_order
            ],
            axis=0,
        ).astype(BF16)

    pick_mine, pick_other = pick(core_me, row, ids), pick(1 - core_me, row, ids)
    end_mine, end_other = pick(core_me, end_row, end_ids), pick(1 - core_me, end_row, end_ids)
    ends = []
    for y in range(ys):
        mine = mine_ref[:, y].reshape(rows, lanes)
        other = other_ref[:, y].reshape(rows, lanes)
        total = dot(pick_mine, mine, ((0,), (0,))) + dot(pick_other, other, ((0,), (0,)))
        ends.append(dot(end_mine, mine, ((0,), (0,))) + dot(end_other, other, ((0,), (0,))))
        coarse_ref[:, y * lanes : (y + 1) * lanes] = total.astype(BF16)
    nodes = own_ref.shape[0]
    even = core_me == 0
    near = near_ref[...].astype(F32)
    following = jnp.where(base > 0, jnp.concatenate(ends, axis=1), next_ref[...].astype(F32))
    from_down = jnp.where(even, following, near)
    from_up = jnp.where(even, near, following)
    fine_ref[:RIM] = (own_ref[:RIM] + from_down).astype(BF16)
    fine_ref[RIM : nodes - RIM] = own_ref[RIM : nodes - RIM].astype(BF16)
    fine_ref[nodes - RIM :] = (own_ref[nodes - RIM :] + from_up).astype(BF16)

    r_in = grad_in_ref.shape[0]
    col_tiles = grad_in_ref.shape[1] // lanes
    for t in range(weight_ref.shape[0]):
        value = (weight_ref[t].astype(F32) + weight_other_ref[t].astype(F32)) * scale
        cols = slice(t % col_tiles * lanes, (t % col_tiles + 1) * lanes)
        for part in range(0, tile, 8):
            first = t // col_tiles * tile + part
            if first < r_in:
                grad_in_ref[first : first + 8, cols] = value[part : part + 8]
            else:
                grad_out_ref[first - r_in : first - r_in + 8, cols] = value[part : part + 8]


SMEM = pl.BlockSpec(memory_space=pltpu.SMEM)
VMEM = pl.BlockSpec(memory_space=pltpu.VMEM)


def plus(a, b):
    return (a.astype(F32) + b.astype(F32)).astype(BF16)


Z_AXES = ("z_pairs", "z_side")


def swap(value, axis, mask):
    count = math.prod(lax.axis_size(a) for a in (axis if isinstance(axis, tuple) else (axis,)))
    return lax.ppermute(value, axis, [(i, i ^ mask) for i in range(count)])


def shards(
    zs,
    xs,
    edges,
    cotangent,
    fine_latents,
    coarse_block,
    w_in,
    w_out,
    senders,
    receivers,
    edge_count,
    coarse_ids,
):
    rows, width = edges.shape[1:]
    nodes = fine_latents.shape[1]
    slots = coarse_block.shape[1]
    depth = 2 * RIM + nodes + slots
    dom_axes = Z_AXES + ("y", "core")
    doms = zs * YS * CORES
    beside = [(i, (i + 1 - 2 * (i % 2)) % doms) for i in range(doms)]
    across = [(i, (i - 1 + 2 * (i % 2)) % doms) for i in range(doms)]
    place = lax.axis_index(dom_axes).astype(jnp.int32).reshape(1)
    even = lax.axis_index("core") == 0

    fine = fine_latents[0]
    first, last = fine[:RIM], fine[nodes - RIM :]
    following = lax.ppermute(jnp.where(even, first, last), dom_axes, across)
    near = lax.ppermute(jnp.where(even, last, first), dom_axes, beside)

    r_weight = (w_in.shape[0] + w_out.shape[0]) // doms
    w_tiles = r_weight // TILE * (width // LANES)
    c_tiles = -(-(NC + 2 * RIM) // (zs * CORES * TILE))
    tiles = w_tiles + c_tiles
    padded = c_tiles * TILE * zs * CORES
    half = zs // 2

    shape = jax.ShapeDtypeStruct
    own_ids = lax.dynamic_slice_in_dim(coarse_ids, place[0], 1, 0)
    names = jnp.concatenate([senders[None], receivers[None], own_ids], axis=1)
    table = jnp.concatenate([fine, coarse_block[0]], axis=0)
    loaded = pl.pallas_call(
        functools.partial(load_kernel, zs),
        out_shape=(
            shape((rows, 2 * width), BF16),
            shape((2 * RIM + nodes + slots, rows), BF16),
            shape((nodes, rows), BF16),
            shape((padded, rows), BF16),
        ),
        in_specs=[SMEM] + [VMEM] * 2,
        out_specs=(VMEM,) * 4,
        compiler_params=pltpu.CompilerParams(vmem_limit_bytes=24 * 2**20),
        cost_estimate=pl.CostEstimate(
            flops=2_000_000_000, bytes_accessed=8_000_000, transcendentals=0
        ),
        name="edge_inputs",
    )(place, table, names)

    block = shape((YS, half, tiles, TILE, LANES), BF16)
    grad_edges, own, near_out, next_out, keep_a, send_a, keep_b, send_b = pl.pallas_call(
        functools.partial(edge_kernel, zs),
        out_shape=(
            shape((rows, width), BF16),
            shape((nodes, width), F32),
            shape((RIM, width), BF16),
            shape((RIM, width), BF16),
            block,
            block,
            block,
            block,
        ),
        in_specs=[SMEM, SMEM] + [VMEM] * 10,
        out_specs=(VMEM,) * 8,
        scratch_shapes=[
            pltpu.VMEM(w_in.shape, F32),
            pltpu.VMEM(w_out.shape, F32),
            pltpu.VMEM((YS, padded, LANES), F32),
        ],
        compiler_params=pltpu.CompilerParams(vmem_limit_bytes=36 * 2**20),
        cost_estimate=pl.CostEstimate(
            flops=1_800_000_000, bytes_accessed=6_000_000, transcendentals=rows * width
        ),
        name="edge_backward",
    )(edge_count, place, *loaded, edges[0], cotangent[0], w_in, w_out, near, following)

    other_a = swap(send_a, "core", 1)
    other_b = swap(send_b, "core", 1)
    two = YS // 2

    def split_plus(a, b, at):
        return plus(a[:at], b[:at]), plus(a[at:], b[at:])

    keep_a, send_a = split_plus(keep_a, other_a, two)
    keep_b, send_b = split_plus(keep_b, other_b, two)
    send_a, near_out, next_out = lax.optimization_barrier((send_a, near_out, next_out))
    other_a = swap(send_a, "y", Y_STEPS[0][0])
    other_b = swap(send_b, "y", Y_STEPS[1][0])
    inner = [(i, j) for i, j in across if abs(i - j) == 1]
    following = lax.ppermute(next_out, dom_axes, inner)
    near = lax.ppermute(near_out, dom_axes, beside)
    other_a, other_b, near, following = lax.optimization_barrier(
        (other_a, other_b, near, following)
    )
    keep_a, send_a = split_plus(keep_a, other_a, 1)
    keep_b, send_b = split_plus(keep_b, other_b, 1)
    other_b = swap(send_b, "y", Y_STEPS[1][1])
    other_a = swap(send_a, "y", Y_STEPS[0][1])
    send = plus(keep_b[0], other_b[0])
    keep = plus(keep_a[0], other_a[0])
    masks = [1 << b for b in range(bits(zs))]
    keep = plus(keep, swap(send, Z_AXES, 1))
    weight, coarse = keep[:, :w_tiles], keep[:, w_tiles:]
    z_order = [
        2 * sum(((i >> b) & 1) << (bits(half) - 1 - b) for b in range(bits(half)))
        for i in range(half)
    ]
    for mask in masks[1:]:
        rest = weight.shape[0] // 2
        turned = jnp.stack([coarse[z_order.index(r ^ mask)] for r in z_order])
        payload = jnp.concatenate(
            [weight[rest:].reshape(-1, TILE, LANES), turned.reshape(-1, TILE, LANES)], axis=0
        )
        other = swap(payload, Z_AXES, mask)
        weight = plus(weight[:rest], other[: rest * w_tiles].reshape(-1, w_tiles, TILE, LANES))
        coarse = plus(coarse, other[rest * w_tiles :].reshape(coarse.shape))
    weight = weight[0]

    x_masks = [2 * (1 << b) - 1 for b in range(bits(xs))]
    weight_steps = [("dp", 1)] + [("member", mask) for mask in x_masks]
    coarse = lax.all_to_all(
        jnp.broadcast_to(coarse[None], (2 * YS,) + coarse.shape),
        (Z_AXES[1], "y"),
        0,
        0,
        tiled=True,
    )
    for step in weight_steps[:-1]:
        weight_other = swap(weight, *step)
        if step == weight_steps[-2]:
            weight_other, coarse = lax.optimization_barrier((weight_other, coarse))
        weight = plus(weight, weight_other)
    weight_other = swap(weight, *weight_steps[-1])
    coarse = coarse.reshape(2, YS, half, c_tiles, TILE, LANES)
    coarse_other = swap(coarse, "core", 1)

    all_edges = rows * doms * xs * lax.axis_size("dp")
    grad_coarse, grad_fine, grad_in, grad_out = pl.pallas_call(
        functools.partial(last_kernel, z_order, 1.0 / math.sqrt(all_edges), 2 * rows),
        out_shape=(
            shape((slots, width), BF16),
            shape((nodes, width), BF16),
            shape((w_in.shape[0] // doms, width), F32),
            shape((w_out.shape[0] // doms, width), F32),
        ),
        in_specs=[SMEM] + [VMEM] * 8,
        out_specs=(VMEM,) * 4,
        compiler_params=pltpu.CompilerParams(vmem_limit_bytes=16 * 2**20),
        name="last_sums",
    )(
        place,
        names,
        coarse,
        coarse_other,
        own,
        near,
        following,
        weight,
        weight_other,
    )
    return (grad_edges[None], grad_fine[None], grad_coarse[None], grad_in, grad_out)


def solution(mesh):
    doms, xs, dps = (mesh.shape[name] for name in ("dom", "member", "dp"))
    zs = doms // (YS * CORES)
    dom = Z_AXES + ("y", "core")
    split = Mesh(
        mesh.devices.reshape(zs // 2, 2, YS, CORES, xs, dps), dom + ("member", "dp")
    )
    sample = ("member", "dp")
    latent = P(sample, dom, None)
    return jax.shard_map(
        functools.partial(shards, zs, xs),
        mesh=split,
        in_specs=(latent,) * 4 + (P(), P(), P(dom), P(dom), P(dom), P()),
        out_specs=(latent,) * 3 + (P(dom, None), P(dom, None)),
        check_vma=False,
    )
```
